512 devices in a mesh: peer: 64 (over x, z, core), tp: 8 (over y).
Axes of the slice: x: 4, y: 8, z: 8, core: 2. Of those that a mesh axis runs over, the one named last changes fastest.
Arguments:
- activations: bfloat16 [16384, 8192], P('peer', 'tp'), may hold values from -24 to 24
- targets: bfloat16 [16384, 1024], P('peer', 'tp'), may hold values from -6 to 6
- routes: int32 [2048, 1], P('peer'), may hold values from 0 to 63; in each aligned block of 32 rows (0 to 31, 32 to 63, ...) no two rows name the same one
- value_weights: bfloat16 [64, 8192, 1024], P('peer', 'tp'), may hold values from -0.0625 to 0.0625
- norm_gains: float32 [64, 8192], P('peer', 'tp'), may hold values from 0.1 to 1.9
Outputs:
- grad_rows: bfloat16 [16384, 8192], P('peer', 'tp')
- values: bfloat16 [16384, 1024], P('peer', 'tp')
- weight_grad: float32 [1024, 8192], P('peer', 'tp')
- gain_grad: float32 [8192], P('tp')
The draws below stay inside these ranges and needn't reach their ends.
Inputs may be any that keep to these rules, and one draw needn't show every extreme that they name: `routes`: one source device sends at most 1 of its 32 pieces to one destination, and some source sends exactly 1 piece to one destination.
All inputs are finite; a program needn't handle non-finite values.
Results may differ from the reference program's by a relative error of at most 0.019.
Values may be sent and summed in bfloat16 or wider, within the bound.
No kernel may reach another device: no remote copies, remote signals or barrier semaphores. Data moves between devices by JAX's collectives and lax.ppermute only.
A program may use at most 64 MiB of HBM per device.

```python
import math
import jax
import jax.numpy as jnp
import numpy as np
from jax import lax

D = 8192
KV = 1024
MB = 8
PIECES = 32
MOST = 1
TOKENS = 16384
N_PEER = 64
N_TP = 8


def draw_activations(key, part):
    key = jax.random.fold_in(key, 17)
    key_rows, key_cols, key_values, key_common, key_loading = jax.random.split(key, 5)
    row_scale = jnp.exp(jax.random.uniform(key_rows, (TOKENS, 1), jnp.float32, math.log(0.1), 0.0))
    column_scale = jnp.exp(jax.random.uniform(key_cols, (1, D), jnp.float32, math.log(0.3), math.log(3.0)))
    entries = jnp.clip(jax.random.normal(key_values, (TOKENS, D), jnp.float32), -4.0, 4.0)
    common = jnp.clip(jax.random.normal(key_common, (1, D), jnp.float32), -3.0, 3.0)
    loading = jnp.clip(jax.random.normal(key_loading, (TOKENS, 1), jnp.float32), -3.0, 3.0)
    common_share = 0.5
    clip_level = 4.5
    growth = math.sqrt(3.0)
    blended = math.sqrt(common_share) * loading * common + math.sqrt(1.0 - common_share) * entries
    blended = jnp.clip(blended, -clip_level, clip_level)
    feature_ramp = jnp.exp(math.log(growth) * jnp.arange(D, dtype=jnp.float32) / D)
    return (blended * row_scale * column_scale * feature_ramp[None, :]).astype(jnp.bfloat16)


def block_levels(own_key, dims, pieces, smallest, high):
    loudness, own = 1.0, jax.random.fold_in(own_key, 6)
    for position, parts in pieces:
        heights = jnp.exp(jax.random.uniform(jax.random.fold_in(own, position), (parts,), jnp.float32, smallest / len(pieces), high / len(pieces)))
        loudness = loudness * jnp.repeat(heights, dims[position] // parts).reshape([-1 if axis == position else 1 for axis in range(len(dims))])
    return loudness


def assign_block(stream_key, own, number, rows, number_of, top, limit, slope):
    order = jax.random.permutation(stream_key, number_of)
    crowded, ordinary = shares(number_of, rows * top, limit, slope, True), shares(number_of, rows * top, limit, slope, False)
    places = jnp.arange(number_of)

    def named(lengths, offset_by):
        used = int((lengths > 0).sum())
        fixed = max(1, used // 4)
        shifted = fixed + (places - fixed + offset_by * (used - fixed)) % max(1, number_of - fixed)
        return jnp.zeros((number_of,), jnp.int32).at[order[jnp.where(places < fixed, places, shifted)]].set(jnp.asarray(lengths, jnp.int32))

    lengths = jnp.where(number % 4 == 0, named(crowded, number // 4), named(ordinary, number - number // 4 - 1))
    mixed = jax.random.permutation(jax.random.fold_in(own, 3), number_of)
    source_of, taker = mixed[0:number_of // 2 * 2:2], mixed[1:number_of // 2 * 2:2]
    room = jnp.minimum(lengths[source_of] - 1, limit - lengths[taker]) // 2
    room = jnp.where((source_of == order[0]) | (taker == order[0]) | (lengths[taker] == 0), 0, jnp.maximum(room, 0))
    shifted = jax.random.randint(jax.random.fold_in(own, 4), (number_of // 2,), 0, 1 << 20) % (room + 1)
    lengths = lengths.at[source_of].add(-shifted).at[taker].add(shifted)
    items = jnp.searchsorted(jnp.cumsum(lengths), jnp.arange(rows * top), side="right").astype(jnp.int32)
    table = items.reshape(top, rows).T
    table = table[jax.random.permutation(jax.random.fold_in(own, 1), rows)]
    offset_by = jax.random.randint(jax.random.fold_in(own, 2), (rows, 1), 0, top)
    return jnp.take_along_axis(table, (jnp.arange(top)[None, :] + offset_by) % top, axis=1)


def shares(count, total, bound, lean, full):
    loads = [(1 << 20) // math.isqrt(grade ** lean) + 1 for grade in range(1, count + 1)]
    largest = bound if full else min(bound, max(-(-total // count), total * loads[0] // sum(loads)))
    least = 1 if total - largest >= count - 1 else 0
    given, surplus = [largest] + [least] * (count - 1), total - largest - least * (count - 1)
    while surplus > 0:
        movable = [i for i in range(1, count) if given[i] < largest] or [i for i in range(1, count) if given[i] < bound]
        whole, budget = sum([loads[i] for i in movable]), surplus
        for i in movable:
            extra = min(bound - given[i], max(1, budget * loads[i] // whole), surplus)
            given[i] = given[i] + extra
            surplus = surplus - extra
    return np.array(given)


def bell_draw(own_key, extent, width, most, pieces=(), kind=jnp.bfloat16):
    result = jax.random.normal(own_key, extent, jnp.float32) * width
    if len(pieces) > 0:
        result = block_levels(own_key, extent, pieces, -0.22, 0.18) * result
    return jnp.clip(result, min=-most, max=most).astype(kind)


def setup_inputs(seed: int = 0) -> dict:
    seeds = jax.random.split(jax.random.key(seed), 6)
    activations = draw_activations(jax.random.fold_in(seeds[5], 71), 0)
    targets = bell_draw(seeds[1], (TOKENS, KV), 1.0, 6.0, ((0, 64), (1, 8)))
    routes_keys = jax.random.split(jax.random.fold_in(seeds[2], 1), (N_PEER * PIECES) // PIECES)
    routes_turns = jax.random.permutation(jax.random.fold_in(seeds[2], 3), (N_PEER * PIECES) // PIECES)
    routes = jax.vmap(lambda own, number: assign_block(jax.random.fold_in(seeds[2], 2), own, number, PIECES, N_PEER, 1, MOST, 4))(routes_keys, routes_turns).reshape((N_PEER * PIECES, 1))
    value_weights = bell_draw(seeds[3], (N_PEER, D, KV), D ** -0.5, 0.0625, ((0, 64), (1, 8)))
    norm_gains = jnp.clip(1.0 + 0.18 * jax.random.normal(seeds[4], (N_PEER, D), jnp.float32), 0.1, 1.9)
    return {"activations": activations, "targets": targets, "routes": routes, "value_weights": value_weights, "norm_gains": norm_gains}


epsilon = 1e-05

def reference(activations, targets, routes, value_weights, norm_gains):
    shard_width = D // N_TP
    target_peer = routes[:, 0].reshape(N_PEER, PIECES).astype(jnp.int32)
    rows_all = activations.reshape(N_PEER, PIECES, MB, D)
    goals_all = targets.reshape(N_PEER, PIECES, MB, KV)

    def per_source(carry, inputs):
        weight_acc, gain_acc = carry
        rows_here, goals_here, chosen = inputs
        weights = value_weights[chosen].astype(jnp.float32)
        gain_rows = norm_gains[chosen].astype(jnp.float32)
        rows_float = rows_here.astype(jnp.float32)
        squares = lax.optimization_barrier(jnp.sum(rows_float * rows_float, axis=2))
        scales = lax.rsqrt(squares / D + epsilon)
        normal = rows_float * scales[:, :, None]
        normed = (normal * gain_rows[:, None, :]).astype(jnp.bfloat16)
        normed_float = normed.astype(jnp.float32)
        split_normed = normed_float.reshape(PIECES, MB, N_TP, shard_width)
        split_weights = weights.reshape(PIECES, N_TP, shard_width, KV)
        partials = jnp.einsum('pmtf,ptfk->pmtk', split_normed, split_weights).astype(jnp.bfloat16)
        value_sum = lax.optimization_barrier(jnp.sum(partials.astype(jnp.float32), axis=2))
        grad_values = (value_sum - goals_here.astype(jnp.float32)).astype(jnp.bfloat16)
        grad_float = grad_values.astype(jnp.float32)
        grad_normed = jnp.einsum('pmk,pfk->pmf', grad_float, weights)
        grad_gained = grad_normed * gain_rows[:, None, :]
        row_dot = lax.optimization_barrier(jnp.sum(grad_gained * normal, axis=2))
        grad_rows = (scales[:, :, None] * (grad_gained - normal * (row_dot / D)[:, :, None])).astype(jnp.bfloat16)
        weight_acc = weight_acc + jnp.einsum('pmk,pmf->kf', grad_float, normed_float)
        gain_acc = gain_acc + lax.optimization_barrier(jnp.sum(grad_normed * normal, axis=(0, 1)))
        return ((weight_acc, gain_acc), (grad_rows, value_sum.astype(jnp.bfloat16)))
    start_carry = (jnp.zeros((KV, D), jnp.float32), jnp.zeros((D,), jnp.float32))
    (weight_acc, gain_acc), (grad_rows, values) = lax.scan(per_source, start_carry, (rows_all, goals_all, target_peer))
    grad_scale = TOKENS ** (-0.5)
    return (grad_rows.reshape(TOKENS, D), values.reshape(TOKENS, KV), weight_acc * grad_scale, gain_acc * grad_scale)
```

```python
import jax
import jax.numpy as jnp
from jax import lax
from jax.experimental import pallas as pl
from jax.experimental.pallas import tpu as pltpu
from jax.sharding import Mesh, PartitionSpec as P

D = 8192
KV = 1024
PIECES = 32
MB = 8
F = 1024
C = 128
NP = 64
NT = 8
X, Z, CORES = 4, 8, 2
ROWS = NP * MB
TILE = 128
NTILES = ROWS // TILE
EXTRA = 16
GRAD_SCALE = (ROWS // 2 * NP) ** (-0.5)

epsilon = 1e-05
f32 = jnp.float32
bf16 = jnp.bfloat16
VMEM = pl.BlockSpec(memory_space=pltpu.VMEM)
SMEM = pl.BlockSpec(memory_space=pltpu.SMEM)


def call(kernel, outs, in_specs, scratch=(), flops=0, size=4 << 20, name=None):
    return pl.pallas_call(
        kernel,
        out_shape=outs,
        in_specs=in_specs,
        out_specs=jax.tree.map(lambda _: VMEM, outs),
        scratch_shapes=scratch,
        compiler_params=pltpu.CompilerParams(vmem_limit_bytes=40 << 20),
        cost_estimate=pl.CostEstimate(flops=flops, bytes_accessed=size, transcendentals=0),
        name=name,
    )


def parts(v):
    high = v.astype(bf16).astype(f32)
    rest = v - high
    mid = rest.astype(bf16).astype(f32)
    return high, mid, rest - mid


def to_lanes(square):
    return jnp.sum(square.T, axis=0, keepdims=True)


def to_rows(lanes):
    return jnp.broadcast_to(lanes, (TILE, TILE)).T


def pack_kernel(routes, acts, goals, out, slot_of):
    def clear(d, _):
        slot_of[d] = -1
        return 0

    lax.fori_loop(0, NP, clear, 0)

    def note(m, _):
        slot_of[routes[m]] = m
        return 0

    lax.fori_loop(0, PIECES, note, 0)

    def fill(d, _):
        m = slot_of[d]

        @pl.when(m >= 0)
        def _():
            out[d, :, :F] = acts[m]
            out[d, :, F:] = goals[m]

        @pl.when(m < 0)
        def _():
            out[d] = jnp.zeros((MB, F + C), bf16)

        return 0

    lax.fori_loop(0, NP, fill, 0)


def value_kernel(rows, gain, weights, out, squares):
    def tile(i, _):
        x = rows[pl.ds(i * 16, 16), :, :F].astype(f32).reshape(TILE, F)
        sq = x * x
        folded = sq[:, :128]
        for j in range(1, F // 128):
            folded = folded + sq[:, j * 128 : (j + 1) * 128]
        squares[pl.ds(i, 1), :] = to_lanes(folded)
        partial = jnp.dot((x * gain[...]).astype(bf16), weights[...], preferred_element_type=f32)
        for t in range(NT):
            out[t, pl.ds(pl.multiple_of(i * TILE, TILE), TILE), :] = partial[:, t * C : (t + 1) * C].astype(bf16)
        return 0

    lax.fori_loop(0, NTILES, tile, 0)
    high, mid, low = parts(squares[0:4, :])
    tail = jnp.concatenate([high, mid, low, jnp.zeros_like(high)], axis=0).astype(bf16)
    for t in range(NT):
        out[t, ROWS:, :] = tail


def loss_kernel(got, goals, value_out, send, scales, dots):
    tail = got[0, ROWS:, :].astype(f32)
    for t in range(1, NT):
        tail = tail + got[t, ROWS:, :].astype(f32)
    total = tail[0:4] + tail[4:8] + tail[8:12]
    scales[0:4, :] = lax.rsqrt(total / D + epsilon)
    scales[4:8, :] = jnp.zeros((4, 128), f32)

    def tile(i, _):
        here = pl.ds(pl.multiple_of(i * TILE, TILE), TILE)
        total = got[0, here, :].astype(f32)
        for t in range(1, NT):
            total = total + got[t, here, :].astype(f32)
        value = total * to_rows(scales[pl.ds(i, 1), :])
        value_out[pl.ds(i * 16, 16)] = value.reshape(16, MB, C).astype(bf16)
        goal = goals[pl.ds(i * 16, 16), :, F:].astype(f32).reshape(TILE, C)
        grad = (value - goal).astype(bf16)
        send[here, :] = grad
        dots[pl.ds(i, 1), :] = to_lanes(grad.astype(f32) * value)
        return 0

    lax.fori_loop(0, NTILES, tile, 0)
    high, mid, low = parts(dots[0:4, :])
    send[ROWS:, :] = jnp.concatenate([high, mid, low, jnp.zeros_like(high)], axis=0).astype(bf16)


def grad_kernel(got, rows, gain, weights, scales, value, back, share, normed, grads, dots, gains):
    tail = got[0, ROWS:, :].astype(f32)
    for t in range(1, NT):
        tail = tail + got[t, ROWS:, :].astype(f32)
    dots[0:4, :] = (tail[0:4] + tail[4:8] + tail[8:12]) / D
    gains[...] = jnp.zeros_like(gains)

    def tile(i, _):
        here = pl.ds(pl.multiple_of(i * TILE, TILE), TILE)
        slots = pl.ds(i * 16, 16)
        for t in range(NT):
            grads[here, t * C : (t + 1) * C] = got[t, here, :]
        grad_normed = lax.dot_general(
            grads[here, :], weights[...], (((1,), (1,)), ((), ())), preferred_element_type=f32
        )
        scale = to_rows(scales[pl.ds(i, 1), :])[:, :1]
        dot = to_rows(dots[pl.ds(i, 1), :])[:, :1]
        normal = rows[slots, :, :F].astype(f32).reshape(TILE, F) * scale
        gained = grad_normed * gain[...]
        row_grad = scale * (gained - normal * dot)
        back[slots, :, :F] = row_grad.reshape(16, MB, F).astype(bf16)
        back[slots, :, F:] = value[slots]
        gains[...] += jnp.sum((grad_normed * normal).reshape(TILE // 8, 8, F), axis=0)
        normed[here, :] = (normal * gain[...]).astype(bf16)
        return 0

    lax.fori_loop(0, NTILES, tile, 0)

    def block(i, _):
        mine = lax.dot_general(
            grads[:, pl.ds(pl.multiple_of(i * 256, 256), 256)],
            normed[...],
            (((0,), (0,)), ((), ())),
            preferred_element_type=f32,
        ).astype(bf16)
        for j in range(16):
            at = pl.multiple_of(i * 128 + (j // 2) * 16, 16)
            share[j % 2, pl.ds(at, 16), :] = mine[j * 16 : (j + 1) * 16, :]
        return 0

    lax.fori_loop(0, KV // 256, block, 0)
    tail = gain_tail(jnp.sum(gains[...], axis=0, keepdims=True))
    for c in range(CORES):
        share[c, 512:, :] = tail


def gain_tail(total):
    high, mid, low = parts(total)
    return jnp.concatenate([high, mid, low, jnp.zeros((EXTRA - 3, F), f32)], axis=0).astype(bf16)


def sum_kernel(given, taken, count, got, out):
    for i in range(taken):
        total = got[0, i * count : (i + 1) * count, :].astype(f32)
        for g in range(1, given):
            total = total + got[g, i * count : (i + 1) * count, :].astype(f32)
        out[i, :count, :] = total.astype(bf16)
    tail = got[0, taken * count :, :].astype(f32)
    for g in range(1, given):
        tail = tail + got[g, taken * count :, :].astype(f32)
    tail = gain_tail(jnp.sum(tail, axis=0, keepdims=True))
    for i in range(taken):
        out[i, count:, :] = tail


def last_kernel(got, weight_out, gain_out):
    total = got[0].astype(f32)
    for g in range(1, Z):
        total = total + got[g].astype(f32)
    weight_out[...] = total[:16] * GRAD_SCALE
    gain_out[...] = jnp.sum(total[16:], axis=0, keepdims=True) * GRAD_SCALE


def unpack_kernel(routes, got, rows, values):
    def take(m, _):
        d = routes[m]
        rows[m] = got[d, :, :F]
        values[m] = got[d, :, F:]
        return 0

    lax.fori_loop(0, PIECES, take, 0)


def shape(*dims, dtype=bf16):
    return jax.ShapeDtypeStruct(dims, dtype)


def exchange(v, axes):
    return lax.all_to_all(v, axes, split_axis=0, concat_axis=0, tiled=True)


def body(activations, targets, routes, value_weights, norm_gains):
    peer = ("x", "z", "core")
    weights = value_weights[0]
    order = routes[:, 0]
    sends = call(
        pack_kernel,
        shape(NP, MB, F + C),
        [SMEM, VMEM, VMEM],
        [pltpu.SMEM((NP,), jnp.int32)],
        name="pack",
    )(order, activations.reshape(PIECES, MB, F), targets.reshape(PIECES, MB, C))
    arrived = exchange(sends, peer)
    partials = call(
        value_kernel,
        shape(NT, ROWS + EXTRA, C),
        [VMEM] * 3,
        [pltpu.VMEM((8, 128), f32)],
        flops=2 * ROWS * F * KV,
        name="partial_values",
    )(arrived, norm_gains, weights)
    value, grad_part, scales = call(
        loss_kernel,
        (shape(NP, MB, C), shape(ROWS + EXTRA, C), shape(8, 128, dtype=f32)),
        [VMEM] * 2,
        [pltpu.VMEM((8, 128), f32)],
        name="loss",
    )(exchange(partials, "tp"), arrived)
    grads = lax.all_gather(grad_part, "tp", axis=0, tiled=False)
    back, share = call(
        grad_kernel,
        (shape(NP, MB, F + C), shape(CORES, KV // CORES + EXTRA, F)),
        [VMEM] * 6,
        [
            pltpu.VMEM((ROWS, F), bf16),
            pltpu.VMEM((ROWS, KV), bf16),
            pltpu.VMEM((8, 128), f32),
            pltpu.VMEM((8, F), f32),
        ],
        flops=4 * ROWS * F * KV,
        size=8 << 20,
        name="grads",
    )(grads, arrived, norm_gains, weights, scales, value)

    rows_back = exchange(back, peer)
    by_core = exchange(share, "core")
    by_core = call(
        lambda *refs: sum_kernel(CORES, X, 128, *refs), shape(X, 128 + EXTRA, F), [VMEM], name="sum_core"
    )(by_core)
    by_x = exchange(by_core, "x")
    by_x = call(lambda *refs: sum_kernel(X, Z, 16, *refs), shape(Z, 16 + EXTRA, F), [VMEM], name="sum_x")(by_x)
    by_z = exchange(by_x, "z")
    weight_grad, gain_grad = call(
        last_kernel, (shape(16, F, dtype=f32), shape(1, F, dtype=f32)), [VMEM], name="sum_z"
    )(by_z)
    grad_rows, values = call(
        unpack_kernel,
        (shape(PIECES, MB, F), shape(PIECES, MB, C)),
        [SMEM, VMEM],
        name="unpack",
    )(order, rows_back)
    return (
        grad_rows.reshape(PIECES * MB, F),
        values.reshape(PIECES * MB, C),
        weight_grad,
        gain_grad[0],
    )


def solution(mesh):
    split = Mesh(mesh.devices.reshape(X, Z, CORES, NT), ("x", "z", "core", "tp"))
    peer = ("x", "z", "core")
    return jax.shard_map(
        body,
        mesh=split,
        in_specs=(
            P(peer, "tp"),
            P(peer, "tp"),
            P(peer, None),
            P(peer, "tp", None),
            P(peer, "tp"),
        ),
        out_specs=(P(peer, "tp"), P(peer, "tp"), P(peer, "tp"), P("tp")),
        check_vma=False,
    )
```

```python
import jax
import jax.numpy as jnp
from jax import lax
from jax.experimental import pallas as pl
from jax.experimental.pallas import tpu as pltpu
from jax.sharding import Mesh, PartitionSpec as P

D = 8192
KV = 1024
PIECES = 32
MB = 8
F = 1024
C = 128
NP = 64
NT = 8
X, Z, CORES = 4, 8, 2
ROWS = NP * MB
TILE = 128
NTILES = ROWS // TILE
EXTRA = 16
GRAD_SCALE = (ROWS // 2 * NP) ** (-0.5)

epsilon = 1e-05
f32 = jnp.float32
bf16 = jnp.bfloat16
VMEM = pl.BlockSpec(memory_space=pltpu.VMEM)
ANY = pl.BlockSpec(memory_space=pl.ANY)
SMEM = pl.BlockSpec(memory_space=pltpu.SMEM)


def call(kernel, outs, in_specs, scratch=(), flops=0, size=4 << 20, name=None):
    return pl.pallas_call(
        kernel,
        out_shape=outs,
        in_specs=in_specs,
        out_specs=jax.tree.map(lambda _: VMEM, outs),
        scratch_shapes=scratch,
        compiler_params=pltpu.CompilerParams(vmem_limit_bytes=40 << 20),
        cost_estimate=pl.CostEstimate(flops=flops, bytes_accessed=size, transcendentals=0),
        name=name,
    )


def parts(v):
    high = v.astype(bf16).astype(f32)
    rest = v - high
    mid = rest.astype(bf16).astype(f32)
    return high, mid, rest - mid


def to_lanes(square):
    return jnp.sum(square.T, axis=0, keepdims=True)


def to_rows(lanes):
    return jnp.broadcast_to(lanes, (TILE, TILE)).T


def pack_kernel(routes, acts, goals, out, order, route_sem, row_sem, goal_sem):
    fetch = pltpu.make_async_copy(routes, order, route_sem)
    fetch.start()

    def clear(d, _):
        out[pl.ds(d * 4, 4)] = jnp.zeros((4, MB, F + C), bf16)
        return 0

    lax.fori_loop(0, NP // 4, clear, 0)
    fetch.wait()

    def send(m, _):
        d = order[m]
        pltpu.make_async_copy(acts.at[m], out.at[d, :, pl.ds(0, F)], row_sem).start()
        pltpu.make_async_copy(goals.at[m], out.at[d, :, pl.ds(F, C)], goal_sem).start()
        return 0

    lax.fori_loop(0, PIECES, send, 0)
    pltpu.make_async_copy(acts, out.at[pl.ds(0, PIECES), :, pl.ds(0, F)], row_sem).wait()
    pltpu.make_async_copy(goals, out.at[pl.ds(0, PIECES), :, pl.ds(F, C)], goal_sem).wait()


def value_kernel(rows, gain, weights, out, squares):
    def tile(i, _):
        x = rows[pl.ds(i * 16, 16), :, :F].astype(f32).reshape(TILE, F)
        sq = x * x
        folded = sq[:, :128]
        for j in range(1, F // 128):
            folded = folded + sq[:, j * 128 : (j + 1) * 128]
        squares[pl.ds(i, 1), :] = to_lanes(folded)
        partial = jnp.dot((x * gain[...]).astype(bf16), weights[...], preferred_element_type=f32)
        for t in range(NT):
            out[t, pl.ds(pl.multiple_of(i * TILE, TILE), TILE), :] = partial[:, t * C : (t + 1) * C].astype(bf16)
        return 0

    lax.fori_loop(0, NTILES, tile, 0)
    high, mid, low = parts(squares[0:4, :])
    tail = jnp.concatenate([high, mid, low, jnp.zeros_like(high)], axis=0).astype(bf16)
    for t in range(NT):
        out[t, ROWS:, :] = tail


def loss_kernel(got, goals, value_out, send, scales, dots):
    tail = got[0, ROWS:, :].astype(f32)
    for t in range(1, NT):
        tail = tail + got[t, ROWS:, :].astype(f32)
    total = tail[0:4] + tail[4:8] + tail[8:12]
    scales[0:4, :] = lax.rsqrt(total / D + epsilon)
    scales[4:8, :] = jnp.zeros((4, 128), f32)

    def tile(i, _):
        here = pl.ds(pl.multiple_of(i * TILE, TILE), TILE)
        total = got[0, here, :].astype(f32)
        for t in range(1, NT):
            total = total + got[t, here, :].astype(f32)
        value = total * to_rows(scales[pl.ds(i, 1), :])
        value_out[pl.ds(i * 16, 16)] = value.reshape(16, MB, C).astype(bf16)
        goal = goals[pl.ds(i * 16, 16), :, F:].astype(f32).reshape(TILE, C)
        grad = (value - goal).astype(bf16)
        for t in range(NT):
            send[t, here, :] = grad
        dots[pl.ds(i, 1), :] = to_lanes(grad.astype(f32) * value)
        return 0

    lax.fori_loop(0, NTILES, tile, 0)
    high, mid, low = parts(dots[0:4, :])
    tail = jnp.concatenate([high, mid, low, jnp.zeros_like(high)], axis=0).astype(bf16)
    for t in range(NT):
        send[t, ROWS:, :] = tail


def grad_kernel(got, rows, gain, weights, scales, value, back, normed, grads, gains, dots):
    tail = got[0, ROWS:, :].astype(f32)
    for t in range(1, NT):
        tail = tail + got[t, ROWS:, :].astype(f32)
    dots[0:4, :] = (tail[0:4] + tail[4:8] + tail[8:12]) / D
    gains[...] = jnp.zeros_like(gains)

    def tile(i, _):
        here = pl.ds(pl.multiple_of(i * TILE, TILE), TILE)
        slots = pl.ds(i * 16, 16)
        for t in range(NT):
            grads[here, t * C : (t + 1) * C] = got[t, here, :]
        grad_normed = lax.dot_general(
            grads[here, :], weights[...], (((1,), (1,)), ((), ())), preferred_element_type=f32
        )
        scale = to_rows(scales[pl.ds(i, 1), :])[:, :1]
        dot = to_rows(dots[pl.ds(i, 1), :])[:, :1]
        normal = rows[slots, :, :F].astype(f32).reshape(TILE, F) * scale
        gained = grad_normed * gain[...]
        row_grad = scale * (gained - normal * dot)
        back[slots, :, :F] = row_grad.reshape(16, MB, F).astype(bf16)
        back[slots, :, F:] = value[slots]
        gains[...] += jnp.sum((grad_normed * normal).reshape(TILE // 8, 8, F), axis=0)
        normed[here, :] = (normal * gain[...]).astype(bf16)
        return 0

    lax.fori_loop(0, NTILES, tile, 0)


def share_kernel(grads, normed, gains, keep, send):
    first = lax.axis_index("core") == 0

    def block(i, _):
        mine = lax.dot_general(
            grads[:, pl.ds(pl.multiple_of(i * 256, 256), 256)],
            normed[...],
            (((0,), (0,)), ((), ())),
            preferred_element_type=f32,
        )
        for j in range(8):
            at = pl.ds(pl.multiple_of(i * 128 + j * 16, 16), 16)
            even = mine[j * 32 : j * 32 + 16, :]
            odd = mine[j * 32 + 16 : j * 32 + 32, :]
            keep[at, :] = jnp.where(first, even, odd)
            send[at, :] = jnp.where(first, odd, even).astype(bf16)
        return 0

    lax.fori_loop(0, KV // 256, block, 0)
    total = jnp.sum(gains[...], axis=0, keepdims=True)
    keep[KV // 2 :, :] = jnp.concatenate([total, jnp.zeros((EXTRA - 1, F), f32)], axis=0)
    send[KV // 2 :, :] = gain_tail(total)


def gain_tail(total):
    high, mid, low = parts(total)
    return jnp.concatenate([high, mid, low, jnp.zeros((EXTRA - 3, F), f32)], axis=0).astype(bf16)


def core_kernel(keep, got, own, *sends):
    me = lax.axis_index("x")
    tail = keep[KV // 2 :, :] + got[KV // 2 :, :].astype(f32)
    tail = jnp.sum(tail, axis=0, keepdims=True)
    here = pl.ds(pl.multiple_of(me * 128, 128), 128)
    own[:128, :] = keep[here, :] + got[here, :].astype(f32)
    own[128:, :] = jnp.concatenate([tail, jnp.zeros((EXTRA - 1, F), f32)], axis=0)
    tail = gain_tail(tail)
    for d, send in enumerate(sends):
        there = pl.ds(pl.multiple_of(lax.rem(me + d + 1, X) * 128, 128), 128)
        send[:128, :] = (keep[there, :] + got[there, :].astype(f32)).astype(bf16)
        send[128:, :] = tail


def x_kernel(own, *refs):
    *got, out = refs
    for i in range(Z):
        at = slice(i * 16, (i + 1) * 16)
        total = own[at, :]
        for g in got:
            total = total + g[at, :].astype(f32)
        out[i, :16, :] = total.astype(bf16)
    tail = own[128:, :]
    for g in got:
        tail = tail + g[128:, :].astype(f32)
    tail = gain_tail(jnp.sum(tail, axis=0, keepdims=True))
    for i in range(Z):
        out[i, 16:, :] = tail


def last_kernel(got, weight_out, gain_out):
    total = got[0].astype(f32)
    for g in range(1, Z):
        total = total + got[g].astype(f32)
    weight_out[...] = total[:16] * GRAD_SCALE
    gain_out[...] = jnp.sum(total[16:], axis=0, keepdims=True) * GRAD_SCALE


def unpack_kernel(routes, got, rows, values):
    def take(m, _):
        d = routes[m]
        rows[m] = got[d, :, :F]
        values[m] = got[d, :, F:]
        return 0

    lax.fori_loop(0, PIECES, take, 0)


def shape(*dims, dtype=bf16):
    return jax.ShapeDtypeStruct(dims, dtype)


def exchange(v, axes):
    return lax.all_to_all(v, axes, split_axis=0, concat_axis=0, tiled=True)


def body(activations, targets, routes, value_weights, norm_gains):
    peer = ("x", "z", "core")
    weights = value_weights[0]
    order = routes[:, 0]
    sends = call(
        pack_kernel,
        shape(NP, MB, F + C),
        [ANY] * 3,
        [pltpu.SMEM((PIECES,), jnp.int32)] + [pltpu.SemaphoreType.DMA] * 3,
        name="pack",
    )(order, activations.reshape(PIECES, MB, F), targets.reshape(PIECES, MB, C))
    arrived = exchange(sends, peer)
    partials = call(
        value_kernel,
        shape(NT, ROWS + EXTRA, C),
        [VMEM] * 3,
        [pltpu.VMEM((8, 128), f32)],
        flops=2 * ROWS * F * KV,
        name="partial_values",
    )(arrived, norm_gains, weights)
    value, grad_part, scales = call(
        loss_kernel,
        (shape(NP, MB, C), shape(NT, ROWS + EXTRA, C), shape(8, 128, dtype=f32)),
        [VMEM] * 2,
        [pltpu.VMEM((8, 128), f32)],
        name="loss",
    )(exchange(partials, "tp"), arrived)
    back, normed, grads, gains = call(
        grad_kernel,
        (shape(NP, MB, F + C), shape(ROWS, F), shape(ROWS, KV), shape(8, F, dtype=f32)),
        [VMEM] * 6,
        [pltpu.VMEM((8, 128), f32)],
        flops=2 * ROWS * F * KV,
        size=8 << 20,
        name="grads",
    )(exchange(grad_part, "tp"), arrived, norm_gains, weights, scales, value)
    rows_back = exchange(back, peer)

    half = (KV // CORES + EXTRA, F)
    keep, send = call(
        share_kernel,
        (shape(*half, dtype=f32), shape(*half)),
        [VMEM] * 3,
        flops=2 * ROWS * F * KV,
        name="share",
    )(grads, normed, gains)
    got = lax.ppermute(send, "core", [(0, 1), (1, 0)])
    block = (KV // CORES // X + EXTRA, F)
    own, *sends = call(
        core_kernel, (shape(*block, dtype=f32),) + (shape(*block),) * (X - 1), [VMEM] * 2, name="sum_core"
    )(keep, got)
    got = [lax.ppermute(v, "x", [(i, (i + d + 1) % X) for i in range(X)]) for d, v in enumerate(sends)]
    by_x = call(x_kernel, shape(Z, 16 + EXTRA, F), [VMEM] * X, name="sum_x")(own, *got)
    by_x, rows_back = lax.optimization_barrier((by_x, rows_back))
    by_z = exchange(by_x, "z")
    weight_grad, gain_grad = call(
        last_kernel, (shape(16, F, dtype=f32), shape(1, F, dtype=f32)), [VMEM], name="sum_z"
    )(by_z)
    grad_rows, values = call(
        unpack_kernel,
        (shape(PIECES, MB, F), shape(PIECES, MB, C)),
        [SMEM, VMEM],
        name="unpack",
    )(order, rows_back)
    return (
        grad_rows.reshape(PIECES * MB, F),
        values.reshape(PIECES * MB, C),
        weight_grad,
        gain_grad[0],
    )


def solution(mesh):
    split = Mesh(mesh.devices.reshape(X, Z, CORES, NT), ("x", "z", "core", "tp"))
    peer = ("x", "z", "core")
    return jax.shard_map(
        body,
        mesh=split,
        in_specs=(
            P(peer, "tp"),
            P(peer, "tp"),
            P(peer, None),
            P(peer, "tp", None),
            P(peer, "tp"),
        ),
        out_specs=(P(peer, "tp"), P(peer, "tp"), P(peer, "tp"), P("tp")),
        check_vma=False,
    )
```

```python
import jax
import jax.numpy as jnp
from jax import lax
from jax.experimental import pallas as pl
from jax.experimental.pallas import tpu as pltpu
from jax.sharding import Mesh, PartitionSpec as P

D = 8192
KV = 1024
PIECES = 32
MB = 8
F = 1024
C = 128
NP = 64
NT = 8
X, Z, CORES = 4, 8, 2
ROWS = NP * MB
TILE = 128
NTILES = ROWS // TILE
EXTRA = 16
GRAD_SCALE = (ROWS // 2 * NP) ** (-0.5)

epsilon = 1e-05
f32 = jnp.float32
bf16 = jnp.bfloat16
VMEM = pl.BlockSpec(memory_space=pltpu.VMEM)
HBM = pl.BlockSpec(memory_space=pltpu.HBM)
SMEM = pl.BlockSpec(memory_space=pltpu.SMEM)


def call(kernel, outs, in_specs, scratch=(), flops=0, size=4 << 20, name=None):
    return pl.pallas_call(
        kernel,
        out_shape=outs,
        in_specs=in_specs,
        out_specs=jax.tree.map(lambda _: VMEM, outs),
        scratch_shapes=scratch,
        compiler_params=pltpu.CompilerParams(vmem_limit_bytes=40 << 20),
        cost_estimate=pl.CostEstimate(flops=flops, bytes_accessed=size, transcendentals=0),
        name=name,
    )


def parts(v):
    high = v.astype(bf16).astype(f32)
    rest = v - high
    mid = rest.astype(bf16).astype(f32)
    return high, mid, rest - mid


def to_lanes(square):
    return jnp.sum(square.T, axis=0, keepdims=True)


def to_rows(lanes):
    return jnp.broadcast_to(lanes, (TILE, TILE)).T


def pack_kernel(routes, acts, goals, out, order, route_sem, row_sem, goal_sem):
    fetch = pltpu.make_async_copy(routes, order, route_sem)
    fetch.start()

    def clear(d, _):
        out[pl.ds(d * 4, 4)] = jnp.zeros((4, MB, F + C), bf16)
        return 0

    lax.fori_loop(0, NP // 4, clear, 0)
    fetch.wait()

    def send(m, _):
        d = order[m]
        pltpu.make_async_copy(acts.at[m], out.at[d, :, pl.ds(0, F)], row_sem).start()
        pltpu.make_async_copy(goals.at[m], out.at[d, :, pl.ds(F, C)], goal_sem).start()
        return 0

    lax.fori_loop(0, PIECES, send, 0)
    pltpu.make_async_copy(acts, out.at[pl.ds(0, PIECES), :, pl.ds(0, F)], row_sem).wait()
    pltpu.make_async_copy(goals, out.at[pl.ds(0, PIECES), :, pl.ds(F, C)], goal_sem).wait()


def value_kernel(rows, gain, weights, out, gained, squares):
    def tile(i, _):
        x = rows[pl.ds(i * 16, 16), :, :F].astype(f32).reshape(TILE, F)
        sq = x * x
        folded = sq[:, :128]
        for j in range(1, F // 128):
            folded = folded + sq[:, j * 128 : (j + 1) * 128]
        squares[pl.ds(i, 1), :] = to_lanes(folded)
        gained[pl.ds(pl.multiple_of(i * TILE, TILE), TILE), :] = (x * gain[...]).astype(bf16)
        return 0

    lax.fori_loop(0, NTILES, tile, 0)
    for i in range(KV // 256):
        partial = jnp.dot(gained[...], weights[:, i * 256 : (i + 1) * 256], preferred_element_type=f32).astype(bf16)
        out[2 * i, :ROWS, :] = partial[:, :C]
        out[2 * i + 1, :ROWS, :] = partial[:, C:]
    high, mid, low = parts(squares[0:4, :])
    tail = jnp.concatenate([high, mid, low, jnp.zeros_like(high)], axis=0).astype(bf16)
    for t in range(NT):
        out[t, ROWS:, :] = tail


def loss_kernel(got, goals, value_out, send, scales, dots):
    tail = got[0, ROWS:, :].astype(f32)
    for t in range(1, NT):
        tail = tail + got[t, ROWS:, :].astype(f32)
    total = tail[0:4] + tail[4:8] + tail[8:12]
    scales[0:4, :] = lax.rsqrt(total / D + epsilon)
    scales[4:8, :] = jnp.zeros((4, 128), f32)

    def tile(i, _):
        here = pl.ds(pl.multiple_of(i * TILE, TILE), TILE)
        total = got[0, here, :].astype(f32)
        for t in range(1, NT):
            total = total + got[t, here, :].astype(f32)
        value = total * to_rows(scales[pl.ds(i, 1), :])
        value_out[pl.ds(i * 16, 16)] = value.reshape(16, MB, C).astype(bf16)
        goal = goals[pl.ds(i * 16, 16), :, F:].astype(f32).reshape(TILE, C)
        grad = (value - goal).astype(bf16)
        for t in range(NT):
            send[t, here, :] = grad
        dots[pl.ds(i, 1), :] = to_lanes(grad.astype(f32) * value)
        return 0

    lax.fori_loop(0, NTILES, tile, 0)
    high, mid, low = parts(dots[0:4, :])
    tail = jnp.concatenate([high, mid, low, jnp.zeros_like(high)], axis=0).astype(bf16)
    for t in range(NT):
        send[t, ROWS:, :] = tail


def normed_kernel(rows, gain, scales, normed):
    def tile(i, _):
        scale = to_rows(scales[pl.ds(i, 1), :])[:, :1]
        normal = rows[pl.ds(i * 16, 16), :, :F].astype(f32).reshape(TILE, F) * scale
        normed[pl.ds(pl.multiple_of(i * TILE, TILE), TILE), :] = (normal * gain[...]).astype(bf16)
        return 0

    lax.fori_loop(0, NTILES, tile, 0)


def grad_kernel(got, rows, gain, weights, scales, value, back, grads, gains, scale_of, dot_of):
    tail = got[0, ROWS:, :].astype(f32)
    for t in range(1, NT):
        tail = tail + got[t, ROWS:, :].astype(f32)
    dots = (tail[0:4] + tail[4:8] + tail[8:12]) / D
    for i in range(NTILES):
        here = slice(i * TILE, (i + 1) * TILE)
        scale = scales[i : i + 1, :]
        scale_of[here, :] = to_rows(scale)
        dot_of[here, :] = to_rows(scale * scale * dots[i : i + 1, :])
    for t in range(NT):
        grads[:, t * C : (t + 1) * C] = got[t, :ROWS, :]
    back[:, :, F:] = value[...]

    for i in range(F // 256):
        at = slice(i * 256, (i + 1) * 256)
        grad_normed = lax.dot_general(
            grads[...], weights[at, :], (((1,), (1,)), ((), ())), preferred_element_type=f32
        )
        scaled = grad_normed * scale_of[:, :1]
        x = rows[:, :, at].astype(f32).reshape(ROWS, 256)
        row_grad = scaled * gain[:, at] - x * dot_of[:, :1]
        back[:, :, at] = row_grad.reshape(NP, MB, 256).astype(bf16)
        gains[:, at] = jnp.sum((scaled * x).reshape(ROWS // 8, 8, 256), axis=0)


def share_kernel(grads, normed, gains, keep, send):
    first = lax.axis_index("core") == 0

    def block(i, _):
        mine = lax.dot_general(
            grads[:, pl.ds(pl.multiple_of(i * 256, 256), 256)],
            normed[...],
            (((0,), (0,)), ((), ())),
            preferred_element_type=f32,
        )
        for j in range(8):
            at = pl.ds(pl.multiple_of(i * 128 + j * 16, 16), 16)
            even = mine[j * 32 : j * 32 + 16, :]
            odd = mine[j * 32 + 16 : j * 32 + 32, :]
            keep[at, :] = jnp.where(first, even, odd)
            send[at, :] = jnp.where(first, odd, even).astype(bf16)
        return 0

    lax.fori_loop(0, KV // 256, block, 0)
    total = jnp.sum(gains[...], axis=0, keepdims=True)
    keep[KV // 2 :, :] = jnp.concatenate([total, jnp.zeros((EXTRA - 1, F), f32)], axis=0)
    high, mid, low = parts(total)
    tail = jnp.concatenate([high, mid, low, jnp.zeros((EXTRA - 3, F), f32)], axis=0)
    send[KV // 2 :, :] = tail.astype(bf16)


def gain_tail(total):
    high = total.astype(bf16).astype(f32)
    return jnp.concatenate([high, total - high], axis=0).astype(bf16)


def core_kernel(keep, got, own, *sends):
    me = lax.axis_index("x")
    tail = keep[KV // 2 :, :] + got[KV // 2 :, :].astype(f32)
    tail = jnp.sum(tail, axis=0, keepdims=True)
    tail = jnp.concatenate([tail[:, j * 128 : (j + 1) * 128] for j in range(F // 128)], axis=0)

    def put(out, d, tail):
        there = pl.ds(pl.multiple_of(lax.rem(me + d, X) * 128, 128), 128)
        total = keep[there, :] + got[there, :].astype(f32)
        for j in range(F // 128):
            out[j * 128 : (j + 1) * 128, :] = total[:, j * 128 : (j + 1) * 128].astype(out.dtype)
        out[F:, :] = tail

    for d, send in enumerate(sends):
        put(send, d + 1, gain_tail(tail))
    put(own, 0, jnp.concatenate([tail, jnp.zeros_like(tail)], axis=0))


def x_kernel(own, *refs):
    *got, out = refs
    for z in range(Z):
        for j in range(F // 128):
            at = slice(j * 128 + z * 16, j * 128 + z * 16 + 16)
            total = own[at, :]
            for g in got:
                total = total + g[at, :].astype(f32)
            out[z, j * 16 : (j + 1) * 16, :] = total.astype(bf16)
    tail = own[F:, :]
    for g in got:
        tail = tail + g[F:, :].astype(f32)
    tail = gain_tail(tail[:8] + tail[8:])
    for z in range(Z):
        out[z, 128:, :] = tail


def last_kernel(got, weight_out, gain_out):
    total = got[0].astype(f32)
    for z in range(1, Z):
        total = total + got[z].astype(f32)
    total = total * GRAD_SCALE
    tail = total[128:136] + total[136:]
    for j in range(F // 128):
        at = slice(j * 128, (j + 1) * 128)
        weight_out[:, at] = total[j * 16 : (j + 1) * 16]
        gain_out[:, at] = tail[j : j + 1]


def unpack_kernel(routes, got, rows, values):
    def take(m, _):
        d = routes[m]
        rows[m] = got[d, :, :F]
        values[m] = got[d, :, F:]
        return 0

    lax.fori_loop(0, PIECES, take, 0)


def shape(*dims, dtype=bf16):
    return jax.ShapeDtypeStruct(dims, dtype)


def exchange(v, axes):
    return lax.all_to_all(v, axes, split_axis=0, concat_axis=0, tiled=True)


def body(activations, targets, routes, value_weights, norm_gains):
    peer = ("x", "z", "core")
    weights = value_weights[0]
    order = routes[:, 0]
    given = order, activations.reshape(PIECES, MB, F), targets.reshape(PIECES, MB, C)
    sends = call(
        pack_kernel,
        shape(NP, MB, F + C),
        [HBM] * 3,
        [pltpu.SMEM((PIECES,), jnp.int32)] + [pltpu.SemaphoreType.DMA] * 3,
        name="pack",
    )(*[pltpu.with_memory_space_constraint(v, pltpu.HBM) for v in given])
    arrived = exchange(sends, peer)
    partials = call(
        value_kernel,
        shape(NT, ROWS + EXTRA, C),
        [VMEM] * 3,
        [pltpu.VMEM((ROWS, F), bf16), pltpu.VMEM((8, 128), f32)],
        flops=2 * ROWS * F * KV,
        name="partial_values",
    )(arrived, norm_gains, weights)
    value, grad_part, scales = call(
        loss_kernel,
        (shape(NP, MB, C), shape(NT, ROWS + EXTRA, C), shape(8, 128, dtype=f32)),
        [VMEM] * 2,
        [pltpu.VMEM((8, 128), f32)],
        name="loss",
    )(exchange(partials, "tp"), arrived)
    normed = call(normed_kernel, shape(ROWS, F), [VMEM] * 3, name="normed")(arrived, norm_gains, scales)
    back, grads, gains = call(
        grad_kernel,
        (shape(NP, MB, F + C), shape(ROWS, KV), shape(8, F, dtype=f32)),
        [VMEM] * 6,
        [pltpu.VMEM((ROWS, 128), f32)] * 2,
        flops=2 * ROWS * F * KV,
        size=8 << 20,
        name="grads",
    )(exchange(grad_part, "tp"), arrived, norm_gains, weights, scales, value)
    rows_back = exchange(back, peer)

    half = (KV // CORES + EXTRA, F)
    keep, send = call(
        share_kernel,
        (shape(*half, dtype=f32), shape(*half)),
        [VMEM] * 3,
        flops=2 * ROWS * F * KV,
        name="share",
    )(grads, normed, gains)
    got = lax.ppermute(send, "core", [(0, 1), (1, 0)])
    block = (F + EXTRA, 128)
    own, *sends = call(
        core_kernel, (shape(*block, dtype=f32),) + (shape(*block),) * (X - 1), [VMEM] * 2, name="sum_core"
    )(keep, got)
    got = [lax.ppermute(v, "x", [(i, (i + d + 1) % X) for i in range(X)]) for d, v in enumerate(sends)]
    by_x = call(x_kernel, shape(Z, 128 + EXTRA, 128), [VMEM] * X, name="sum_x")(own, *got)
    by_x, rows_back = lax.optimization_barrier((by_x, rows_back))
    by_z = exchange(by_x, "z")
    weight_grad, gain_grad = call(
        last_kernel, (shape(16, F, dtype=f32), shape(1, F, dtype=f32)), [VMEM], name="sum_z"
    )(by_z)
    grad_rows, values = call(
        unpack_kernel,
        (shape(PIECES, MB, F), shape(PIECES, MB, C)),
        [SMEM, VMEM],
        name="unpack",
    )(order, rows_back)
    return (
        grad_rows.reshape(PIECES * MB, F),
        values.reshape(PIECES * MB, C),
        weight_grad,
        gain_grad[0],
    )


def solution(mesh):
    split = Mesh(mesh.devices.reshape(X, Z, CORES, NT), ("x", "z", "core", "tp"))
    peer = ("x", "z", "core")
    return jax.shard_map(
        body,
        mesh=split,
        in_specs=(
            P(peer, "tp"),
            P(peer, "tp"),
            P(peer, None),
            P(peer, "tp", None),
            P(peer, "tp"),
        ),
        out_specs=(P(peer, "tp"), P(peer, "tp"), P(peer, "tp"), P("tp")),
        check_vma=False,
    )
```

```python
import functools

import jax
import jax.numpy as jnp
from jax import lax
from jax.experimental import pallas as pl
from jax.experimental.pallas import tpu as pltpu
from jax.sharding import Mesh, PartitionSpec as P

D = 8192
KV = 1024
PIECES = 32
MB = 8
F = 1024
C = 128
NP = 64
NT = 8
X, Z, CORES = 4, 8, 2
ROWS = NP * MB
TILE = 128
NTILES = ROWS // TILE
EXTRA = 16
GRAD_SCALE = (ROWS // 2 * NP) ** (-0.5)

epsilon = 1e-05
f32 = jnp.float32
bf16 = jnp.bfloat16
VMEM = pl.BlockSpec(memory_space=pltpu.VMEM)
HBM = pl.BlockSpec(memory_space=pltpu.HBM)
SMEM = pl.BlockSpec(memory_space=pltpu.SMEM)


def call(kernel, outs, in_specs, scratch=(), flops=0, size=4 << 20, name=None):
    return pl.pallas_call(
        kernel,
        out_shape=outs,
        in_specs=in_specs,
        out_specs=jax.tree.map(lambda _: VMEM, outs),
        scratch_shapes=scratch,
        compiler_params=pltpu.CompilerParams(vmem_limit_bytes=18 << 20),
        cost_estimate=pl.CostEstimate(flops=flops, bytes_accessed=size, transcendentals=0),
        name=name,
    )


def parts(v):
    high = v.astype(bf16).astype(f32)
    rest = v - high
    mid = rest.astype(bf16).astype(f32)
    return high, mid, rest - mid


def to_lanes(square):
    return jnp.sum(square.T, axis=0, keepdims=True)


def to_rows(lanes):
    return jnp.broadcast_to(lanes, (TILE, TILE)).T


def pack_kernel(routes, acts, goals, out, order, route_sem, row_sem, goal_sem):
    fetch = pltpu.make_async_copy(routes, order, route_sem)
    fetch.start()

    def clear(d, _):
        out[pl.ds(d * 4, 4)] = jnp.zeros((4, MB, F + C), bf16)
        return 0

    lax.fori_loop(0, NP // 4, clear, 0)
    fetch.wait()

    def send(m, _):
        d = order[m]
        pltpu.make_async_copy(acts.at[m], out.at[d, :, pl.ds(0, F)], row_sem).start()
        pltpu.make_async_copy(goals.at[m], out.at[d, :, pl.ds(F, C)], goal_sem).start()
        return 0

    lax.fori_loop(0, PIECES, send, 0)
    pltpu.make_async_copy(acts, out.at[pl.ds(0, PIECES), :, pl.ds(0, F)], row_sem).wait()
    pltpu.make_async_copy(goals, out.at[pl.ds(0, PIECES), :, pl.ds(F, C)], goal_sem).wait()


def value_kernel(rows, gain, weights, out, gained, squares):
    def tile(i, _):
        x = rows[pl.ds(i * 16, 16), :, :F].astype(f32).reshape(TILE, F)
        sq = x * x
        folded = sq[:, :128]
        for j in range(1, F // 128):
            folded = folded + sq[:, j * 128 : (j + 1) * 128]
        squares[pl.ds(i, 1), :] = to_lanes(folded)
        gained[pl.ds(pl.multiple_of(i * TILE, TILE), TILE), :] = (x * gain[...]).astype(bf16)
        return 0

    lax.fori_loop(0, NTILES, tile, 0)
    for i in range(KV // 256):
        partial = jnp.dot(gained[...], weights[:, i * 256 : (i + 1) * 256], preferred_element_type=f32).astype(bf16)
        out[2 * i, :ROWS, :] = partial[:, :C]
        out[2 * i + 1, :ROWS, :] = partial[:, C:]
    high, mid, low = parts(squares[0:4, :])
    tail = jnp.concatenate([high, mid, low, jnp.zeros_like(high)], axis=0).astype(bf16)
    for t in range(NT):
        out[t, ROWS:, :] = tail


def loss_kernel(got, goals, value_out, send, scales, dots):
    tail = got[0, ROWS:, :].astype(f32)
    for t in range(1, NT):
        tail = tail + got[t, ROWS:, :].astype(f32)
    total = tail[0:4] + tail[4:8] + tail[8:12]
    scales[0:4, :] = lax.rsqrt(total / D + epsilon)
    scales[4:8, :] = jnp.zeros((4, 128), f32)

    def tile(i, _):
        here = pl.ds(pl.multiple_of(i * TILE, TILE), TILE)
        total = got[0, here, :].astype(f32)
        for t in range(1, NT):
            total = total + got[t, here, :].astype(f32)
        value = total * to_rows(scales[pl.ds(i, 1), :])
        value_out[pl.ds(i * 16, 16)] = value.reshape(16, MB, C).astype(bf16)
        goal = goals[pl.ds(i * 16, 16), :, F:].astype(f32).reshape(TILE, C)
        grad = (value - goal).astype(bf16)
        for t in range(NT):
            send[t, here, :] = grad
        dots[pl.ds(i, 1), :] = to_lanes(grad.astype(f32) * value)
        return 0

    lax.fori_loop(0, NTILES, tile, 0)
    high, mid, low = parts(dots[0:4, :])
    tail = jnp.concatenate([high, mid, low, jnp.zeros_like(high)], axis=0).astype(bf16)
    for t in range(NT):
        send[t, ROWS:, :] = tail


def normal_kernel(rows, scales, normal):
    def tile(i, _):
        scale = to_rows(scales[pl.ds(i, 1), :])[:, :1]
        x = rows[pl.ds(i * 16, 16), :, :F].astype(f32).reshape(TILE, F)
        normal[pl.ds(pl.multiple_of(i * TILE, TILE), TILE), :] = (x * scale).astype(bf16)
        return 0

    lax.fori_loop(0, NTILES, tile, 0)


def share_kernel(got, normal, gain, flipped, keep, send, grads, gains):
    first = lax.axis_index("core") == 0
    gains[...] = jnp.zeros_like(gains)

    def block(i, _):
        both = jnp.concatenate([got[2 * i, :ROWS, :], got[2 * i + 1, :ROWS, :]], axis=1)
        grads[i] = both
        mine = lax.dot_general(both, normal[...], (((0,), (0,)), ((), ())), preferred_element_type=f32)
        here = pl.ds(pl.multiple_of(i * 256, 256), 256)
        gains[...] += jnp.sum((mine * flipped[here, :].astype(f32)).reshape(32, 8, F), axis=0)
        mine = mine * gain[...]
        for j in range(8):
            at = pl.ds(pl.multiple_of(i * 128 + j * 16, 16), 16)
            even = mine[j * 32 : j * 32 + 16, :]
            odd = mine[j * 32 + 16 : j * 32 + 32, :]
            keep[at, :] = jnp.where(first, even, odd)
            send[at, :] = jnp.where(first, odd, even).astype(bf16)
        return 0

    lax.fori_loop(0, KV // 256, block, 0)
    total = jnp.sum(gains[...], axis=0, keepdims=True)
    keep[KV // 2 :, :] = jnp.concatenate([total, jnp.zeros((EXTRA - 1, F), f32)], axis=0)
    high, mid, low = parts(total)
    tail = jnp.concatenate([high, mid, low, jnp.zeros((EXTRA - 3, F), f32)], axis=0)
    send[KV // 2 :, :] = tail.astype(bf16)


def grad_kernel(got, grads, rows, gain, flipped, scales, value, back, scale_of, dot_of):
    tail = got[0, ROWS:, :].astype(f32)
    for t in range(1, NT):
        tail = tail + got[t, ROWS:, :].astype(f32)
    dots = (tail[0:4] + tail[4:8] + tail[8:12]) / D
    for i in range(NTILES):
        here = slice(i * TILE, (i + 1) * TILE)
        scale = scales[i : i + 1, :]
        scale_of[here, :] = to_rows(scale)
        dot_of[here, :] = to_rows(scale * scale * dots[i : i + 1, :])
    back[:, :, F:] = value[...]

    for i in range(F // 256):
        at = slice(i * 256, (i + 1) * 256)
        grad_normed = jnp.zeros((ROWS, 256), f32)
        for k in range(KV // 256):
            grad_normed += jnp.dot(
                grads[k], flipped[k * 256 : (k + 1) * 256, at], preferred_element_type=f32
            )
        x = rows[:, :, at].astype(f32).reshape(ROWS, 256)
        row_grad = grad_normed * scale_of[:, :1] * gain[:, at] - x * dot_of[:, :1]
        back[:, :, at] = row_grad.reshape(NP, MB, 256).astype(bf16)


def gain_tail(total):
    high = total.astype(bf16).astype(f32)
    return jnp.concatenate([high, total - high], axis=0).astype(bf16)


def own_tail(total):
    return jnp.concatenate([total, jnp.zeros_like(total)], axis=0)


def core_kernel(keep, got, own, *sends):
    me = lax.axis_index("x")
    tail = keep[KV // 2 :, :] + got[KV // 2 :, :].astype(f32)
    tail = jnp.sum(tail, axis=0, keepdims=True)
    tail = jnp.concatenate([tail[:, j * 128 : (j + 1) * 128] for j in range(F // 128)], axis=0)

    def put(out, d, tail):
        there = pl.ds(pl.multiple_of(lax.rem(me + d, X) * 128, 128), 128)
        total = keep[there, :] + got[there, :].astype(f32)
        for j in range(F // 128):
            out[j * 128 : (j + 1) * 128, :] = total[:, j * 128 : (j + 1) * 128].astype(out.dtype)
        out[F:, :] = tail

    for d, send in enumerate(sends):
        put(send, d + 1, gain_tail(tail))
    put(own, 0, own_tail(tail))


def x_kernel(own, *refs):
    *got, keep, send = refs
    bit = lax.rem(lax.axis_index("z"), 2)

    def put(out, bit, tail):
        for q in range(Z // 2):
            for j in range(F // 128):
                at = pl.ds(pl.multiple_of(j * 128 + (2 * q + bit) * 16, 16), 16)
                total = own[at, :]
                for g in got:
                    total = total + g[at, :].astype(f32)
                out[q * 128 + j * 16 : q * 128 + (j + 1) * 16, :] = total.astype(out.dtype)
        out[Z // 2 * 128 :, :] = tail

    tail = own[F:, :]
    for g in got:
        tail = tail + g[F:, :].astype(f32)
    tail = tail[:8] + tail[8:]
    put(send, 1 - bit, gain_tail(tail))
    put(keep, bit, own_tail(tail))


def z_kernel(count, own, got, keep, send):
    bit = lax.rem(lax.axis_index("z") // (Z // count), 2)

    def put(out, bit, tail):
        for q in range(count // 2):
            at = pl.ds(pl.multiple_of((2 * q + bit) * 128, 128), 128)
            out[q * 128 : (q + 1) * 128, :] = (own[at, :] + got[at, :].astype(f32)).astype(out.dtype)
        out[count // 2 * 128 :, :] = tail

    tail = own[count * 128 :, :] + got[count * 128 :, :].astype(f32)
    tail = tail[:8] + tail[8:]
    put(send, 1 - bit, gain_tail(tail))
    put(keep, bit, own_tail(tail))


def last_kernel(own, got, weight_out, gain_out):
    total = (own[...] + got[...].astype(f32)) * GRAD_SCALE
    tail = total[128:136] + total[136:]
    for j in range(F // 128):
        at = slice(j * 128, (j + 1) * 128)
        weight_out[:, at] = total[j * 16 : (j + 1) * 16]
        gain_out[:, at] = tail[j : j + 1]


def unpack_kernel(routes, got, rows, values):
    def take(m, _):
        d = routes[m]
        rows[m] = got[d, :, :F]
        values[m] = got[d, :, F:]
        return 0

    lax.fori_loop(0, PIECES, take, 0)


def shape(*dims, dtype=bf16):
    return jax.ShapeDtypeStruct(dims, dtype)


def exchange(v, axes):
    return lax.all_to_all(v, axes, split_axis=0, concat_axis=0, tiled=True)


def body(activations, targets, routes, value_weights, norm_gains):
    peer = ("x", "z", "core")
    weights = value_weights[0]
    flipped = weights.T
    order = routes[:, 0]
    given = order, activations.reshape(PIECES, MB, F), targets.reshape(PIECES, MB, C)
    sends = call(
        pack_kernel,
        shape(NP, MB, F + C),
        [HBM] * 3,
        [pltpu.SMEM((PIECES,), jnp.int32)] + [pltpu.SemaphoreType.DMA] * 3,
        name="pack",
    )(*[pltpu.with_memory_space_constraint(v, pltpu.HBM) for v in given])
    arrived = exchange(sends, peer)
    partials = call(
        value_kernel,
        shape(NT, ROWS + EXTRA, C),
        [VMEM] * 3,
        [pltpu.VMEM((ROWS, F), bf16), pltpu.VMEM((8, 128), f32)],
        flops=2 * ROWS * F * KV,
        name="partial_values",
    )(arrived, norm_gains, weights)
    value, grad_part, scales = call(
        loss_kernel,
        (shape(NP, MB, C), shape(NT, ROWS + EXTRA, C), shape(8, 128, dtype=f32)),
        [VMEM] * 2,
        [pltpu.VMEM((8, 128), f32)],
        name="loss",
    )(exchange(partials, "tp"), arrived)
    normal = call(normal_kernel, shape(ROWS, F), [VMEM] * 2, name="normal")(arrived, scales)
    got = exchange(grad_part, "tp")

    half = (KV // CORES + EXTRA, F)
    keep, send, grads = call(
        share_kernel,
        (shape(*half, dtype=f32), shape(*half), shape(KV // 256, ROWS, 256)),
        [VMEM] * 4,
        [pltpu.VMEM((8, F), f32)],
        flops=2 * ROWS * F * KV,
        name="share",
    )(got, normal, norm_gains, flipped)
    by_core = lax.ppermute(send, "core", [(0, 1), (1, 0)])
    back = call(
        grad_kernel,
        shape(NP, MB, F + C),
        [VMEM] * 7,
        [pltpu.VMEM((ROWS, 128), f32)] * 2,
        flops=2 * ROWS * F * KV,
        size=8 << 20,
        name="grads",
    )(got, grads, arrived, norm_gains, flipped, scales, value)

    block = (F + EXTRA, 128)
    own, *sends = call(
        core_kernel, (shape(*block, dtype=f32),) + (shape(*block),) * (X - 1), [VMEM] * 2, name="sum_core"
    )(keep, by_core)
    by_x = [lax.ppermute(v, "x", [(i, (i + d + 1) % X) for i in range(X)]) for d, v in enumerate(sends)]
    back, by_x = lax.optimization_barrier((back, by_x))
    rows_back = exchange(back, peer)

    def halves(count):
        return shape(count * 128 + EXTRA, 128, dtype=f32), shape(count * 128 + EXTRA, 128)

    def swap(v, step):
        return lax.ppermute(v, "z", [(i, i ^ step) for i in range(Z)])

    keep, send = call(x_kernel, halves(4), [VMEM] * X, name="sum_x")(own, *by_x)
    keep, send = call(functools.partial(z_kernel, 4), halves(2), [VMEM] * 2, name="sum_z1")(keep, swap(send, 1))
    keep, send = call(functools.partial(z_kernel, 2), halves(1), [VMEM] * 2, name="sum_z2")(keep, swap(send, 2))
    weight_grad, gain_grad = call(
        last_kernel, (shape(16, F, dtype=f32), shape(1, F, dtype=f32)), [VMEM] * 2, name="sum_z4"
    )(keep, swap(send, 4))
    grad_rows, values = call(
        unpack_kernel,
        (shape(PIECES, MB, F), shape(PIECES, MB, C)),
        [SMEM, VMEM],
        name="unpack",
    )(order, rows_back)
    return (
        grad_rows.reshape(PIECES * MB, F),
        values.reshape(PIECES * MB, C),
        weight_grad,
        gain_grad[0],
    )


def solution(mesh):
    split = Mesh(mesh.devices.reshape(X, Z, CORES, NT), ("x", "z", "core", "tp"))
    peer = ("x", "z", "core")
    return jax.shard_map(
        body,
        mesh=split,
        in_specs=(
            P(peer, "tp"),
            P(peer, "tp"),
            P(peer, None),
            P(peer, "tp", None),
            P(peer, "tp"),
        ),
        out_specs=(P(peer, "tp"), P(peer, "tp"), P(peer, "tp"), P("tp")),
        check_vma=False,
    )
```

```python
import jax
import jax.numpy as jnp
from jax import lax
from jax.experimental import pallas as pl
from jax.experimental.pallas import tpu as pltpu
from jax.sharding import Mesh, PartitionSpec as P

D = 8192
KV = 1024
PIECES = 32
MB = 8
F = 1024
C = 128
NP = 64
NT = 8
X, Z, CORES = 4, 8, 2
ROWS = NP * MB
TILE = 128
NTILES = ROWS // TILE
EXTRA = 16
GRAD_SCALE = (ROWS // 2 * NP) ** (-0.5)

epsilon = 1e-05
f32 = jnp.float32
bf16 = jnp.bfloat16
VMEM = pl.BlockSpec(memory_space=pltpu.VMEM)
HBM = pl.BlockSpec(memory_space=pltpu.HBM)
SMEM = pl.BlockSpec(memory_space=pltpu.SMEM)


def call(kernel, outs, in_specs, scratch=(), flops=0, size=4 << 20, name=None):
    return pl.pallas_call(
        kernel,
        out_shape=outs,
        in_specs=in_specs,
        out_specs=jax.tree.map(lambda _: VMEM, outs),
        scratch_shapes=scratch,
        compiler_params=pltpu.CompilerParams(vmem_limit_bytes=40 << 20),
        cost_estimate=pl.CostEstimate(flops=flops, bytes_accessed=size, transcendentals=0),
        name=name,
    )


def parts(v):
    high = v.astype(bf16).astype(f32)
    rest = v - high
    mid = rest.astype(bf16).astype(f32)
    return high, mid, rest - mid


def to_lanes(square):
    return jnp.sum(square.T, axis=0, keepdims=True)


def to_rows(lanes):
    return jnp.broadcast_to(lanes, (TILE, TILE)).T


def pack_kernel(routes, acts, goals, out, order, route_sem, row_sem, goal_sem):
    fetch = pltpu.make_async_copy(routes, order, route_sem)
    fetch.start()

    def clear(d, _):
        out[pl.ds(d * 4, 4)] = jnp.zeros((4, MB, F + C), bf16)
        return 0

    lax.fori_loop(0, NP // 4, clear, 0)
    fetch.wait()

    def send(m, _):
        d = order[m]
        pltpu.make_async_copy(acts.at[m], out.at[d, :, pl.ds(0, F)], row_sem).start()
        pltpu.make_async_copy(goals.at[m], out.at[d, :, pl.ds(F, C)], goal_sem).start()
        return 0

    lax.fori_loop(0, PIECES, send, 0)
    pltpu.make_async_copy(acts, out.at[pl.ds(0, PIECES), :, pl.ds(0, F)], row_sem).wait()
    pltpu.make_async_copy(goals, out.at[pl.ds(0, PIECES), :, pl.ds(F, C)], goal_sem).wait()


def value_kernel(rows, gain, weights, out, gained, squares):
    def tile(i, _):
        x = rows[pl.ds(i * 16, 16), :, :F].astype(f32).reshape(TILE, F)
        sq = x * x
        folded = sq[:, :128]
        for j in range(1, F // 128):
            folded = folded + sq[:, j * 128 : (j + 1) * 128]
        squares[pl.ds(i, 1), :] = to_lanes(folded)
        gained[pl.ds(pl.multiple_of(i * TILE, TILE), TILE), :] = (x * gain[...]).astype(bf16)
        return 0

    lax.fori_loop(0, NTILES, tile, 0)
    for i in range(KV // 256):
        partial = jnp.dot(gained[...], weights[:, i * 256 : (i + 1) * 256], preferred_element_type=f32).astype(bf16)
        out[2 * i, :ROWS, :] = partial[:, :C]
        out[2 * i + 1, :ROWS, :] = partial[:, C:]
    high, mid, low = parts(squares[0:4, :])
    tail = jnp.concatenate([high, mid, low, jnp.zeros_like(high)], axis=0).astype(bf16)
    for t in range(NT):
        out[t, ROWS:, :] = tail


def loss_kernel(got, goals, value_out, send, scales, dots):
    tail = got[0, ROWS:, :].astype(f32)
    for t in range(1, NT):
        tail = tail + got[t, ROWS:, :].astype(f32)
    total = tail[0:4] + tail[4:8] + tail[8:12]
    scales[0:4, :] = lax.rsqrt(total / D + epsilon)
    scales[4:8, :] = jnp.zeros((4, 128), f32)

    def tile(i, _):
        here = pl.ds(pl.multiple_of(i * TILE, TILE), TILE)
        total = got[0, here, :].astype(f32)
        for t in range(1, NT):
            total = total + got[t, here, :].astype(f32)
        value = total * to_rows(scales[pl.ds(i, 1), :])
        value_out[pl.ds(i * 16, 16)] = value.reshape(16, MB, C).astype(bf16)
        goal = goals[pl.ds(i * 16, 16), :, F:].astype(f32).reshape(TILE, C)
        grad = (value - goal).astype(bf16)
        for t in range(NT):
            send[t, here, :] = grad
        dots[pl.ds(i, 1), :] = to_lanes(grad.astype(f32) * value)
        return 0

    lax.fori_loop(0, NTILES, tile, 0)
    high, mid, low = parts(dots[0:4, :])
    tail = jnp.concatenate([high, mid, low, jnp.zeros_like(high)], axis=0).astype(bf16)
    for t in range(NT):
        send[t, ROWS:, :] = tail


def normed_kernel(rows, gain, scales, normed):
    def tile(i, _):
        scale = to_rows(scales[pl.ds(i, 1), :])[:, :1]
        normal = rows[pl.ds(i * 16, 16), :, :F].astype(f32).reshape(TILE, F) * scale
        normed[pl.ds(pl.multiple_of(i * TILE, TILE), TILE), :] = (normal * gain[...]).astype(bf16)
        return 0

    lax.fori_loop(0, NTILES, tile, 0)


def grad_kernel(got, rows, gain, weights, scales, value, back, grads, gains, scale_of, dot_of):
    tail = got[0, ROWS:, :].astype(f32)
    for t in range(1, NT):
        tail = tail + got[t, ROWS:, :].astype(f32)
    dots = (tail[0:4] + tail[4:8] + tail[8:12]) / D
    for i in range(NTILES):
        here = slice(i * TILE, (i + 1) * TILE)
        scale = scales[i : i + 1, :]
        scale_of[here, :] = to_rows(scale)
        dot_of[here, :] = to_rows(scale * scale * dots[i : i + 1, :])
    for t in range(NT):
        grads[:, t * C : (t + 1) * C] = got[t, :ROWS, :]
    back[:, :, F:] = value[...]

    for i in range(F // 256):
        at = slice(i * 256, (i + 1) * 256)
        grad_normed = lax.dot_general(
            grads[...], weights[at, :], (((1,), (1,)), ((), ())), preferred_element_type=f32
        )
        scaled = grad_normed * scale_of[:, :1]
        x = rows[:, :, at].astype(f32).reshape(ROWS, 256)
        row_grad = scaled * gain[:, at] - x * dot_of[:, :1]
        back[:, :, at] = row_grad.reshape(NP, MB, 256).astype(bf16)
        gains[:, at] = jnp.sum((scaled * x).reshape(ROWS // 8, 8, 256), axis=0)


def share_kernel(grads, normed, gains, keep, send):
    first = lax.axis_index("core") == 0

    def block(i, _):
        mine = lax.dot_general(
            grads[:, pl.ds(pl.multiple_of(i * 256, 256), 256)],
            normed[...],
            (((0,), (0,)), ((), ())),
            preferred_element_type=f32,
        )
        for j in range(8):
            at = pl.ds(pl.multiple_of(i * 128 + j * 16, 16), 16)
            even = mine[j * 32 : j * 32 + 16, :]
            odd = mine[j * 32 + 16 : j * 32 + 32, :]
            keep[at, :] = jnp.where(first, even, odd)
            send[at, :] = jnp.where(first, odd, even).astype(bf16)
        return 0

    lax.fori_loop(0, KV // 256, block, 0)
    total = jnp.sum(gains[...], axis=0, keepdims=True)
    keep[KV // 2 :, :] = jnp.concatenate([total, jnp.zeros((EXTRA - 1, F), f32)], axis=0)
    high, mid, low = parts(total)
    tail = jnp.concatenate([high, mid, low, jnp.zeros((EXTRA - 3, F), f32)], axis=0)
    send[KV // 2 :, :] = tail.astype(bf16)


def gain_tail(total):
    high = total.astype(bf16).astype(f32)
    return jnp.concatenate([high, total - high], axis=0).astype(bf16)


def core_kernel(keep, got, own, *sends):
    me = lax.axis_index("x")
    tail = keep[KV // 2 :, :] + got[KV // 2 :, :].astype(f32)
    tail = jnp.sum(tail, axis=0, keepdims=True)
    tail = jnp.concatenate([tail[:, j * 128 : (j + 1) * 128] for j in range(F // 128)], axis=0)

    def put(out, d, tail):
        there = pl.ds(pl.multiple_of(lax.rem(me + d, X) * 128, 128), 128)
        total = keep[there, :] + got[there, :].astype(f32)
        for j in range(F // 128):
            out[j * 128 : (j + 1) * 128, :] = total[:, j * 128 : (j + 1) * 128].astype(out.dtype)
        out[F:, :] = tail

    for d, send in enumerate(sends):
        put(send, d + 1, gain_tail(tail))
    put(own, 0, jnp.concatenate([tail, jnp.zeros_like(tail)], axis=0))


def x_kernel(own, *refs):
    *got, out = refs
    for z in range(Z):
        for j in range(F // 128):
            at = slice(j * 128 + z * 16, j * 128 + z * 16 + 16)
            total = own[at, :]
            for g in got:
                total = total + g[at, :].astype(f32)
            out[z, j * 16 : (j + 1) * 16, :] = total.astype(bf16)
    tail = own[F:, :]
    for g in got:
        tail = tail + g[F:, :].astype(f32)
    tail = gain_tail(tail[:8] + tail[8:])
    for z in range(Z):
        out[z, 128:, :] = tail


def last_kernel(got, weight_out, gain_out):
    total = got[0].astype(f32)
    for z in range(1, Z):
        total = total + got[z].astype(f32)
    total = total * GRAD_SCALE
    tail = total[128:136] + total[136:]
    for j in range(F // 128):
        at = slice(j * 128, (j + 1) * 128)
        weight_out[:, at] = total[j * 16 : (j + 1) * 16]
        gain_out[:, at] = tail[j : j + 1]


def unpack_kernel(routes, got, rows, values):
    def take(m, _):
        d = routes[m]
        rows[m] = got[d, :, :F]
        values[m] = got[d, :, F:]
        return 0

    lax.fori_loop(0, PIECES, take, 0)


def shape(*dims, dtype=bf16):
    return jax.ShapeDtypeStruct(dims, dtype)


def exchange(v, axes):
    return lax.all_to_all(v, axes, split_axis=0, concat_axis=0, tiled=True)


def body(activations, targets, routes, value_weights, norm_gains):
    peer = ("x", "z", "core")
    weights = value_weights[0]
    order = routes[:, 0]
    given = order, activations.reshape(PIECES, MB, F), targets.reshape(PIECES, MB, C)
    sends = call(
        pack_kernel,
        shape(NP, MB, F + C),
        [HBM] * 3,
        [pltpu.SMEM((PIECES,), jnp.int32)] + [pltpu.SemaphoreType.DMA] * 3,
        name="pack",
    )(*[pltpu.with_memory_space_constraint(v, pltpu.HBM) for v in given])
    arrived = exchange(sends, peer)
    partials = call(
        value_kernel,
        shape(NT, ROWS + EXTRA, C),
        [VMEM] * 3,
        [pltpu.VMEM((ROWS, F), bf16), pltpu.VMEM((8, 128), f32)],
        flops=2 * ROWS * F * KV,
        name="partial_values",
    )(arrived, norm_gains, weights)
    value, grad_part, scales = call(
        loss_kernel,
        (shape(NP, MB, C), shape(NT, ROWS + EXTRA, C), shape(8, 128, dtype=f32)),
        [VMEM] * 2,
        [pltpu.VMEM((8, 128), f32)],
        name="loss",
    )(exchange(partials, "tp"), arrived)
    normed = call(normed_kernel, shape(ROWS, F), [VMEM] * 3, name="normed")(arrived, norm_gains, scales)
    back, grads, gains = call(
        grad_kernel,
        (shape(NP, MB, F + C), shape(ROWS, KV), shape(8, F, dtype=f32)),
        [VMEM] * 6,
        [pltpu.VMEM((ROWS, 128), f32)] * 2,
        flops=2 * ROWS * F * KV,
        size=8 << 20,
        name="grads",
    )(exchange(grad_part, "tp"), arrived, norm_gains, weights, scales, value)
    rows_back = exchange(back, peer)

    half = (KV // CORES + EXTRA, F)
    keep, send = call(
        share_kernel,
        (shape(*half, dtype=f32), shape(*half)),
        [VMEM] * 3,
        flops=2 * ROWS * F * KV,
        name="share",
    )(grads, normed, gains)
    got = lax.ppermute(send, "core", [(0, 1), (1, 0)])
    block = (F + EXTRA, 128)
    own, *sends = call(
        core_kernel, (shape(*block, dtype=f32),) + (shape(*block),) * (X - 1), [VMEM] * 2, name="sum_core"
    )(keep, got)
    got = [lax.ppermute(v, "x", [(i, (i + d + 1) % X) for i in range(X)]) for d, v in enumerate(sends)]
    grad_rows, values = call(
        unpack_kernel,
        (shape(PIECES, MB, F), shape(PIECES, MB, C)),
        [SMEM, VMEM],
        name="unpack",
    )(order, rows_back)
    got, grad_rows, values = lax.optimization_barrier((got, grad_rows, values))
    by_x = call(x_kernel, shape(Z, 128 + EXTRA, 128), [VMEM] * X, name="sum_x")(own, *got)
    by_z = exchange(by_x, "z")
    weight_grad, gain_grad = call(
        last_kernel, (shape(16, F, dtype=f32), shape(1, F, dtype=f32)), [VMEM], name="sum_z"
    )(by_z)
    return (
        grad_rows.reshape(PIECES * MB, F),
        values.reshape(PIECES * MB, C),
        weight_grad,
        gain_grad[0],
    )


def solution(mesh):
    split = Mesh(mesh.devices.reshape(X, Z, CORES, NT), ("x", "z", "core", "tp"))
    peer = ("x", "z", "core")
    return jax.shard_map(
        body,
        mesh=split,
        in_specs=(
            P(peer, "tp"),
            P(peer, "tp"),
            P(peer, None),
            P(peer, "tp", None),
            P(peer, "tp"),
        ),
        out_specs=(P(peer, "tp"), P(peer, "tp"), P(peer, "tp"), P("tp")),
        check_vma=False,
    )
```

```python
import jax
import jax.numpy as jnp
from jax import lax
from jax.experimental import pallas as pl
from jax.experimental.pallas import tpu as pltpu
from jax.sharding import Mesh, PartitionSpec as P

D = 8192
KV = 1024
PIECES = 32
MB = 8
F = 1024
C = 128
NP = 64
NT = 8
X, Z, CORES = 4, 8, 2
ROWS = NP * MB
TILE = 128
NTILES = ROWS // TILE
EXTRA = 16
GRAD_SCALE = (ROWS // 2 * NP) ** (-0.5)

epsilon = 1e-05
f32 = jnp.float32
bf16 = jnp.bfloat16
VMEM = pl.BlockSpec(memory_space=pltpu.VMEM)
HBM = pl.BlockSpec(memory_space=pltpu.HBM)
SMEM = pl.BlockSpec(memory_space=pltpu.SMEM)


def call(kernel, outs, in_specs, scratch=(), flops=0, size=4 << 20, name=None):
    return pl.pallas_call(
        kernel,
        out_shape=outs,
        in_specs=in_specs,
        out_specs=jax.tree.map(lambda _: VMEM, outs),
        scratch_shapes=scratch,
        compiler_params=pltpu.CompilerParams(vmem_limit_bytes=40 << 20),
        cost_estimate=pl.CostEstimate(flops=flops, bytes_accessed=size, transcendentals=0),
        name=name,
    )


def parts(v):
    high = v.astype(bf16).astype(f32)
    rest = v - high
    mid = rest.astype(bf16).astype(f32)
    return high, mid, rest - mid


def to_lanes(square):
    return jnp.sum(square.T, axis=0, keepdims=True)


def to_rows(lanes):
    return jnp.broadcast_to(lanes, (TILE, TILE)).T


def pack_kernel(routes, acts, goals, out, order, route_sem, row_sem, goal_sem):
    fetch = pltpu.make_async_copy(routes, order, route_sem)
    fetch.start()

    def clear(d, _):
        out[pl.ds(d * 4, 4)] = jnp.zeros((4, MB, F + C), bf16)
        return 0

    lax.fori_loop(0, NP // 4, clear, 0)
    fetch.wait()

    def send(m, _):
        d = order[m]
        pltpu.make_async_copy(acts.at[m], out.at[d, :, pl.ds(0, F)], row_sem).start()
        pltpu.make_async_copy(goals.at[m], out.at[d, :, pl.ds(F, C)], goal_sem).start()
        return 0

    lax.fori_loop(0, PIECES, send, 0)
    pltpu.make_async_copy(acts, out.at[pl.ds(0, PIECES), :, pl.ds(0, F)], row_sem).wait()
    pltpu.make_async_copy(goals, out.at[pl.ds(0, PIECES), :, pl.ds(F, C)], goal_sem).wait()


def value_kernel(rows, gain, weights, out, gained, squares):
    for i in range(NTILES):
        x = rows[i * 16 : (i + 1) * 16, :, :F].astype(f32).reshape(TILE, F)
        sq = x * x
        folded = sq[:, :128]
        for j in range(1, F // 128):
            folded = folded + sq[:, j * 128 : (j + 1) * 128]
        squares[i : i + 1, :] = to_lanes(folded)
        gained[i * TILE : (i + 1) * TILE, :] = (x * gain[...]).astype(bf16)
    for i in range(KV // 256):
        partial = jnp.dot(gained[...], weights[:, i * 256 : (i + 1) * 256], preferred_element_type=f32).astype(bf16)
        out[2 * i, :ROWS, :] = partial[:, :C]
        out[2 * i + 1, :ROWS, :] = partial[:, C:]
    high, mid, low = parts(squares[0:4, :])
    tail = jnp.concatenate([high, mid, low, jnp.zeros_like(high)], axis=0).astype(bf16)
    for t in range(NT):
        out[t, ROWS:, :] = tail


def loss_kernel(got, goals, value_out, send, scales, dots):
    tail = got[0, ROWS:, :].astype(f32)
    for t in range(1, NT):
        tail = tail + got[t, ROWS:, :].astype(f32)
    total = tail[0:4] + tail[4:8] + tail[8:12]
    scales[0:4, :] = lax.rsqrt(total / D + epsilon)
    scales[4:8, :] = jnp.zeros((4, 128), f32)

    for i in range(NTILES):
        here = slice(i * TILE, (i + 1) * TILE)
        total = got[0, here, :].astype(f32)
        for t in range(1, NT):
            total = total + got[t, here, :].astype(f32)
        value = total * to_rows(scales[i : i + 1, :])
        value_out[i * 16 : (i + 1) * 16] = value.reshape(16, MB, C).astype(bf16)
        goal = goals[i * 16 : (i + 1) * 16, :, F:].astype(f32).reshape(TILE, C)
        grad = (value - goal).astype(bf16)
        for t in range(NT):
            send[t, here, :] = grad
        dots[i : i + 1, :] = to_lanes(grad.astype(f32) * value)

    high, mid, low = parts(dots[0:4, :])
    tail = jnp.concatenate([high, mid, low, jnp.zeros_like(high)], axis=0).astype(bf16)
    for t in range(NT):
        send[t, ROWS:, :] = tail


def grad_kernel(got, rows, gain, weights, scales, value, back, grads, gains, scale_of, dot_of):
    tail = got[0, ROWS:, :].astype(f32)
    for t in range(1, NT):
        tail = tail + got[t, ROWS:, :].astype(f32)
    dots = (tail[0:4] + tail[4:8] + tail[8:12]) / D
    for i in range(NTILES):
        here = slice(i * TILE, (i + 1) * TILE)
        scale = scales[i : i + 1, :]
        scale_of[here, :] = to_rows(scale)
        dot_of[here, :] = to_rows(scale * scale * dots[i : i + 1, :])
    for t in range(NT):
        grads[:, t * C : (t + 1) * C] = got[t, :ROWS, :]
    back[:, :, F:] = value[...]

    for i in range(F // 256):
        at = slice(i * 256, (i + 1) * 256)
        grad_normed = lax.dot_general(
            grads[...], weights[at, :], (((1,), (1,)), ((), ())), preferred_element_type=f32
        )
        scaled = grad_normed * jnp.concatenate([scale_of[...]] * 2, axis=1)
        x = rows[:, :, at].astype(f32).reshape(ROWS, 256)
        row_grad = scaled * gain[:, at] - x * jnp.concatenate([dot_of[...]] * 2, axis=1)
        back[:, :, at] = row_grad.reshape(NP, MB, 256).astype(bf16)
        gains[:, at] = jnp.sum((scaled * x).reshape(ROWS // 8, 8, 256), axis=0)


def share_kernel(grads, scales, gained, gains, keep, send):
    first = lax.axis_index("core") == 0
    scale = jnp.concatenate([to_rows(scales[i : i + 1, :]) for i in range(NTILES)], axis=0)
    scale = jnp.concatenate([scale, scale], axis=1)
    for i in range(KV // 256):
        scaled = (grads[:, i * 256 : (i + 1) * 256].astype(f32) * scale).astype(bf16)
        mine = lax.dot_general(scaled, gained[...], (((0,), (0,)), ((), ())), preferred_element_type=f32)
        for j in range(8):
            at = slice(i * 128 + j * 16, i * 128 + (j + 1) * 16)
            even = mine[j * 32 : j * 32 + 16, :]
            odd = mine[j * 32 + 16 : j * 32 + 32, :]
            keep[at, :] = jnp.where(first, even, odd)
            send[at, :] = jnp.where(first, odd, even).astype(bf16)

    total = jnp.sum(gains[...], axis=0, keepdims=True)
    keep[KV // 2 :, :] = jnp.concatenate([total, jnp.zeros((EXTRA - 1, F), f32)], axis=0)
    high, mid, low = parts(total)
    tail = jnp.concatenate([high, mid, low, jnp.zeros((EXTRA - 3, F), f32)], axis=0)
    send[KV // 2 :, :] = tail.astype(bf16)


def gain_tail(total):
    high = total.astype(bf16).astype(f32)
    return jnp.concatenate([high, total - high], axis=0).astype(bf16)


def core_kernel(keep, got, own, *sends):
    me = lax.axis_index("x")
    tail = keep[KV // 2 :, :] + got[KV // 2 :, :].astype(f32)
    tail = jnp.sum(tail, axis=0, keepdims=True)
    tail = jnp.concatenate([tail[:, j * 128 : (j + 1) * 128] for j in range(F // 128)], axis=0)

    def put(out, d, tail):
        there = pl.ds(pl.multiple_of(lax.rem(me + d, X) * 128, 128), 128)
        total = keep[there, :] + got[there, :].astype(f32)
        for j in range(F // 128):
            out[j * 128 : (j + 1) * 128, :] = total[:, j * 128 : (j + 1) * 128].astype(out.dtype)
        out[F:, :] = tail

    for d, send in enumerate(sends):
        put(send, d + 1, gain_tail(tail))
    put(own, 0, jnp.concatenate([tail, jnp.zeros_like(tail)], axis=0))


def x_kernel(own, *refs):
    *got, out = refs
    for z in range(Z):
        for j in range(F // 128):
            at = slice(j * 128 + z * 16, j * 128 + z * 16 + 16)
            total = own[at, :]
            for g in got:
                total = total + g[at, :].astype(f32)
            out[z, j * 16 : (j + 1) * 16, :] = total.astype(bf16)
    tail = own[F:, :]
    for g in got:
        tail = tail + g[F:, :].astype(f32)
    tail = gain_tail(tail[:8] + tail[8:])
    for z in range(Z):
        out[z, 128:, :] = tail


def last_kernel(got, weight_out, gain_out):
    total = got[0].astype(f32)
    for z in range(1, Z):
        total = total + got[z].astype(f32)
    total = total * GRAD_SCALE
    tail = total[128:136] + total[136:]
    for j in range(F // 128):
        at = slice(j * 128, (j + 1) * 128)
        weight_out[:, at] = total[j * 16 : (j + 1) * 16]
        gain_out[:, at] = tail[j : j + 1]


def unpack_kernel(routes, got, rows, values):
    def take(m, _):
        d = routes[m]
        rows[m] = got[d, :, :F]
        values[m] = got[d, :, F:]
        return 0

    lax.fori_loop(0, PIECES, take, 0)


def shape(*dims, dtype=bf16):
    return jax.ShapeDtypeStruct(dims, dtype)


def exchange(v, axes):
    return lax.all_to_all(v, axes, split_axis=0, concat_axis=0, tiled=True)


def body(activations, targets, routes, value_weights, norm_gains):
    peer = ("x", "z", "core")
    weights = value_weights[0]
    order = routes[:, 0]
    given = order, activations.reshape(PIECES, MB, F), targets.reshape(PIECES, MB, C)
    sends = call(
        pack_kernel,
        shape(NP, MB, F + C),
        [HBM] * 3,
        [pltpu.SMEM((PIECES,), jnp.int32)] + [pltpu.SemaphoreType.DMA] * 3,
        name="pack",
    )(*[pltpu.with_memory_space_constraint(v, pltpu.HBM) for v in given])
    arrived = exchange(sends, peer)
    partials, gained = call(
        value_kernel,
        (shape(NT, ROWS + EXTRA, C), shape(ROWS, F)),
        [VMEM] * 3,
        [pltpu.VMEM((8, 128), f32)],
        flops=2 * ROWS * F * KV,
        name="partial_values",
    )(arrived, norm_gains, weights)
    value, grad_part, scales = call(
        loss_kernel,
        (shape(NP, MB, C), shape(NT, ROWS + EXTRA, C), shape(8, 128, dtype=f32)),
        [VMEM] * 2,
        [pltpu.VMEM((8, 128), f32)],
        name="loss",
    )(exchange(partials, "tp"), arrived)
    back, grads, gains = call(
        grad_kernel,
        (shape(NP, MB, F + C), shape(ROWS, KV), shape(8, F, dtype=f32)),
        [VMEM] * 6,
        [pltpu.VMEM((ROWS, 128), f32)] * 2,
        flops=2 * ROWS * F * KV,
        size=8 << 20,
        name="grads",
    )(exchange(grad_part, "tp"), arrived, norm_gains, weights, scales, value)
    rows_back = exchange(back, peer)

    half = (KV // CORES + EXTRA, F)
    keep, send = call(
        share_kernel,
        (shape(*half, dtype=f32), shape(*half)),
        [VMEM] * 4,
        flops=2 * ROWS * F * KV,
        name="share",
    )(grads, scales, gained, gains)
    got = lax.ppermute(send, "core", [(0, 1), (1, 0)])
    block = (F + EXTRA, 128)
    own, *sends = call(
        core_kernel, (shape(*block, dtype=f32),) + (shape(*block),) * (X - 1), [VMEM] * 2, name="sum_core"
    )(keep, got)
    got = [lax.ppermute(v, "x", [(i, (i + d + 1) % X) for i in range(X)]) for d, v in enumerate(sends)]
    grad_rows, values = call(
        unpack_kernel,
        (shape(PIECES, MB, F), shape(PIECES, MB, C)),
        [SMEM, VMEM],
        name="unpack",
    )(order, rows_back)
    got, grad_rows, values = lax.optimization_barrier((got, grad_rows, values))
    by_x = call(x_kernel, shape(Z, 128 + EXTRA, 128), [VMEM] * X, name="sum_x")(own, *got)
    by_z = exchange(by_x, "z")
    weight_grad, gain_grad = call(
        last_kernel, (shape(16, F, dtype=f32), shape(1, F, dtype=f32)), [VMEM], name="sum_z"
    )(by_z)
    return (
        grad_rows.reshape(PIECES * MB, F),
        values.reshape(PIECES * MB, C),
        weight_grad,
        gain_grad[0],
    )


def solution(mesh):
    split = Mesh(mesh.devices.reshape(X, Z, CORES, NT), ("x", "z", "core", "tp"))
    peer = ("x", "z", "core")
    return jax.shard_map(
        body,
        mesh=split,
        in_specs=(
            P(peer, "tp"),
            P(peer, "tp"),
            P(peer, None),
            P(peer, "tp", None),
            P(peer, "tp"),
        ),
        out_specs=(P(peer, "tp"), P(peer, "tp"), P(peer, "tp"), P("tp")),
        check_vma=False,
    )
```

```python
import jax
import jax.numpy as jnp
from jax import lax
from jax.experimental import pallas as pl
from jax.experimental.pallas import tpu as pltpu
from jax.sharding import Mesh, PartitionSpec as P

D = 8192
KV = 1024
PIECES = 32
MB = 8
F = 1024
C = 128
NP = 64
NT = 8
X, Z, CORES = 4, 8, 2
ROWS = NP * MB
TILE = 128
NTILES = ROWS // TILE
EXTRA = 16
GRAD_SCALE = (ROWS // 2 * NP) ** (-0.5)

epsilon = 1e-05
f32 = jnp.float32
bf16 = jnp.bfloat16
VMEM = pl.BlockSpec(memory_space=pltpu.VMEM)
HBM = pl.BlockSpec(memory_space=pltpu.HBM)
SMEM = pl.BlockSpec(memory_space=pltpu.SMEM)


def call(kernel, outs, in_specs, scratch=(), out_specs=None, flops=0, size=4 << 20, name=None):
    return pl.pallas_call(
        kernel,
        out_shape=outs,
        in_specs=in_specs,
        out_specs=jax.tree.map(lambda _: VMEM, outs) if out_specs is None else out_specs,
        scratch_shapes=scratch,
        compiler_params=pltpu.CompilerParams(vmem_limit_bytes=40 << 20),
        cost_estimate=pl.CostEstimate(flops=flops, bytes_accessed=size, transcendentals=0),
        name=name,
    )


def parts(v):
    high = v.astype(bf16).astype(f32)
    rest = v - high
    mid = rest.astype(bf16).astype(f32)
    return high, mid, rest - mid


def to_lanes(square):
    return jnp.sum(square.T, axis=0, keepdims=True)


def to_rows(lanes):
    return jnp.broadcast_to(lanes, (TILE, TILE)).T


def pack_kernel(routes, acts, goals, out, order, rows, columns, route_sem, row_sem, goal_sem):
    copies = [
        pltpu.make_async_copy(routes, order, route_sem),
        pltpu.make_async_copy(acts, rows, row_sem),
        pltpu.make_async_copy(goals, columns, goal_sem),
    ]
    for copy in copies:
        copy.start()

    def clear(d, _):
        out[pl.ds(d * 4, 4)] = jnp.zeros((4, MB, F + C), bf16)
        return 0

    lax.fori_loop(0, NP // 4, clear, 0)
    for copy in copies:
        copy.wait()

    def put(m, _):
        d = order[m]
        out[d, :, :F] = rows[m]
        out[d, :, F:] = columns[m]
        return 0

    lax.fori_loop(0, PIECES, put, 0, unroll=4)


def value_kernel(rows, gain, weights, out, gained, squares):
    for i in range(NTILES):
        x = rows[i * 16 : (i + 1) * 16, :, :F].astype(f32).reshape(TILE, F)
        sq = x * x
        folded = sq[:, :128]
        for j in range(1, F // 128):
            folded = folded + sq[:, j * 128 : (j + 1) * 128]
        squares[i : i + 1, :] = to_lanes(folded)
        gained[i * TILE : (i + 1) * TILE, :] = (x * gain[...]).astype(bf16)
    for i in range(KV // 256):
        partial = jnp.dot(gained[...], weights[:, i * 256 : (i + 1) * 256], preferred_element_type=f32).astype(bf16)
        out[2 * i, :ROWS, :] = partial[:, :C]
        out[2 * i + 1, :ROWS, :] = partial[:, C:]
    high, mid, low = parts(squares[0:4, :])
    tail = jnp.concatenate([high, mid, low, jnp.zeros_like(high)], axis=0).astype(bf16)
    for t in range(NT):
        out[t, ROWS:, :] = tail


def loss_kernel(got, goals, value_out, send, scales, dots):
    tail = got[0, ROWS:, :].astype(f32)
    for t in range(1, NT):
        tail = tail + got[t, ROWS:, :].astype(f32)
    total = tail[0:4] + tail[4:8] + tail[8:12]
    scales[0:4, :] = lax.rsqrt(total / D + epsilon)
    scales[4:8, :] = jnp.zeros((4, 128), f32)

    for i in range(NTILES):
        here = slice(i * TILE, (i + 1) * TILE)
        total = got[0, here, :].astype(f32)
        for t in range(1, NT):
            total = total + got[t, here, :].astype(f32)
        value = total * to_rows(scales[i : i + 1, :])
        value_out[i * 16 : (i + 1) * 16] = value.reshape(16, MB, C).astype(bf16)
        goal = goals[i * 16 : (i + 1) * 16, :, F:].astype(f32).reshape(TILE, C)
        grad = (value - goal).astype(bf16)
        for t in range(NT):
            send[t, here, :] = grad
        dots[i : i + 1, :] = to_lanes(grad.astype(f32) * value)

    high, mid, low = parts(dots[0:4, :])
    tail = jnp.concatenate([high, mid, low, jnp.zeros_like(high)], axis=0).astype(bf16)
    for t in range(NT):
        send[t, ROWS:, :] = tail


def grad_kernel(got, rows, gain, weights, scales, value, back, grads, gains, made, sems):
    tail = got[0, ROWS:, :].astype(f32)
    for t in range(1, NT):
        tail = tail + got[t, ROWS:, :].astype(f32)
    dots = (tail[0:4] + tail[4:8] + tail[8:12]) / D
    copies = []
    sums = [0.0] * (F // 256)
    for half in range(2):
        here = slice(half * ROWS // 2, (half + 1) * ROWS // 2)
        slots = slice(half * NP // 2, (half + 1) * NP // 2)
        for t in range(NT):
            grads[here, t * C : (t + 1) * C] = got[t, here, :]
        tiles = range(half * NTILES // 2, (half + 1) * NTILES // 2)
        scale = [scales[i : i + 1, :] for i in tiles]
        dot = [v * v * dots[i : i + 1, :] for i, v in zip(tiles, scale)]
        scale = jnp.concatenate([to_rows(v) for v in scale], axis=0)
        scale = jnp.concatenate([scale, scale], axis=1)
        dot = jnp.concatenate([to_rows(v) for v in dot], axis=0)
        dot = jnp.concatenate([dot, dot], axis=1)
        made[slots, :, F:] = value[slots]
        for i in range(F // 256):
            at = slice(i * 256, (i + 1) * 256)
            grad_normed = lax.dot_general(
                grads[here, :], weights[at, :], (((1,), (1,)), ((), ())), preferred_element_type=f32
            )
            scaled = grad_normed * scale
            x = rows[slots, :, at].astype(f32).reshape(ROWS // 2, 256)
            row_grad = scaled * gain[:, at] - x * dot
            made[slots, :, at] = row_grad.reshape(NP // 2, MB, 256).astype(bf16)
            sums[i] += jnp.sum((scaled * x).reshape(ROWS // 16, 8, 256), axis=0)
        where = pl.ds(half * NP // 2, NP // 2)
        copies.append(pltpu.make_async_copy(made.at[where], back.at[where], sems.at[half]))
        copies[-1].start()
    for i in range(F // 256):
        gains[:, i * 256 : (i + 1) * 256] = sums[i]
    for copy in copies:
        copy.wait()


def share_kernel(grads, scales, gained, gains, keep, send):
    first = lax.axis_index("core") == 0
    scale = jnp.concatenate([to_rows(scales[i : i + 1, :]) for i in range(NTILES)], axis=0)
    scale = jnp.concatenate([scale, scale], axis=1)
    for i in range(KV // 256):
        scaled = (grads[:, i * 256 : (i + 1) * 256].astype(f32) * scale).astype(bf16)
        mine = lax.dot_general(scaled, gained[...], (((0,), (0,)), ((), ())), preferred_element_type=f32)
        for j in range(8):
            at = slice(i * 128 + j * 16, i * 128 + (j + 1) * 16)
            even = mine[j * 32 : j * 32 + 16, :]
            odd = mine[j * 32 + 16 : j * 32 + 32, :]
            keep[at, :] = jnp.where(first, even, odd)
            send[at, :] = jnp.where(first, odd, even).astype(bf16)

    total = jnp.sum(gains[...], axis=0, keepdims=True)
    keep[KV // 2 :, :] = jnp.concatenate([total, jnp.zeros((EXTRA - 1, F), f32)], axis=0)
    high, mid, low = parts(total)
    tail = jnp.concatenate([high, mid, low, jnp.zeros((EXTRA - 3, F), f32)], axis=0)
    send[KV // 2 :, :] = tail.astype(bf16)


def gain_tail(total):
    high = total.astype(bf16).astype(f32)
    return jnp.concatenate([high, total - high], axis=0).astype(bf16)


def core_kernel(keep, got, own, *sends):
    me = lax.axis_index("x")
    tail = keep[KV // 2 :, :] + got[KV // 2 :, :].astype(f32)
    tail = jnp.sum(tail, axis=0, keepdims=True)
    tail = jnp.concatenate([tail[:, j * 128 : (j + 1) * 128] for j in range(F // 128)], axis=0)

    def put(out, d, tail):
        there = pl.ds(pl.multiple_of(lax.rem(me + d, X) * 128, 128), 128)
        total = keep[there, :] + got[there, :].astype(f32)
        for j in range(F // 128):
            out[j * 128 : (j + 1) * 128, :] = total[:, j * 128 : (j + 1) * 128].astype(out.dtype)
        out[F:, :] = tail

    for d, send in enumerate(sends):
        put(send, d + 1, gain_tail(tail))
    put(own, 0, jnp.concatenate([tail, jnp.zeros_like(tail)], axis=0))


def x_kernel(own, *refs):
    *got, out = refs
    for z in range(Z):
        for j in range(F // 128):
            at = slice(j * 128 + z * 16, j * 128 + z * 16 + 16)
            total = own[at, :]
            for g in got:
                total = total + g[at, :].astype(f32)
            out[z, j * 16 : (j + 1) * 16, :] = total.astype(bf16)
    tail = own[F:, :]
    for g in got:
        tail = tail + g[F:, :].astype(f32)
    tail = gain_tail(tail[:8] + tail[8:])
    for z in range(Z):
        out[z, 128:, :] = tail


def last_kernel(got, weight_out, gain_out):
    total = got[0].astype(f32)
    for z in range(1, Z):
        total = total + got[z].astype(f32)
    total = total * GRAD_SCALE
    tail = total[128:136] + total[136:]
    for j in range(F // 128):
        at = slice(j * 128, (j + 1) * 128)
        weight_out[:, at] = total[j * 16 : (j + 1) * 16]
        gain_out[:, at] = tail[j : j + 1]


def unpack_kernel(routes, got, rows, values):
    def take(m, _):
        d = routes[m]
        rows[m] = got[d, :, :F]
        values[m] = got[d, :, F:]
        return 0

    lax.fori_loop(0, PIECES, take, 0)


def shape(*dims, dtype=bf16):
    return jax.ShapeDtypeStruct(dims, dtype)


def exchange(v, axes):
    return lax.all_to_all(v, axes, split_axis=0, concat_axis=0, tiled=True)


def body(activations, targets, routes, value_weights, norm_gains):
    peer = ("x", "z", "core")
    weights = value_weights[0]
    order = routes[:, 0]
    given = order, activations.reshape(PIECES, MB, F), targets.reshape(PIECES, MB, C)
    sends = call(
        pack_kernel,
        shape(NP, MB, F + C),
        [HBM] * 3,
        [
            pltpu.SMEM((PIECES,), jnp.int32),
            pltpu.VMEM((PIECES, MB, F), bf16),
            pltpu.VMEM((PIECES, MB, C), bf16),
        ]
        + [pltpu.SemaphoreType.DMA] * 3,
        name="pack",
    )(*[pltpu.with_memory_space_constraint(v, pltpu.HBM) for v in given])
    arrived = exchange(sends, peer)
    partials, gained = call(
        value_kernel,
        (shape(NT, ROWS + EXTRA, C), shape(ROWS, F)),
        [VMEM] * 3,
        [pltpu.VMEM((8, 128), f32)],
        flops=2 * ROWS * F * KV,
        name="partial_values",
    )(arrived, norm_gains, weights)
    value, grad_part, scales = call(
        loss_kernel,
        (shape(NP, MB, C), shape(NT, ROWS + EXTRA, C), shape(8, 128, dtype=f32)),
        [VMEM] * 2,
        [pltpu.VMEM((8, 128), f32)],
        name="loss",
    )(exchange(partials, "tp"), arrived)
    back, grads, gains = call(
        grad_kernel,
        (shape(NP, MB, F + C), shape(ROWS, KV), shape(8, F, dtype=f32)),
        [VMEM] * 6,
        [pltpu.VMEM((NP, MB, F + C), bf16), pltpu.SemaphoreType.DMA((2,))],
        out_specs=(HBM, VMEM, VMEM),
        flops=2 * ROWS * F * KV,
        size=8 << 20,
        name="grads",
    )(exchange(grad_part, "tp"), arrived, norm_gains, weights, scales, value)
    rows_back = exchange(back, peer)

    half = (KV // CORES + EXTRA, F)
    keep, send = call(
        share_kernel,
        (shape(*half, dtype=f32), shape(*half)),
        [VMEM] * 4,
        flops=2 * ROWS * F * KV,
        name="share",
    )(grads, scales, gained, gains)
    got = lax.ppermute(send, "core", [(0, 1), (1, 0)])
    block = (F + EXTRA, 128)
    own, *sends = call(
        core_kernel, (shape(*block, dtype=f32),) + (shape(*block),) * (X - 1), [VMEM] * 2, name="sum_core"
    )(keep, got)
    got = [lax.ppermute(v, "x", [(i, (i + d + 1) % X) for i in range(X)]) for d, v in enumerate(sends)]
    grad_rows, values = call(
        unpack_kernel,
        (shape(PIECES, MB, F), shape(PIECES, MB, C)),
        [SMEM, VMEM],
        name="unpack",
    )(order, rows_back)
    got, grad_rows, values = lax.optimization_barrier((got, grad_rows, values))
    by_x = call(x_kernel, shape(Z, 128 + EXTRA, 128), [VMEM] * X, name="sum_x")(own, *got)
    by_z = exchange(by_x, "z")
    weight_grad, gain_grad = call(
        last_kernel, (shape(16, F, dtype=f32), shape(1, F, dtype=f32)), [VMEM], name="sum_z"
    )(by_z)
    return (
        grad_rows.reshape(PIECES * MB, F),
        values.reshape(PIECES * MB, C),
        weight_grad,
        gain_grad[0],
    )


def solution(mesh):
    split = Mesh(mesh.devices.reshape(X, Z, CORES, NT), ("x", "z", "core", "tp"))
    peer = ("x", "z", "core")
    return jax.shard_map(
        body,
        mesh=split,
        in_specs=(
            P(peer, "tp"),
            P(peer, "tp"),
            P(peer, None),
            P(peer, "tp", None),
            P(peer, "tp"),
        ),
        out_specs=(P(peer, "tp"), P(peer, "tp"), P(peer, "tp"), P("tp")),
        check_vma=False,
    )
```

```python
import jax
import jax.numpy as jnp
from jax import lax
from jax.experimental import pallas as pl
from jax.experimental.pallas import tpu as pltpu
from jax.sharding import Mesh, PartitionSpec as P

D = 8192
KV = 1024
PIECES = 32
MB = 8
F = 1024
C = 128
NP = 64
NT = 8
X, Z, CORES = 4, 8, 2
X_STEPS = (2, 1, 3)
ROWS = NP * MB
TILE = 128
NTILES = ROWS // TILE
EXTRA = 16
GRAD_SCALE = (ROWS // 2 * NP) ** (-0.5)

epsilon = 1e-05
f32 = jnp.float32
bf16 = jnp.bfloat16
VMEM = pl.BlockSpec(memory_space=pltpu.VMEM)
HBM = pl.BlockSpec(memory_space=pltpu.HBM)
SMEM = pl.BlockSpec(memory_space=pltpu.SMEM)


def call(kernel, outs, in_specs, scratch=(), out_specs=None, flops=0, size=4 << 20, name=None):
    return pl.pallas_call(
        kernel,
        out_shape=outs,
        in_specs=in_specs,
        out_specs=jax.tree.map(lambda _: VMEM, outs) if out_specs is None else out_specs,
        scratch_shapes=scratch,
        compiler_params=pltpu.CompilerParams(vmem_limit_bytes=40 << 20),
        cost_estimate=pl.CostEstimate(flops=flops, bytes_accessed=size, transcendentals=0),
        name=name,
    )


def parts(v):
    high = v.astype(bf16).astype(f32)
    rest = v - high
    mid = rest.astype(bf16).astype(f32)
    return high, mid, rest - mid


def to_lanes(square):
    return jnp.sum(square.T, axis=0, keepdims=True)


def to_rows(lanes):
    return jnp.broadcast_to(lanes, (TILE, TILE)).T


def pack_kernel(routes, acts, goals, out, order, rows, columns, route_sem, row_sem, goal_sem):
    copies = [
        pltpu.make_async_copy(routes, order, route_sem),
        pltpu.make_async_copy(acts, rows, row_sem),
        pltpu.make_async_copy(goals, columns, goal_sem),
    ]
    for copy in copies:
        copy.start()

    def clear(d, _):
        out[pl.ds(d * 4, 4)] = jnp.zeros((4, MB, F + C), bf16)
        return 0

    lax.fori_loop(0, NP // 4, clear, 0)
    for copy in copies:
        copy.wait()

    def put(m, _):
        d = order[m]
        out[d, :, :F] = rows[m]
        out[d, :, F:] = columns[m]
        return 0

    lax.fori_loop(0, PIECES, put, 0, unroll=4)


def value_kernel(rows, gain, weights, out, gained, squares):
    for i in range(NTILES):
        x = rows[i * 16 : (i + 1) * 16, :, :F].astype(f32).reshape(TILE, F)
        sq = x * x
        folded = sq[:, :128]
        for j in range(1, F // 128):
            folded = folded + sq[:, j * 128 : (j + 1) * 128]
        squares[i : i + 1, :] = to_lanes(folded)
        gained[i * TILE : (i + 1) * TILE, :] = (x * gain[...]).astype(bf16)
    for i in range(KV // 256):
        partial = jnp.dot(gained[...], weights[:, i * 256 : (i + 1) * 256], preferred_element_type=f32).astype(bf16)
        out[2 * i, :ROWS, :] = partial[:, :C]
        out[2 * i + 1, :ROWS, :] = partial[:, C:]
    high, mid, low = parts(squares[0:4, :])
    tail = jnp.concatenate([high, mid, low, jnp.zeros_like(high)], axis=0).astype(bf16)
    for t in range(NT):
        out[t, ROWS:, :] = tail


def loss_kernel(got, goals, value_out, send, scales, dots):
    tail = got[0, ROWS:, :].astype(f32)
    for t in range(1, NT):
        tail = tail + got[t, ROWS:, :].astype(f32)
    total = tail[0:4] + tail[4:8] + tail[8:12]
    scales[0:4, :] = lax.rsqrt(total / D + epsilon)
    scales[4:8, :] = jnp.zeros((4, 128), f32)

    for i in range(NTILES):
        here = slice(i * TILE, (i + 1) * TILE)
        total = got[0, here, :].astype(f32)
        for t in range(1, NT):
            total = total + got[t, here, :].astype(f32)
        value = total * to_rows(scales[i : i + 1, :])
        value_out[i * 16 : (i + 1) * 16] = value.reshape(16, MB, C).astype(bf16)
        goal = goals[i * 16 : (i + 1) * 16, :, F:].astype(f32).reshape(TILE, C)
        grad = (value - goal).astype(bf16)
        for t in range(NT):
            send[t, here, :] = grad
        dots[i : i + 1, :] = to_lanes(grad.astype(f32) * value)

    high, mid, low = parts(dots[0:4, :])
    tail = jnp.concatenate([high, mid, low, jnp.zeros_like(high)], axis=0).astype(bf16)
    for t in range(NT):
        send[t, ROWS:, :] = tail


def grad_kernel(got, rows, gain, weights, scales, value, back, grads, gains, made, sems):
    tail = got[0, ROWS:, :].astype(f32)
    for t in range(1, NT):
        tail = tail + got[t, ROWS:, :].astype(f32)
    dots = (tail[0:4] + tail[4:8] + tail[8:12]) / D
    copies = []
    sums = [0.0] * (F // 256)
    for half in range(2):
        here = slice(half * ROWS // 2, (half + 1) * ROWS // 2)
        slots = slice(half * NP // 2, (half + 1) * NP // 2)
        for t in range(NT):
            grads[here, t * C : (t + 1) * C] = got[t, here, :]
        tiles = range(half * NTILES // 2, (half + 1) * NTILES // 2)
        scale = [scales[i : i + 1, :] for i in tiles]
        dot = [v * v * dots[i : i + 1, :] for i, v in zip(tiles, scale)]
        scale = jnp.concatenate([to_rows(v) for v in scale], axis=0)
        scale = jnp.concatenate([scale, scale], axis=1)
        dot = jnp.concatenate([to_rows(v) for v in dot], axis=0)
        dot = jnp.concatenate([dot, dot], axis=1)
        made[slots, :, F:] = value[slots]
        for i in range(F // 256):
            at = slice(i * 256, (i + 1) * 256)
            grad_normed = lax.dot_general(
                grads[here, :], weights[at, :], (((1,), (1,)), ((), ())), preferred_element_type=f32
            )
            scaled = grad_normed * scale
            x = rows[slots, :, at].astype(f32).reshape(ROWS // 2, 256)
            row_grad = scaled * gain[:, at] - x * dot
            made[slots, :, at] = row_grad.reshape(NP // 2, MB, 256).astype(bf16)
            sums[i] += jnp.sum((scaled * x).reshape(ROWS // 16, 8, 256), axis=0)
        where = pl.ds(half * NP // 2, NP // 2)
        copies.append(pltpu.make_async_copy(made.at[where], back.at[where], sems.at[half]))
        copies[-1].start()
    for i in range(F // 256):
        gains[:, i * 256 : (i + 1) * 256] = sums[i]
    for copy in copies:
        copy.wait()


def share_kernel(grads, scales, gained, gains, keep, send):
    first = lax.axis_index("core") == 0
    scale = jnp.concatenate([to_rows(scales[i : i + 1, :]) for i in range(NTILES)], axis=0)
    scale = jnp.concatenate([scale, scale], axis=1)
    for i in range(KV // 256):
        scaled = (grads[:, i * 256 : (i + 1) * 256].astype(f32) * scale).astype(bf16)
        mine = lax.dot_general(scaled, gained[...], (((0,), (0,)), ((), ())), preferred_element_type=f32)
        for j in range(8):
            at = slice(i * 128 + j * 16, i * 128 + (j + 1) * 16)
            even = mine[j * 32 : j * 32 + 16, :]
            odd = mine[j * 32 + 16 : j * 32 + 32, :]
            keep[at, :] = jnp.where(first, even, odd)
            send[at, :] = jnp.where(first, odd, even).astype(bf16)

    total = jnp.sum(gains[...], axis=0, keepdims=True)
    keep[KV // 2 :, :] = jnp.concatenate([total, jnp.zeros((EXTRA - 1, F), f32)], axis=0)
    high, mid, low = parts(total)
    tail = jnp.concatenate([high, mid, low, jnp.zeros((EXTRA - 3, F), f32)], axis=0)
    send[KV // 2 :, :] = tail.astype(bf16)


def gain_tail(total):
    high = total.astype(bf16).astype(f32)
    return jnp.concatenate([high, total - high], axis=0).astype(bf16)


def core_kernel(keep, got, own, *sends):
    me = lax.axis_index("x")
    tail = keep[KV // 2 :, :] + got[KV // 2 :, :].astype(f32)
    tail = jnp.sum(tail, axis=0, keepdims=True)
    tail = jnp.concatenate([tail[:, j * 128 : (j + 1) * 128] for j in range(F // 128)], axis=0)

    def put(out, d, tail):
        there = pl.ds(pl.multiple_of(lax.rem(me + d, X) * 128, 128), 128)
        total = keep[there, :] + got[there, :].astype(f32)
        for j in range(F // 128):
            out[j * 128 : (j + 1) * 128, :] = total[:, j * 128 : (j + 1) * 128].astype(out.dtype)
        out[F:, :] = tail

    for d, send in zip(X_STEPS, sends):
        put(send, d, gain_tail(tail))
    put(own, 0, jnp.concatenate([tail, jnp.zeros_like(tail)], axis=0))


def x_kernel(own, *refs):
    *got, out = refs
    for z in range(Z):
        for j in range(F // 128):
            at = slice(j * 128 + z * 16, j * 128 + z * 16 + 16)
            total = own[at, :]
            for g in got:
                total = total + g[at, :].astype(f32)
            out[z, j * 16 : (j + 1) * 16, :] = total.astype(bf16)
    tail = own[F:, :]
    for g in got:
        tail = tail + g[F:, :].astype(f32)
    tail = gain_tail(tail[:8] + tail[8:])
    for z in range(Z):
        out[z, 128:, :] = tail


def last_kernel(got, weight_out, gain_out):
    total = got[0].astype(f32)
    for z in range(1, Z):
        total = total + got[z].astype(f32)
    total = total * GRAD_SCALE
    tail = total[128:136] + total[136:]
    for j in range(F // 128):
        at = slice(j * 128, (j + 1) * 128)
        weight_out[:, at] = total[j * 16 : (j + 1) * 16]
        gain_out[:, at] = tail[j : j + 1]


def unpack_kernel(routes, got, rows, values):
    def take(m, _):
        d = routes[m]
        rows[m] = got[d, :, :F]
        values[m] = got[d, :, F:]
        return 0

    lax.fori_loop(0, PIECES, take, 0)


def shape(*dims, dtype=bf16):
    return jax.ShapeDtypeStruct(dims, dtype)


def exchange(v, axes):
    return lax.all_to_all(v, axes, split_axis=0, concat_axis=0, tiled=True)


def body(activations, targets, routes, value_weights, norm_gains):
    peer = ("x", "z", "core")
    weights = value_weights[0]
    order = routes[:, 0]
    given = order, activations.reshape(PIECES, MB, F), targets.reshape(PIECES, MB, C)
    sends = call(
        pack_kernel,
        shape(NP, MB, F + C),
        [HBM] * 3,
        [
            pltpu.SMEM((PIECES,), jnp.int32),
            pltpu.VMEM((PIECES, MB, F), bf16),
            pltpu.VMEM((PIECES, MB, C), bf16),
        ]
        + [pltpu.SemaphoreType.DMA] * 3,
        name="pack",
    )(*[pltpu.with_memory_space_constraint(v, pltpu.HBM) for v in given])
    arrived = exchange(sends, peer)
    partials, gained = call(
        value_kernel,
        (shape(NT, ROWS + EXTRA, C), shape(ROWS, F)),
        [VMEM] * 3,
        [pltpu.VMEM((8, 128), f32)],
        flops=2 * ROWS * F * KV,
        name="partial_values",
    )(arrived, norm_gains, weights)
    value, grad_part, scales = call(
        loss_kernel,
        (shape(NP, MB, C), shape(NT, ROWS + EXTRA, C), shape(8, 128, dtype=f32)),
        [VMEM] * 2,
        [pltpu.VMEM((8, 128), f32)],
        name="loss",
    )(exchange(partials, "tp"), arrived)
    back, grads, gains = call(
        grad_kernel,
        (shape(NP, MB, F + C), shape(ROWS, KV), shape(8, F, dtype=f32)),
        [VMEM] * 6,
        [pltpu.VMEM((NP, MB, F + C), bf16), pltpu.SemaphoreType.DMA((2,))],
        out_specs=(HBM, VMEM, VMEM),
        flops=2 * ROWS * F * KV,
        size=8 << 20,
        name="grads",
    )(exchange(grad_part, "tp"), arrived, norm_gains, weights, scales, value)
    rows_back = exchange(back, peer)

    half = (KV // CORES + EXTRA, F)
    keep, send = call(
        share_kernel,
        (shape(*half, dtype=f32), shape(*half)),
        [VMEM] * 4,
        flops=2 * ROWS * F * KV,
        name="share",
    )(grads, scales, gained, gains)
    got = lax.ppermute(send, "core", [(0, 1), (1, 0)])
    block = (F + EXTRA, 128)
    own, *sends = call(
        core_kernel, (shape(*block, dtype=f32),) + (shape(*block),) * (X - 1), [VMEM] * 2, name="sum_core"
    )(keep, got)
    got = [lax.ppermute(v, "x", [(i, (i + d) % X) for i in range(X)]) for d, v in zip(X_STEPS, sends)]
    grad_rows, values = call(
        unpack_kernel,
        (shape(PIECES, MB, F), shape(PIECES, MB, C)),
        [SMEM, VMEM],
        name="unpack",
    )(order, rows_back)
    got, grad_rows, values = lax.optimization_barrier((got, grad_rows, values))
    by_x = call(x_kernel, shape(Z, 128 + EXTRA, 128), [VMEM] * X, name="sum_x")(own, *got)
    by_z = exchange(by_x, "z")
    weight_grad, gain_grad = call(
        last_kernel, (shape(16, F, dtype=f32), shape(1, F, dtype=f32)), [VMEM], name="sum_z"
    )(by_z)
    return (
        grad_rows.reshape(PIECES * MB, F),
        values.reshape(PIECES * MB, C),
        weight_grad,
        gain_grad[0],
    )


def solution(mesh):
    split = Mesh(mesh.devices.reshape(X, Z, CORES, NT), ("x", "z", "core", "tp"))
    peer = ("x", "z", "core")
    return jax.shard_map(
        body,
        mesh=split,
        in_specs=(
            P(peer, "tp"),
            P(peer, "tp"),
            P(peer, None),
            P(peer, "tp", None),
            P(peer, "tp"),
        ),
        out_specs=(P(peer, "tp"), P(peer, "tp"), P(peer, "tp"), P("tp")),
        check_vma=False,
    )
```

```python
import jax
import jax.numpy as jnp
from jax import lax
from jax.experimental import pallas as pl
from jax.experimental.pallas import tpu as pltpu
from jax.sharding import Mesh, PartitionSpec as P

D = 8192
KV = 1024
PIECES = 32
MB = 8
F = 1024
C = 128
NP = 64
NT = 8
X, Z, CORES = 4, 8, 2
X_STEPS = (2, 1, 3)
ROWS = NP * MB
TILE = 128
NTILES = ROWS // TILE
EXTRA = 16
GRAD_SCALE = (ROWS // 2 * NP) ** (-0.5)

epsilon = 1e-05
f32 = jnp.float32
bf16 = jnp.bfloat16
VMEM = pl.BlockSpec(memory_space=pltpu.VMEM)
HBM = pl.BlockSpec(memory_space=pltpu.HBM)
SMEM = pl.BlockSpec(memory_space=pltpu.SMEM)


def call(kernel, outs, in_specs, scratch=(), out_specs=None, flops=0, size=4 << 20, name=None):
    return pl.pallas_call(
        kernel,
        out_shape=outs,
        in_specs=in_specs,
        out_specs=jax.tree.map(lambda _: VMEM, outs) if out_specs is None else out_specs,
        scratch_shapes=scratch,
        compiler_params=pltpu.CompilerParams(vmem_limit_bytes=40 << 20),
        cost_estimate=pl.CostEstimate(flops=flops, bytes_accessed=size, transcendentals=0),
        name=name,
    )


def parts(v):
    high = v.astype(bf16).astype(f32)
    rest = v - high
    mid = rest.astype(bf16).astype(f32)
    return high, mid, rest - mid


def to_lanes(square):
    return jnp.sum(square.T, axis=0, keepdims=True)


def to_rows(lanes):
    return jnp.broadcast_to(lanes, (TILE, TILE)).T


def pack_kernel(routes, acts, goals, out, order, rows, columns, route_sem, row_sem, goal_sem):
    copies = [
        pltpu.make_async_copy(routes, order, route_sem),
        pltpu.make_async_copy(acts, rows, row_sem),
        pltpu.make_async_copy(goals, columns, goal_sem),
    ]
    for copy in copies:
        copy.start()

    def clear(d, _):
        out[pl.ds(d * 4, 4)] = jnp.zeros((4, MB, F + C), bf16)
        return 0

    lax.fori_loop(0, NP // 4, clear, 0)
    for copy in copies:
        copy.wait()

    def put(m, _):
        d = order[m]
        out[d, :, :F] = rows[m]
        out[d, :, F:] = columns[m]
        return 0

    lax.fori_loop(0, PIECES, put, 0, unroll=4)


def value_kernel(rows, gain, weights, out, gained, squares):
    for i in range(NTILES):
        x = rows[i * 16 : (i + 1) * 16, :, :F].astype(f32).reshape(TILE, F)
        sq = x * x
        folded = sq[:, :128]
        for j in range(1, F // 128):
            folded = folded + sq[:, j * 128 : (j + 1) * 128]
        squares[i : i + 1, :] = to_lanes(folded)
        gained[i * TILE : (i + 1) * TILE, :] = (x * gain[...]).astype(bf16)
    for i in range(KV // 256):
        partial = jnp.dot(gained[...], weights[:, i * 256 : (i + 1) * 256], preferred_element_type=f32).astype(bf16)
        out[2 * i, :ROWS, :] = partial[:, :C]
        out[2 * i + 1, :ROWS, :] = partial[:, C:]
    high, mid, low = parts(squares[0:4, :])
    tail = jnp.concatenate([high, mid, low, jnp.zeros_like(high)], axis=0).astype(bf16)
    for t in range(NT):
        out[t, ROWS:, :] = tail


def loss_kernel(got, goals, value_out, send, scales, dots):
    tail = got[0, ROWS:, :].astype(f32)
    for t in range(1, NT):
        tail = tail + got[t, ROWS:, :].astype(f32)
    total = tail[0:4] + tail[4:8] + tail[8:12]
    scales[0:4, :] = lax.rsqrt(total / D + epsilon)
    scales[4:8, :] = jnp.zeros((4, 128), f32)

    for i in range(NTILES):
        here = slice(i * TILE, (i + 1) * TILE)
        total = got[0, here, :].astype(f32)
        for t in range(1, NT):
            total = total + got[t, here, :].astype(f32)
        value = total * to_rows(scales[i : i + 1, :])
        value_out[i * 16 : (i + 1) * 16] = value.reshape(16, MB, C).astype(bf16)
        goal = goals[i * 16 : (i + 1) * 16, :, F:].astype(f32).reshape(TILE, C)
        grad = (value - goal).astype(bf16)
        for t in range(NT):
            send[t, here, :] = grad
        dots[i : i + 1, :] = to_lanes(grad.astype(f32) * value)

    high, mid, low = parts(dots[0:4, :])
    tail = jnp.concatenate([high, mid, low, jnp.zeros_like(high)], axis=0).astype(bf16)
    for t in range(NT):
        send[t, ROWS:, :] = tail


def grad_kernel(got, rows, gain, weights, scales, value, back, grads, gains, made, sems):
    tail = got[0, ROWS:, :].astype(f32)
    for t in range(1, NT):
        tail = tail + got[t, ROWS:, :].astype(f32)
    dots = (tail[0:4] + tail[4:8] + tail[8:12]) / D
    copies = []
    sums = [0.0] * (F // 256)
    for half in range(2):
        here = slice(half * ROWS // 2, (half + 1) * ROWS // 2)
        slots = slice(half * NP // 2, (half + 1) * NP // 2)
        for t in range(NT):
            grads[here, t * C : (t + 1) * C] = got[t, here, :]
        tiles = range(half * NTILES // 2, (half + 1) * NTILES // 2)
        scale = [scales[i : i + 1, :] for i in tiles]
        dot = [v * v * dots[i : i + 1, :] for i, v in zip(tiles, scale)]
        scale = jnp.concatenate([to_rows(v) for v in scale], axis=0)
        scale = jnp.concatenate([scale, scale], axis=1)
        dot = jnp.concatenate([to_rows(v) for v in dot], axis=0)
        dot = jnp.concatenate([dot, dot], axis=1)
        made[slots, :, F:] = value[slots]
        for i in range(F // 256):
            at = slice(i * 256, (i + 1) * 256)
            grad_normed = lax.dot_general(
                grads[here, :], weights[at, :], (((1,), (1,)), ((), ())), preferred_element_type=f32
            )
            scaled = grad_normed * scale
            x = rows[slots, :, at].astype(f32).reshape(ROWS // 2, 256)
            row_grad = scaled * gain[:, at] - x * dot
            made[slots, :, at] = row_grad.reshape(NP // 2, MB, 256).astype(bf16)
            sums[i] += jnp.sum((scaled * x).reshape(ROWS // 16, 8, 256), axis=0)
        where = pl.ds(half * NP // 2, NP // 2)
        copies.append(pltpu.make_async_copy(made.at[where], back.at[where], sems.at[half]))
        copies[-1].start()
    for i in range(F // 256):
        gains[:, i * 256 : (i + 1) * 256] = sums[i]
    for copy in copies:
        copy.wait()


def share_kernel(grads, scales, gained, gains, keep, send):
    first = lax.axis_index("core") == 0
    scale = jnp.concatenate([to_rows(scales[i : i + 1, :]) for i in range(NTILES)], axis=0)
    scale = jnp.concatenate([scale, scale], axis=1)
    for i in range(KV // 256):
        scaled = (grads[:, i * 256 : (i + 1) * 256].astype(f32) * scale).astype(bf16)
        mine = lax.dot_general(scaled, gained[...], (((0,), (0,)), ((), ())), preferred_element_type=f32)
        for j in range(8):
            at = slice(i * 128 + j * 16, i * 128 + (j + 1) * 16)
            even = mine[j * 32 : j * 32 + 16, :]
            odd = mine[j * 32 + 16 : j * 32 + 32, :]
            keep[at, :] = jnp.where(first, even, odd)
            send[at, :] = jnp.where(first, odd, even).astype(bf16)

    total = jnp.sum(gains[...], axis=0, keepdims=True)
    keep[KV // 2 :, :] = jnp.concatenate([total, jnp.zeros((EXTRA - 1, F), f32)], axis=0)
    high, mid, low = parts(total)
    tail = jnp.concatenate([high, mid, low, jnp.zeros((EXTRA - 3, F), f32)], axis=0)
    send[KV // 2 :, :] = tail.astype(bf16)


def gain_tail(total):
    high = total.astype(bf16).astype(f32)
    return jnp.concatenate([high, total - high], axis=0).astype(bf16)


def core_kernel(keep, got, own, *sends):
    me = lax.axis_index("x")
    tail = keep[KV // 2 :, :] + got[KV // 2 :, :].astype(f32)
    tail = jnp.sum(tail, axis=0, keepdims=True)
    tail = jnp.concatenate([tail[:, j * 128 : (j + 1) * 128] for j in range(F // 128)], axis=0)

    def put(out, d, tail):
        there = pl.ds(pl.multiple_of((me ^ d) * 128, 128), 128)
        total = keep[there, :] + got[there, :].astype(f32)
        for j in range(F // 128):
            out[j * 128 : (j + 1) * 128, :] = total[:, j * 128 : (j + 1) * 128].astype(out.dtype)
        out[F:, :] = tail

    for d, send in zip(X_STEPS, sends):
        put(send, d, gain_tail(tail))
    put(own, 0, jnp.concatenate([tail, jnp.zeros_like(tail)], axis=0))


def x_kernel(own, *refs):
    *got, out = refs
    for z in range(Z):
        for j in range(F // 128):
            at = slice(j * 128 + z * 16, j * 128 + z * 16 + 16)
            total = own[at, :]
            for g in got:
                total = total + g[at, :].astype(f32)
            out[z, j * 16 : (j + 1) * 16, :] = total.astype(bf16)
    tail = own[F:, :]
    for g in got:
        tail = tail + g[F:, :].astype(f32)
    tail = gain_tail(tail[:8] + tail[8:])
    for z in range(Z):
        out[z, 128:, :] = tail


def last_kernel(got, weight_out, gain_out):
    total = got[0].astype(f32)
    for z in range(1, Z):
        total = total + got[z].astype(f32)
    total = total * GRAD_SCALE
    tail = total[128:136] + total[136:]
    for j in range(F // 128):
        at = slice(j * 128, (j + 1) * 128)
        weight_out[:, at] = total[j * 16 : (j + 1) * 16]
        gain_out[:, at] = tail[j : j + 1]


def unpack_kernel(routes, got, rows, values):
    def take(m, _):
        d = routes[m]
        rows[m] = got[d, :, :F]
        values[m] = got[d, :, F:]
        return 0

    lax.fori_loop(0, PIECES, take, 0)


def shape(*dims, dtype=bf16):
    return jax.ShapeDtypeStruct(dims, dtype)


def exchange(v, axes):
    return lax.all_to_all(v, axes, split_axis=0, concat_axis=0, tiled=True)


def body(activations, targets, routes, value_weights, norm_gains):
    peer = ("x", "z", "core")
    weights = value_weights[0]
    order = routes[:, 0]
    given = order, activations.reshape(PIECES, MB, F), targets.reshape(PIECES, MB, C)
    sends = call(
        pack_kernel,
        shape(NP, MB, F + C),
        [HBM] * 3,
        [
            pltpu.SMEM((PIECES,), jnp.int32),
            pltpu.VMEM((PIECES, MB, F), bf16),
            pltpu.VMEM((PIECES, MB, C), bf16),
        ]
        + [pltpu.SemaphoreType.DMA] * 3,
        name="pack",
    )(*[pltpu.with_memory_space_constraint(v, pltpu.HBM) for v in given])
    arrived = exchange(sends, peer)
    partials, gained = call(
        value_kernel,
        (shape(NT, ROWS + EXTRA, C), shape(ROWS, F)),
        [VMEM] * 3,
        [pltpu.VMEM((8, 128), f32)],
        flops=2 * ROWS * F * KV,
        name="partial_values",
    )(arrived, norm_gains, weights)
    value, grad_part, scales = call(
        loss_kernel,
        (shape(NP, MB, C), shape(NT, ROWS + EXTRA, C), shape(8, 128, dtype=f32)),
        [VMEM] * 2,
        [pltpu.VMEM((8, 128), f32)],
        name="loss",
    )(exchange(partials, "tp"), arrived)
    back, grads, gains = call(
        grad_kernel,
        (shape(NP, MB, F + C), shape(ROWS, KV), shape(8, F, dtype=f32)),
        [VMEM] * 6,
        [pltpu.VMEM((NP, MB, F + C), bf16), pltpu.SemaphoreType.DMA((2,))],
        out_specs=(HBM, VMEM, VMEM),
        flops=2 * ROWS * F * KV,
        size=8 << 20,
        name="grads",
    )(exchange(grad_part, "tp"), arrived, norm_gains, weights, scales, value)
    rows_back = exchange(back, peer)

    half = (KV // CORES + EXTRA, F)
    keep, send = call(
        share_kernel,
        (shape(*half, dtype=f32), shape(*half)),
        [VMEM] * 4,
        flops=2 * ROWS * F * KV,
        name="share",
    )(grads, scales, gained, gains)
    got = lax.ppermute(send, "core", [(0, 1), (1, 0)])
    block = (F + EXTRA, 128)
    own, *sends = call(
        core_kernel, (shape(*block, dtype=f32),) + (shape(*block),) * (X - 1), [VMEM] * 2, name="sum_core"
    )(keep, got)
    got = [lax.ppermute(v, "x", [(i, i ^ d) for i in range(X)]) for d, v in zip(X_STEPS, sends)]
    grad_rows, values = call(
        unpack_kernel,
        (shape(PIECES, MB, F), shape(PIECES, MB, C)),
        [SMEM, VMEM],
        name="unpack",
    )(order, rows_back)
    got, grad_rows, values = lax.optimization_barrier((got, grad_rows, values))
    by_x = call(x_kernel, shape(Z, 128 + EXTRA, 128), [VMEM] * X, name="sum_x")(own, *got)
    by_z = exchange(by_x, "z")
    weight_grad, gain_grad = call(
        last_kernel, (shape(16, F, dtype=f32), shape(1, F, dtype=f32)), [VMEM], name="sum_z"
    )(by_z)
    return (
        grad_rows.reshape(PIECES * MB, F),
        values.reshape(PIECES * MB, C),
        weight_grad,
        gain_grad[0],
    )


def solution(mesh):
    split = Mesh(mesh.devices.reshape(X, Z, CORES, NT), ("x", "z", "core", "tp"))
    peer = ("x", "z", "core")
    return jax.shard_map(
        body,
        mesh=split,
        in_specs=(
            P(peer, "tp"),
            P(peer, "tp"),
            P(peer, None),
            P(peer, "tp", None),
            P(peer, "tp"),
        ),
        out_specs=(P(peer, "tp"), P(peer, "tp"), P(peer, "tp"), P("tp")),
        check_vma=False,
    )
```

```python
import jax
import jax.numpy as jnp
from jax import lax
from jax.experimental import pallas as pl
from jax.experimental.pallas import tpu as pltpu
from jax.sharding import Mesh, PartitionSpec as P

D = 8192
KV = 1024
PIECES = 32
MB = 8
F = 1024
C = 128
NP = 64
NT = 8
X, Z, CORES = 4, 8, 2
X_STEPS = (2, 1, 3)
ROWS = NP * MB
TILE = 128
NTILES = ROWS // TILE
EXTRA = 16
GRAD_SCALE = (ROWS // 2 * NP) ** (-0.5)

epsilon = 1e-05
f32 = jnp.float32
bf16 = jnp.bfloat16
VMEM = pl.BlockSpec(memory_space=pltpu.VMEM)
HBM = pl.BlockSpec(memory_space=pltpu.HBM)
SMEM = pl.BlockSpec(memory_space=pltpu.SMEM)


def call(kernel, outs, in_specs, scratch=(), out_specs=None, flops=0, size=4 << 20, name=None):
    return pl.pallas_call(
        kernel,
        out_shape=outs,
        in_specs=in_specs,
        out_specs=jax.tree.map(lambda _: VMEM, outs) if out_specs is None else out_specs,
        scratch_shapes=scratch,
        compiler_params=pltpu.CompilerParams(vmem_limit_bytes=40 << 20),
        cost_estimate=pl.CostEstimate(flops=flops, bytes_accessed=size, transcendentals=0),
        name=name,
    )


def parts(v):
    high = v.astype(bf16).astype(f32)
    rest = v - high
    mid = rest.astype(bf16).astype(f32)
    return high, mid, rest - mid


def to_lanes(square):
    return jnp.sum(square.T, axis=0, keepdims=True)


def to_rows(lanes):
    return jnp.broadcast_to(lanes, (TILE, TILE)).T


def pack_kernel(routes, acts, goals, out, order, rows, columns, route_sem, row_sem, goal_sem):
    copies = [
        pltpu.make_async_copy(routes, order, route_sem),
        pltpu.make_async_copy(acts, rows, row_sem),
        pltpu.make_async_copy(goals, columns, goal_sem),
    ]
    for copy in copies:
        copy.start()

    def clear(d, _):
        out[pl.ds(d * 4, 4)] = jnp.zeros((4, MB, F + C), bf16)
        return 0

    lax.fori_loop(0, NP // 4, clear, 0)
    for copy in copies:
        copy.wait()

    def put(m, _):
        d = order[m]
        out[d, :, :F] = rows[m]
        out[d, :, F:] = columns[m]
        return 0

    lax.fori_loop(0, PIECES, put, 0, unroll=4)


def value_kernel(rows, gain, weights, out, gained, squares):
    for i in range(NTILES):
        x = rows[i * 16 : (i + 1) * 16, :, :F].astype(f32).reshape(TILE, F)
        sq = x * x
        folded = sq[:, :128]
        for j in range(1, F // 128):
            folded = folded + sq[:, j * 128 : (j + 1) * 128]
        squares[i : i + 1, :] = to_lanes(folded)
        gained[i * TILE : (i + 1) * TILE, :] = (x * gain[...]).astype(bf16)
    for i in range(KV // 256):
        partial = jnp.dot(gained[...], weights[:, i * 256 : (i + 1) * 256], preferred_element_type=f32).astype(bf16)
        out[2 * i, :ROWS, :] = partial[:, :C]
        out[2 * i + 1, :ROWS, :] = partial[:, C:]
    high, mid, low = parts(squares[0:4, :])
    tail = jnp.concatenate([high, mid, low, jnp.zeros_like(high)], axis=0).astype(bf16)
    for t in range(NT):
        out[t, ROWS:, :] = tail


def loss_kernel(got, goals, value_out, send, scales, dots):
    tail = got[0, ROWS:, :].astype(f32)
    for t in range(1, NT):
        tail = tail + got[t, ROWS:, :].astype(f32)
    total = tail[0:4] + tail[4:8] + tail[8:12]
    scales[0:4, :] = lax.rsqrt(total / D + epsilon)
    scales[4:8, :] = jnp.zeros((4, 128), f32)

    for i in range(NTILES):
        here = slice(i * TILE, (i + 1) * TILE)
        total = got[0, here, :].astype(f32)
        for t in range(1, NT):
            total = total + got[t, here, :].astype(f32)
        value = total * to_rows(scales[i : i + 1, :])
        value_out[i * 16 : (i + 1) * 16] = value.reshape(16, MB, C).astype(bf16)
        goal = goals[i * 16 : (i + 1) * 16, :, F:].astype(f32).reshape(TILE, C)
        grad = (value - goal).astype(bf16)
        for t in range(NT):
            send[t, here, :] = grad
        dots[i : i + 1, :] = to_lanes(grad.astype(f32) * value)

    high, mid, low = parts(dots[0:4, :])
    tail = jnp.concatenate([high, mid, low, jnp.zeros_like(high)], axis=0).astype(bf16)
    for t in range(NT):
        send[t, ROWS:, :] = tail


def grad_kernel(got, rows, gain, weights, scales, value, back, grads, gains, made, sems):
    tail = got[0, ROWS:, :].astype(f32)
    for t in range(1, NT):
        tail = tail + got[t, ROWS:, :].astype(f32)
    dots = (tail[0:4] + tail[4:8] + tail[8:12]) / D
    copies = []
    sums = [0.0] * (F // 256)
    for half in range(2):
        here = slice(half * ROWS // 2, (half + 1) * ROWS // 2)
        slots = slice(half * NP // 2, (half + 1) * NP // 2)
        for t in range(NT):
            grads[here, t * C : (t + 1) * C] = got[t, here, :]
        tiles = range(half * NTILES // 2, (half + 1) * NTILES // 2)
        scale = [scales[i : i + 1, :] for i in tiles]
        dot = [v * v * dots[i : i + 1, :] for i, v in zip(tiles, scale)]
        scale = jnp.concatenate([to_rows(v) for v in scale], axis=0)
        scale = jnp.concatenate([scale, scale], axis=1)
        dot = jnp.concatenate([to_rows(v) for v in dot], axis=0)
        dot = jnp.concatenate([dot, dot], axis=1)
        made[slots, :, F:] = value[slots]
        for i in range(F // 256):
            at = slice(i * 256, (i + 1) * 256)
            grad_normed = lax.dot_general(
                grads[here, :], weights[at, :], (((1,), (1,)), ((), ())), preferred_element_type=f32
            )
            scaled = grad_normed * scale
            x = rows[slots, :, at].astype(f32).reshape(ROWS // 2, 256)
            row_grad = scaled * gain[:, at] - x * dot
            made[slots, :, at] = row_grad.reshape(NP // 2, MB, 256).astype(bf16)
            sums[i] += jnp.sum((scaled * x).reshape(ROWS // 16, 8, 256), axis=0)
        where = pl.ds(half * NP // 2, NP // 2)
        copies.append(pltpu.make_async_copy(made.at[where], back.at[where], sems.at[half]))
        copies[-1].start()
    for i in range(F // 256):
        gains[:, i * 256 : (i + 1) * 256] = sums[i]
    for copy in copies:
        copy.wait()


def share_kernel(grads, scales, gained, gains, keep, send):
    first = lax.axis_index("core") == 0
    scale = jnp.concatenate([to_rows(scales[i : i + 1, :]) for i in range(NTILES)], axis=0)
    scale = jnp.concatenate([scale, scale], axis=1)
    for i in range(KV // 256):
        scaled = (grads[:, i * 256 : (i + 1) * 256].astype(f32) * scale).astype(bf16)
        mine = lax.dot_general(scaled, gained[...], (((0,), (0,)), ((), ())), preferred_element_type=f32)
        for j in range(8):
            at = slice(i * 128 + j * 16, i * 128 + (j + 1) * 16)
            even = mine[j * 32 : j * 32 + 16, :]
            odd = mine[j * 32 + 16 : j * 32 + 32, :]
            keep[at, :] = jnp.where(first, even, odd)
            send[at, :] = jnp.where(first, odd, even).astype(bf16)

    total = jnp.sum(gains[...], axis=0, keepdims=True)
    keep[KV // 2 :, :] = jnp.concatenate([total, jnp.zeros((EXTRA - 1, F), f32)], axis=0)
    high, mid, low = parts(total)
    tail = jnp.concatenate([high, mid, low, jnp.zeros((EXTRA - 3, F), f32)], axis=0)
    send[KV // 2 :, :] = tail.astype(bf16)


def gain_tail(total):
    high = total.astype(bf16).astype(f32)
    return jnp.concatenate([high, total - high], axis=0).astype(bf16)


def core_kernel(keep, got, own, *sends):
    me = lax.axis_index("x")
    tail = keep[KV // 2 :, :] + got[KV // 2 :, :].astype(f32)
    tail = jnp.sum(tail, axis=0, keepdims=True)
    tail = jnp.concatenate([tail[:, j * 128 : (j + 1) * 128] for j in range(F // 128)], axis=0)

    def put(out, d, tail):
        there = pl.ds(pl.multiple_of(lax.rem(me + d, X) * 128, 128), 128)
        total = keep[there, :] + got[there, :].astype(f32)
        for j in range(F // 128):
            out[j * 128 : (j + 1) * 128, :] = total[:, j * 128 : (j + 1) * 128].astype(out.dtype)
        out[F:, :] = tail

    for d, send in zip(X_STEPS, sends):
        put(send, d, gain_tail(tail))
    put(own, 0, jnp.concatenate([tail, jnp.zeros_like(tail)], axis=0))


def x_kernel(own, *refs):
    *got, out = refs
    for z in range(Z):
        for j in range(F // 128):
            at = slice(j * 128 + z * 16, j * 128 + z * 16 + 16)
            total = own[at, :]
            for g in got:
                total = total + g[at, :].astype(f32)
            out[z, j * 16 : (j + 1) * 16, :] = total.astype(bf16)
    tail = own[F:, :]
    for g in got:
        tail = tail + g[F:, :].astype(f32)
    tail = gain_tail(tail[:8] + tail[8:])
    for z in range(Z):
        out[z, 128:, :] = tail


def last_kernel(got, weight_out, gain_out):
    total = got[0].astype(f32)
    for z in range(1, Z):
        total = total + got[z].astype(f32)
    total = total * GRAD_SCALE
    tail = total[128:136] + total[136:]
    for j in range(F // 128):
        at = slice(j * 128, (j + 1) * 128)
        weight_out[:, at] = total[j * 16 : (j + 1) * 16]
        gain_out[:, at] = tail[j : j + 1]


def unpack_kernel(routes, got, rows, values):
    def take(m, _):
        d = routes[m]
        rows[m] = got[d, :, :F]
        values[m] = got[d, :, F:]
        return 0

    lax.fori_loop(0, PIECES, take, 0)


def shape(*dims, dtype=bf16):
    return jax.ShapeDtypeStruct(dims, dtype)


def exchange(v, axes):
    return lax.all_to_all(v, axes, split_axis=0, concat_axis=0, tiled=True)


def body(activations, targets, routes, value_weights, norm_gains):
    peer = ("x", "z", "core")
    weights = value_weights[0]
    order = routes[:, 0]
    given = order, activations.reshape(PIECES, MB, F), targets.reshape(PIECES, MB, C)
    sends = call(
        pack_kernel,
        shape(NP, MB, F + C),
        [HBM] * 3,
        [
            pltpu.SMEM((PIECES,), jnp.int32),
            pltpu.VMEM((PIECES, MB, F), bf16),
            pltpu.VMEM((PIECES, MB, C), bf16),
        ]
        + [pltpu.SemaphoreType.DMA] * 3,
        name="pack",
    )(*[pltpu.with_memory_space_constraint(v, pltpu.HBM) for v in given])
    arrived = exchange(sends, peer)
    partials, gained = call(
        value_kernel,
        (shape(NT, ROWS + EXTRA, C), shape(ROWS, F)),
        [VMEM] * 3,
        [pltpu.VMEM((8, 128), f32)],
        flops=2 * ROWS * F * KV,
        name="partial_values",
    )(arrived, norm_gains, weights)
    value, grad_part, scales = call(
        loss_kernel,
        (shape(NP, MB, C), shape(NT, ROWS + EXTRA, C), shape(8, 128, dtype=f32)),
        [VMEM] * 2,
        [pltpu.VMEM((8, 128), f32)],
        name="loss",
    )(exchange(partials, "tp"), arrived)
    back, grads, gains = call(
        grad_kernel,
        (shape(NP, MB, F + C), shape(ROWS, KV), shape(8, F, dtype=f32)),
        [VMEM] * 6,
        [pltpu.VMEM((NP, MB, F + C), bf16), pltpu.SemaphoreType.DMA((2,))],
        out_specs=(HBM, VMEM, VMEM),
        flops=2 * ROWS * F * KV,
        size=8 << 20,
        name="grads",
    )(exchange(grad_part, "tp"), arrived, norm_gains, weights, scales, value)
    rows_back = exchange(back, peer)

    half = (KV // CORES + EXTRA, F)
    keep, send = call(
        share_kernel,
        (shape(*half, dtype=f32), shape(*half)),
        [VMEM] * 4,
        flops=2 * ROWS * F * KV,
        name="share",
    )(grads, scales, gained, gains)
    got = lax.ppermute(send, "core", [(0, 1), (1, 0)])
    block = (F + EXTRA, 128)
    own, *sends = call(
        core_kernel, (shape(*block, dtype=f32),) + (shape(*block),) * (X - 1), [VMEM] * 2, name="sum_core"
    )(keep, got)
    got = [lax.ppermute(v, "x", [(i, (i + d) % X) for i in range(X)]) for d, v in zip(X_STEPS, sends)]
    by_x = call(x_kernel, shape(Z, 128 + EXTRA, 128), [VMEM] * X, name="sum_x")(own, *got)
    by_x, rows_back = lax.optimization_barrier((by_x, rows_back))
    by_z = exchange(by_x, "z")
    weight_grad, gain_grad = call(
        last_kernel, (shape(16, F, dtype=f32), shape(1, F, dtype=f32)), [VMEM], name="sum_z"
    )(by_z)
    grad_rows, values = call(
        unpack_kernel,
        (shape(PIECES, MB, F), shape(PIECES, MB, C)),
        [SMEM, VMEM],
        name="unpack",
    )(order, rows_back)
    return (
        grad_rows.reshape(PIECES * MB, F),
        values.reshape(PIECES * MB, C),
        weight_grad,
        gain_grad[0],
    )


def solution(mesh):
    split = Mesh(mesh.devices.reshape(X, Z, CORES, NT), ("x", "z", "core", "tp"))
    peer = ("x", "z", "core")
    return jax.shard_map(
        body,
        mesh=split,
        in_specs=(
            P(peer, "tp"),
            P(peer, "tp"),
            P(peer, None),
            P(peer, "tp", None),
            P(peer, "tp"),
        ),
        out_specs=(P(peer, "tp"), P(peer, "tp"), P(peer, "tp"), P("tp")),
        check_vma=False,
    )
```

```python
import jax
import jax.numpy as jnp
from jax import lax
from jax.experimental import pallas as pl
from jax.experimental.pallas import tpu as pltpu
from jax.sharding import Mesh, PartitionSpec as P

D = 8192
KV = 1024
PIECES = 32
MB = 8
F = 1024
C = 128
NP = 64
NT = 8
X, Z, CORES = 4, 8, 2
X_STEPS = (2, 1, 3)
ROWS = NP * MB
TILE = 128
NTILES = ROWS // TILE
EXTRA = 16
SUMS = 8
GRAD_SCALE = (ROWS // 2 * NP) ** (-0.5)

epsilon = 1e-05
f32 = jnp.float32
bf16 = jnp.bfloat16
VMEM = pl.BlockSpec(memory_space=pltpu.VMEM)
HBM = pl.BlockSpec(memory_space=pltpu.HBM)
SMEM = pl.BlockSpec(memory_space=pltpu.SMEM)


def call(kernel, outs, in_specs, scratch=(), out_specs=None, flops=0, size=4 << 20, name=None):
    return pl.pallas_call(
        kernel,
        out_shape=outs,
        in_specs=in_specs,
        out_specs=jax.tree.map(lambda _: VMEM, outs) if out_specs is None else out_specs,
        scratch_shapes=scratch,
        compiler_params=pltpu.CompilerParams(vmem_limit_bytes=40 << 20),
        cost_estimate=pl.CostEstimate(flops=flops, bytes_accessed=size, transcendentals=0),
        name=name,
    )


def parts(v):
    high = v.astype(bf16).astype(f32)
    rest = v - high
    mid = rest.astype(bf16).astype(f32)
    return high, mid, rest - mid


def halves(v):
    high = v.astype(bf16).astype(f32)
    return high, v - high


def to_lanes(square):
    return jnp.sum(square.T, axis=0, keepdims=True)


def to_rows(lanes):
    return jnp.broadcast_to(lanes, (TILE, TILE)).T


def pack_kernel(routes, acts, goals, out, order, rows, columns, route_sem, row_sem, goal_sem):
    copies = [
        pltpu.make_async_copy(routes, order, route_sem),
        pltpu.make_async_copy(acts, rows, row_sem),
        pltpu.make_async_copy(goals, columns, goal_sem),
    ]
    for copy in copies:
        copy.start()

    def clear(d, _):
        out[pl.ds(d * 4, 4)] = jnp.zeros((4, MB, F + C), bf16)
        return 0

    lax.fori_loop(0, NP // 4, clear, 0)
    for copy in copies:
        copy.wait()

    def put(m, _):
        d = order[m]
        out[d, :, :F] = rows[m]
        out[d, :, F:] = columns[m]
        return 0

    lax.fori_loop(0, PIECES, put, 0, unroll=4)


def value_kernel(rows, gain, weights, out, gained, squares):
    for i in range(NTILES):
        x = rows[i * 16 : (i + 1) * 16, :, :F].astype(f32).reshape(TILE, F)
        sq = x * x
        folded = sq[:, :128]
        for j in range(1, F // 128):
            folded = folded + sq[:, j * 128 : (j + 1) * 128]
        squares[i : i + 1, :] = to_lanes(folded)
        gained[i * TILE : (i + 1) * TILE, :] = (x * gain[...]).astype(bf16)
    for i in range(KV // 256):
        partial = jnp.dot(gained[...], weights[:, i * 256 : (i + 1) * 256], preferred_element_type=f32).astype(bf16)
        out[2 * i, :ROWS, :] = partial[:, :C]
        out[2 * i + 1, :ROWS, :] = partial[:, C:]
    high, rest = halves(squares[0:4, :])
    tail = jnp.concatenate([high, rest], axis=0).astype(bf16)
    for t in range(NT):
        out[t, ROWS:, :] = tail


def loss_kernel(got, goals, value_out, send, scales, dots):
    tail = got[0, ROWS:, :].astype(f32)
    for t in range(1, NT):
        tail = tail + got[t, ROWS:, :].astype(f32)
    total = tail[0:4] + tail[4:8]
    scales[0:4, :] = lax.rsqrt(total / D + epsilon)
    scales[4:8, :] = jnp.zeros((4, 128), f32)

    for i in range(NTILES):
        here = slice(i * TILE, (i + 1) * TILE)
        total = got[0, here, :].astype(f32)
        for t in range(1, NT):
            total = total + got[t, here, :].astype(f32)
        value = total * to_rows(scales[i : i + 1, :])
        value_out[i * 16 : (i + 1) * 16] = value.reshape(16, MB, C).astype(bf16)
        goal = goals[i * 16 : (i + 1) * 16, :, F:].astype(f32).reshape(TILE, C)
        grad = (value - goal).astype(bf16)
        for t in range(NT):
            send[t, here, :] = grad
        dots[i : i + 1, :] = to_lanes(grad.astype(f32) * value)

    high, rest = halves(dots[0:4, :])
    tail = jnp.concatenate([high, rest], axis=0).astype(bf16)
    for t in range(NT):
        send[t, ROWS:, :] = tail


def grad_kernel(got, rows, gain, weights, scales, value, back, grads, gains, made, sems):
    tail = got[0, ROWS:, :].astype(f32)
    for t in range(1, NT):
        tail = tail + got[t, ROWS:, :].astype(f32)
    dots = (tail[0:4] + tail[4:8]) / D
    copies = []
    sums = [0.0] * (F // 256)
    for half in range(2):
        here = slice(half * ROWS // 2, (half + 1) * ROWS // 2)
        slots = slice(half * NP // 2, (half + 1) * NP // 2)
        for t in range(NT):
            grads[here, t * C : (t + 1) * C] = got[t, here, :]
        tiles = range(half * NTILES // 2, (half + 1) * NTILES // 2)
        scale = [scales[i : i + 1, :] for i in tiles]
        dot = [v * v * dots[i : i + 1, :] for i, v in zip(tiles, scale)]
        scale = jnp.concatenate([to_rows(v) for v in scale], axis=0)
        scale = jnp.concatenate([scale, scale], axis=1)
        dot = jnp.concatenate([to_rows(v) for v in dot], axis=0)
        dot = jnp.concatenate([dot, dot], axis=1)
        made[slots, :, F:] = value[slots]
        for i in range(F // 256):
            at = slice(i * 256, (i + 1) * 256)
            grad_normed = lax.dot_general(
                grads[here, :], weights[at, :], (((1,), (1,)), ((), ())), preferred_element_type=f32
            )
            scaled = grad_normed * scale
            x = rows[slots, :, at].astype(f32).reshape(ROWS // 2, 256)
            row_grad = scaled * gain[:, at] - x * dot
            made[slots, :, at] = row_grad.reshape(NP // 2, MB, 256).astype(bf16)
            sums[i] += jnp.sum((scaled * x).reshape(ROWS // 16, 8, 256), axis=0)
        where = pl.ds(half * NP // 2, NP // 2)
        copies.append(pltpu.make_async_copy(made.at[where], back.at[where], sems.at[half]))
        copies[-1].start()
    for i in range(F // 256):
        gains[:, i * 256 : (i + 1) * 256] = sums[i]
    for copy in copies:
        copy.wait()


def share_kernel(grads, scales, gained, gains, keep, send):
    first = lax.axis_index("core") == 0
    scale = jnp.concatenate([to_rows(scales[i : i + 1, :]) for i in range(NTILES)], axis=0)
    scale = jnp.concatenate([scale, scale], axis=1)
    for i in range(KV // 256):
        scaled = (grads[:, i * 256 : (i + 1) * 256].astype(f32) * scale).astype(bf16)
        mine = lax.dot_general(scaled, gained[...], (((0,), (0,)), ((), ())), preferred_element_type=f32)
        for j in range(8):
            at = slice(i * 128 + j * 16, i * 128 + (j + 1) * 16)
            even = mine[j * 32 : j * 32 + 16, :]
            odd = mine[j * 32 + 16 : j * 32 + 32, :]
            keep[at, :] = jnp.where(first, even, odd)
            send[at, :] = jnp.where(first, odd, even).astype(bf16)

    total = jnp.sum(gains[...], axis=0, keepdims=True)
    keep[KV // 2 :, :] = jnp.concatenate([total, jnp.zeros((EXTRA - 1, F), f32)], axis=0)
    high, mid, low = parts(total)
    tail = jnp.concatenate([high, mid, low, jnp.zeros((EXTRA - 3, F), f32)], axis=0)
    send[KV // 2 :, :] = tail.astype(bf16)


def gain_tail(total):
    high = total.astype(bf16).astype(f32)
    return jnp.concatenate([high, total - high], axis=0).astype(bf16)


def core_kernel(keep, got, own, *sends):
    me = lax.axis_index("x")
    tail = keep[KV // 2 :, :] + got[KV // 2 :, :].astype(f32)
    tail = jnp.sum(tail, axis=0, keepdims=True)
    tail = jnp.concatenate([tail[:, j * 128 : (j + 1) * 128] for j in range(F // 128)], axis=0)

    def put(out, d, tail):
        there = pl.ds(pl.multiple_of(lax.rem(me + d, X) * 128, 128), 128)
        total = keep[there, :] + got[there, :].astype(f32)
        for j in range(F // 128):
            out[j * 128 : (j + 1) * 128, :] = total[:, j * 128 : (j + 1) * 128].astype(out.dtype)
        out[F:, :] = tail

    for d, send in zip(X_STEPS, sends):
        put(send, d, gain_tail(tail))
    put(own, 0, jnp.concatenate([tail, jnp.zeros_like(tail)], axis=0))


def x_kernel(own, *refs):
    *got, out = refs
    for z in range(Z):
        for j in range(F // 128):
            at = slice(j * 128 + z * 16, j * 128 + z * 16 + 16)
            total = own[at, :]
            for g in got:
                total = total + g[at, :].astype(f32)
            out[z, j * 16 : (j + 1) * 16, :] = total.astype(bf16)
    tail = own[F:, :]
    for g in got:
        tail = tail + g[F:, :].astype(f32)
    tail = gain_tail(tail[:8] + tail[8:])
    for z in range(Z):
        out[z, 128:, :] = tail


def last_kernel(got, weight_out, gain_out):
    total = got[0].astype(f32)
    for z in range(1, Z):
        total = total + got[z].astype(f32)
    total = total * GRAD_SCALE
    tail = total[128:136] + total[136:]
    for j in range(F // 128):
        at = slice(j * 128, (j + 1) * 128)
        weight_out[:, at] = total[j * 16 : (j + 1) * 16]
        gain_out[:, at] = tail[j : j + 1]


def unpack_kernel(routes, got, rows, values):
    def take(m, _):
        d = routes[m]
        rows[m] = got[d, :, :F]
        values[m] = got[d, :, F:]
        return 0

    lax.fori_loop(0, PIECES, take, 0)


def shape(*dims, dtype=bf16):
    return jax.ShapeDtypeStruct(dims, dtype)


def exchange(v, axes):
    return lax.all_to_all(v, axes, split_axis=0, concat_axis=0, tiled=True)


def body(activations, targets, routes, value_weights, norm_gains):
    peer = ("x", "z", "core")
    weights = value_weights[0]
    order = routes[:, 0]
    given = order, activations.reshape(PIECES, MB, F), targets.reshape(PIECES, MB, C)
    sends = call(
        pack_kernel,
        shape(NP, MB, F + C),
        [HBM] * 3,
        [
            pltpu.SMEM((PIECES,), jnp.int32),
            pltpu.VMEM((PIECES, MB, F), bf16),
            pltpu.VMEM((PIECES, MB, C), bf16),
        ]
        + [pltpu.SemaphoreType.DMA] * 3,
        name="pack",
    )(*[pltpu.with_memory_space_constraint(v, pltpu.HBM) for v in given])
    arrived = exchange(sends, peer)
    partials, gained = call(
        value_kernel,
        (shape(NT, ROWS + SUMS, C), shape(ROWS, F)),
        [VMEM] * 3,
        [pltpu.VMEM((8, 128), f32)],
        flops=2 * ROWS * F * KV,
        name="partial_values",
    )(arrived, norm_gains, weights)
    value, grad_part, scales = call(
        loss_kernel,
        (shape(NP, MB, C), shape(NT, ROWS + SUMS, C), shape(8, 128, dtype=f32)),
        [VMEM] * 2,
        [pltpu.VMEM((8, 128), f32)],
        name="loss",
    )(exchange(partials, "tp"), arrived)
    back, grads, gains = call(
        grad_kernel,
        (shape(NP, MB, F + C), shape(ROWS, KV), shape(8, F, dtype=f32)),
        [VMEM] * 6,
        [pltpu.VMEM((NP, MB, F + C), bf16), pltpu.SemaphoreType.DMA((2,))],
        out_specs=(HBM, VMEM, VMEM),
        flops=2 * ROWS * F * KV,
        size=8 << 20,
        name="grads",
    )(exchange(grad_part, "tp"), arrived, norm_gains, weights, scales, value)
    rows_back = exchange(back, peer)

    half = (KV // CORES + EXTRA, F)
    keep, send = call(
        share_kernel,
        (shape(*half, dtype=f32), shape(*half)),
        [VMEM] * 4,
        flops=2 * ROWS * F * KV,
        name="share",
    )(grads, scales, gained, gains)
    got = lax.ppermute(send, "core", [(0, 1), (1, 0)])
    block = (F + EXTRA, 128)
    own, *sends = call(
        core_kernel, (shape(*block, dtype=f32),) + (shape(*block),) * (X - 1), [VMEM] * 2, name="sum_core"
    )(keep, got)
    got = [lax.ppermute(v, "x", [(i, (i + d) % X) for i in range(X)]) for d, v in zip(X_STEPS, sends)]
    grad_rows, values = call(
        unpack_kernel,
        (shape(PIECES, MB, F), shape(PIECES, MB, C)),
        [SMEM, VMEM],
        name="unpack",
    )(order, rows_back)
    got, grad_rows, values = lax.optimization_barrier((got, grad_rows, values))
    by_x = call(x_kernel, shape(Z, 128 + EXTRA, 128), [VMEM] * X, name="sum_x")(own, *got)
    by_z = exchange(by_x, "z")
    weight_grad, gain_grad = call(
        last_kernel, (shape(16, F, dtype=f32), shape(1, F, dtype=f32)), [VMEM], name="sum_z"
    )(by_z)
    return (
        grad_rows.reshape(PIECES * MB, F),
        values.reshape(PIECES * MB, C),
        weight_grad,
        gain_grad[0],
    )


def solution(mesh):
    split = Mesh(mesh.devices.reshape(X, Z, CORES, NT), ("x", "z", "core", "tp"))
    peer = ("x", "z", "core")
    return jax.shard_map(
        body,
        mesh=split,
        in_specs=(
            P(peer, "tp"),
            P(peer, "tp"),
            P(peer, None),
            P(peer, "tp", None),
            P(peer, "tp"),
        ),
        out_specs=(P(peer, "tp"), P(peer, "tp"), P(peer, "tp"), P("tp")),
        check_vma=False,
    )
```

```python
import jax
import jax.numpy as jnp
from jax import lax
from jax.experimental import pallas as pl
from jax.experimental.pallas import tpu as pltpu
from jax.sharding import Mesh, PartitionSpec as P

D = 8192
KV = 1024
PIECES = 32
MB = 8
F = 1024
C = 128
NP = 64
NT = 8
X, Z, CORES = 4, 8, 2
X_STEPS = (2, 1, 3)
ROWS = NP * MB
TILE = 128
NTILES = ROWS // TILE
EXTRA = 16
SUMS = 8
GRAD_SCALE = (ROWS // 2 * NP) ** (-0.5)

epsilon = 1e-05
f32 = jnp.float32
bf16 = jnp.bfloat16
VMEM = pl.BlockSpec(memory_space=pltpu.VMEM)
HBM = pl.BlockSpec(memory_space=pltpu.HBM)
SMEM = pl.BlockSpec(memory_space=pltpu.SMEM)


def call(kernel, outs, in_specs, scratch=(), out_specs=None, flops=0, size=4 << 20, name=None):
    return pl.pallas_call(
        kernel,
        out_shape=outs,
        in_specs=in_specs,
        out_specs=jax.tree.map(lambda _: VMEM, outs) if out_specs is None else out_specs,
        scratch_shapes=scratch,
        compiler_params=pltpu.CompilerParams(vmem_limit_bytes=40 << 20),
        cost_estimate=pl.CostEstimate(flops=flops, bytes_accessed=size, transcendentals=0),
        name=name,
    )


def parts(v):
    high = v.astype(bf16).astype(f32)
    rest = v - high
    mid = rest.astype(bf16).astype(f32)
    return high, mid, rest - mid


def halves(v):
    high = v.astype(bf16).astype(f32)
    return high, v - high


def to_lanes(square):
    return jnp.sum(square.T, axis=0, keepdims=True)


def to_rows(lanes):
    return jnp.broadcast_to(lanes, (TILE, TILE)).T


def pack_kernel(routes, acts, goals, out, order, rows, columns, route_sem, row_sem, goal_sem):
    copies = [
        pltpu.make_async_copy(routes, order, route_sem),
        pltpu.make_async_copy(acts, rows, row_sem),
        pltpu.make_async_copy(goals, columns, goal_sem),
    ]
    for copy in copies:
        copy.start()

    def clear(d, _):
        out[pl.ds(d * 4, 4)] = jnp.zeros((4, MB, F + C), bf16)
        return 0

    lax.fori_loop(0, NP // 4, clear, 0)
    for copy in copies:
        copy.wait()

    def put(m, _):
        d = order[m]
        out[d, :, :F] = rows[m]
        out[d, :, F:] = columns[m]
        return 0

    lax.fori_loop(0, PIECES, put, 0, unroll=4)


def value_kernel(rows, gain, weights, out, gained, squares):
    for i in range(NTILES):
        x = rows[i * 16 : (i + 1) * 16, :, :F].astype(f32).reshape(TILE, F)
        sq = x * x
        folded = sq[:, :128]
        for j in range(1, F // 128):
            folded = folded + sq[:, j * 128 : (j + 1) * 128]
        squares[i : i + 1, :] = to_lanes(folded)
        gained[i * TILE : (i + 1) * TILE, :] = (x * gain[...]).astype(bf16)
    for i in range(KV // 256):
        partial = jnp.dot(gained[...], weights[:, i * 256 : (i + 1) * 256], preferred_element_type=f32).astype(bf16)
        out[2 * i, :ROWS, :] = partial[:, :C]
        out[2 * i + 1, :ROWS, :] = partial[:, C:]
    high, rest = halves(squares[0:4, :])
    tail = jnp.concatenate([high, rest], axis=0).astype(bf16)
    for t in range(NT):
        out[t, ROWS:, :] = tail


def loss_kernel(got, goals, value_out, send, scales, dots):
    tail = got[0, ROWS:, :].astype(f32)
    for t in range(1, NT):
        tail = tail + got[t, ROWS:, :].astype(f32)
    total = tail[0:4] + tail[4:8]
    scales[0:4, :] = lax.rsqrt(total / D + epsilon)
    scales[4:8, :] = jnp.zeros((4, 128), f32)

    for i in range(NTILES):
        here = slice(i * TILE, (i + 1) * TILE)
        total = got[0, here, :].astype(f32)
        for t in range(1, NT):
            total = total + got[t, here, :].astype(f32)
        value = total * to_rows(scales[i : i + 1, :])
        value_out[i * 16 : (i + 1) * 16] = value.reshape(16, MB, C).astype(bf16)
        goal = goals[i * 16 : (i + 1) * 16, :, F:].astype(f32).reshape(TILE, C)
        grad = (value - goal).astype(bf16)
        for t in range(NT):
            send[t, here, :] = grad
        dots[i : i + 1, :] = to_lanes(grad.astype(f32) * value)

    high, rest = halves(dots[0:4, :])
    tail = jnp.concatenate([high, rest], axis=0).astype(bf16)
    for t in range(NT):
        send[t, ROWS:, :] = tail


def grad_kernel(got, rows, gain, weights, scales, value, back, grads, gains, made, sems):
    tail = got[0, ROWS:, :].astype(f32)
    for t in range(1, NT):
        tail = tail + got[t, ROWS:, :].astype(f32)
    dots = (tail[0:4] + tail[4:8]) / D
    copies = []
    sums = [0.0] * (F // 256)
    for half in range(2):
        here = slice(half * ROWS // 2, (half + 1) * ROWS // 2)
        slots = slice(half * NP // 2, (half + 1) * NP // 2)
        for t in range(NT):
            grads[here, t * C : (t + 1) * C] = got[t, here, :]
        tiles = range(half * NTILES // 2, (half + 1) * NTILES // 2)
        scale = [scales[i : i + 1, :] for i in tiles]
        dot = [v * v * dots[i : i + 1, :] for i, v in zip(tiles, scale)]
        scale = jnp.concatenate([to_rows(v) for v in scale], axis=0)
        scale = jnp.concatenate([scale, scale], axis=1)
        dot = jnp.concatenate([to_rows(v) for v in dot], axis=0)
        dot = jnp.concatenate([dot, dot], axis=1)
        made[slots, :, F:] = value[slots]
        for i in range(F // 256):
            at = slice(i * 256, (i + 1) * 256)
            grad_normed = lax.dot_general(
                grads[here, :], weights[at, :], (((1,), (1,)), ((), ())), preferred_element_type=f32
            )
            scaled = grad_normed * scale
            x = rows[slots, :, at].astype(f32).reshape(ROWS // 2, 256)
            row_grad = scaled * gain[:, at] - x * dot
            made[slots, :, at] = row_grad.reshape(NP // 2, MB, 256).astype(bf16)
            sums[i] += jnp.sum((scaled * x).reshape(ROWS // 16, 8, 256), axis=0)
        where = pl.ds(half * NP // 2, NP // 2)
        copies.append(pltpu.make_async_copy(made.at[where], back.at[where], sems.at[half]))
        copies[-1].start()
    for i in range(F // 256):
        gains[:, i * 256 : (i + 1) * 256] = sums[i]
    for copy in copies:
        copy.wait()


def share_kernel(grads, scales, gained, gains, keep, send):
    first = lax.axis_index("core") == 0
    scale = jnp.concatenate([to_rows(scales[i : i + 1, :]) for i in range(NTILES)], axis=0)
    scale = jnp.concatenate([scale, scale], axis=1)
    for i in range(KV // 256):
        scaled = (grads[:, i * 256 : (i + 1) * 256].astype(f32) * scale).astype(bf16)
        mine = lax.dot_general(scaled, gained[...], (((0,), (0,)), ((), ())), preferred_element_type=f32)
        for j in range(8):
            at = slice(i * 128 + j * 16, i * 128 + (j + 1) * 16)
            even = mine[j * 32 : j * 32 + 16, :]
            odd = mine[j * 32 + 16 : j * 32 + 32, :]
            keep[at, :] = jnp.where(first, even, odd)
            send[at, :] = jnp.where(first, odd, even).astype(bf16)

    total = jnp.sum(gains[...], axis=0, keepdims=True)
    keep[KV // 2 :, :] = jnp.concatenate([total, jnp.zeros((EXTRA - 1, F), f32)], axis=0)
    high, mid, low = parts(total)
    tail = jnp.concatenate([high, mid, low, jnp.zeros((EXTRA - 3, F), f32)], axis=0)
    send[KV // 2 :, :] = tail.astype(bf16)


def gain_tail(total):
    high = total.astype(bf16).astype(f32)
    return jnp.concatenate([high, total - high], axis=0).astype(bf16)


def core_kernel(keep, got, own, *sends):
    me = lax.axis_index("x")
    tail = keep[KV // 2 :, :] + got[KV // 2 :, :].astype(f32)
    tail = jnp.sum(tail, axis=0, keepdims=True)
    tail = jnp.concatenate([tail[:, j * 128 : (j + 1) * 128] for j in range(F // 128)], axis=0)

    def put(out, d, tail):
        there = pl.ds(pl.multiple_of(lax.rem(me + d, X) * 128, 128), 128)
        total = keep[there, :] + got[there, :].astype(f32)
        for j in range(F // 128):
            out[j * 128 : (j + 1) * 128, :] = total[:, j * 128 : (j + 1) * 128].astype(out.dtype)
        out[F:, :] = tail

    for d, send in zip(X_STEPS, sends):
        put(send, d, gain_tail(tail))
    put(own, 0, jnp.concatenate([tail, jnp.zeros_like(tail)], axis=0))


def x_kernel(own, *refs):
    *got, out = refs
    for z in range(Z):
        for j in range(F // 128):
            at = slice(j * 128 + z * 16, j * 128 + z * 16 + 16)
            total = own[at, :]
            for g in got:
                total = total + g[at, :].astype(f32)
            out[z, j * 16 : (j + 1) * 16, :] = total.astype(bf16)
    tail = own[F:, :]
    for g in got:
        tail = tail + g[F:, :].astype(f32)
    tail = (tail[:8] + tail[8:]).astype(bf16)
    for z in range(Z):
        out[z, 128:, :] = tail


def last_kernel(got, weight_out, gain_out):
    total = got[0].astype(f32)
    for z in range(1, Z):
        total = total + got[z].astype(f32)
    total = total * GRAD_SCALE
    tail = total[128:]
    for j in range(F // 128):
        at = slice(j * 128, (j + 1) * 128)
        weight_out[:, at] = total[j * 16 : (j + 1) * 16]
        gain_out[:, at] = tail[j : j + 1]


def unpack_kernel(routes, got, rows, values):
    def take(m, _):
        d = routes[m]
        rows[m] = got[d, :, :F]
        values[m] = got[d, :, F:]
        return 0

    lax.fori_loop(0, PIECES, take, 0)


def shape(*dims, dtype=bf16):
    return jax.ShapeDtypeStruct(dims, dtype)


def exchange(v, axes):
    return lax.all_to_all(v, axes, split_axis=0, concat_axis=0, tiled=True)


def body(activations, targets, routes, value_weights, norm_gains):
    peer = ("x", "z", "core")
    weights = value_weights[0]
    order = routes[:, 0]
    given = order, activations.reshape(PIECES, MB, F), targets.reshape(PIECES, MB, C)
    sends = call(
        pack_kernel,
        shape(NP, MB, F + C),
        [HBM] * 3,
        [
            pltpu.SMEM((PIECES,), jnp.int32),
            pltpu.VMEM((PIECES, MB, F), bf16),
            pltpu.VMEM((PIECES, MB, C), bf16),
        ]
        + [pltpu.SemaphoreType.DMA] * 3,
        name="pack",
    )(*[pltpu.with_memory_space_constraint(v, pltpu.HBM) for v in given])
    arrived = exchange(sends, peer)
    partials, gained = call(
        value_kernel,
        (shape(NT, ROWS + SUMS, C), shape(ROWS, F)),
        [VMEM] * 3,
        [pltpu.VMEM((8, 128), f32)],
        flops=2 * ROWS * F * KV,
        name="partial_values",
    )(arrived, norm_gains, weights)
    value, grad_part, scales = call(
        loss_kernel,
        (shape(NP, MB, C), shape(NT, ROWS + SUMS, C), shape(8, 128, dtype=f32)),
        [VMEM] * 2,
        [pltpu.VMEM((8, 128), f32)],
        name="loss",
    )(exchange(partials, "tp"), arrived)
    back, grads, gains = call(
        grad_kernel,
        (shape(NP, MB, F + C), shape(ROWS, KV), shape(8, F, dtype=f32)),
        [VMEM] * 6,
        [pltpu.VMEM((NP, MB, F + C), bf16), pltpu.SemaphoreType.DMA((2,))],
        out_specs=(HBM, VMEM, VMEM),
        flops=2 * ROWS * F * KV,
        size=8 << 20,
        name="grads",
    )(exchange(grad_part, "tp"), arrived, norm_gains, weights, scales, value)
    rows_back = exchange(back, peer)

    half = (KV // CORES + EXTRA, F)
    keep, send = call(
        share_kernel,
        (shape(*half, dtype=f32), shape(*half)),
        [VMEM] * 4,
        flops=2 * ROWS * F * KV,
        name="share",
    )(grads, scales, gained, gains)
    got = lax.ppermute(send, "core", [(0, 1), (1, 0)])
    block = (F + EXTRA, 128)
    own, *sends = call(
        core_kernel, (shape(*block, dtype=f32),) + (shape(*block),) * (X - 1), [VMEM] * 2, name="sum_core"
    )(keep, got)
    got = [lax.ppermute(v, "x", [(i, (i + d) % X) for i in range(X)]) for d, v in zip(X_STEPS, sends)]
    grad_rows, values = call(
        unpack_kernel,
        (shape(PIECES, MB, F), shape(PIECES, MB, C)),
        [SMEM, VMEM],
        name="unpack",
    )(order, rows_back)
    got, grad_rows, values = lax.optimization_barrier((got, grad_rows, values))
    by_x = call(x_kernel, shape(Z, 128 + 8, 128), [VMEM] * X, name="sum_x")(own, *got)
    by_z = exchange(by_x, "z")
    weight_grad, gain_grad = call(
        last_kernel, (shape(16, F, dtype=f32), shape(1, F, dtype=f32)), [VMEM], name="sum_z"
    )(by_z)
    return (
        grad_rows.reshape(PIECES * MB, F),
        values.reshape(PIECES * MB, C),
        weight_grad,
        gain_grad[0],
    )


def solution(mesh):
    split = Mesh(mesh.devices.reshape(X, Z, CORES, NT), ("x", "z", "core", "tp"))
    peer = ("x", "z", "core")
    return jax.shard_map(
        body,
        mesh=split,
        in_specs=(
            P(peer, "tp"),
            P(peer, "tp"),
            P(peer, None),
            P(peer, "tp", None),
            P(peer, "tp"),
        ),
        out_specs=(P(peer, "tp"), P(peer, "tp"), P(peer, "tp"), P("tp")),
        check_vma=False,
    )
```

```python
import jax
import jax.numpy as jnp
from jax import lax
from jax.experimental import pallas as pl
from jax.experimental.pallas import tpu as pltpu
from jax.sharding import Mesh, PartitionSpec as P

D = 8192
KV = 1024
PIECES = 32
MB = 8
F = 1024
C = 128
NP = 64
NT = 8
X, Z, CORES = 4, 8, 2
X_STEPS = (2, 1, 3)
ROWS = NP * MB
TILE = 128
NTILES = ROWS // TILE
EXTRA = 16
SUMS = 8
GRAD_SCALE = (ROWS // 2 * NP) ** (-0.5)

epsilon = 1e-05
f32 = jnp.float32
bf16 = jnp.bfloat16
VMEM = pl.BlockSpec(memory_space=pltpu.VMEM)
HBM = pl.BlockSpec(memory_space=pltpu.HBM)
SMEM = pl.BlockSpec(memory_space=pltpu.SMEM)


def call(kernel, outs, in_specs, scratch=(), out_specs=None, flops=0, size=4 << 20, name=None):
    return pl.pallas_call(
        kernel,
        out_shape=outs,
        in_specs=in_specs,
        out_specs=jax.tree.map(lambda _: VMEM, outs) if out_specs is None else out_specs,
        scratch_shapes=scratch,
        compiler_params=pltpu.CompilerParams(vmem_limit_bytes=40 << 20),
        cost_estimate=pl.CostEstimate(flops=flops, bytes_accessed=size, transcendentals=0),
        name=name,
    )


def parts(v):
    high = v.astype(bf16).astype(f32)
    rest = v - high
    mid = rest.astype(bf16).astype(f32)
    return high, mid, rest - mid


def halves(v):
    high = v.astype(bf16).astype(f32)
    return high, v - high


def to_lanes(square):
    return jnp.sum(square.T, axis=0, keepdims=True)


def to_rows(lanes):
    return jnp.broadcast_to(lanes, (TILE, TILE)).T


def pack_kernel(routes, acts, goals, out, order, rows, columns, route_sem, row_sem, goal_sem):
    copies = [
        pltpu.make_async_copy(routes, order, route_sem),
        pltpu.make_async_copy(acts, rows, row_sem),
        pltpu.make_async_copy(goals, columns, goal_sem),
    ]
    for copy in copies:
        copy.start()

    def clear(d, _):
        out[pl.ds(d * 4, 4)] = jnp.zeros((4, MB, F + C), bf16)
        return 0

    lax.fori_loop(0, NP // 4, clear, 0)
    for copy in copies:
        copy.wait()

    def put(m, _):
        d = order[m]
        out[d, :, :F] = rows[m]
        out[d, :, F:] = columns[m]
        return 0

    lax.fori_loop(0, PIECES, put, 0, unroll=8)


def value_kernel(rows, gain, weights, out, gained, squares):
    for i in range(NTILES):
        x = rows[i * 16 : (i + 1) * 16, :, :F].astype(f32).reshape(TILE, F)
        sq = x * x
        folded = sq[:, :128]
        for j in range(1, F // 128):
            folded = folded + sq[:, j * 128 : (j + 1) * 128]
        squares[i : i + 1, :] = to_lanes(folded)
        gained[i * TILE : (i + 1) * TILE, :] = (x * gain[...]).astype(bf16)
    for i in range(KV // 256):
        partial = jnp.dot(gained[...], weights[:, i * 256 : (i + 1) * 256], preferred_element_type=f32).astype(bf16)
        out[2 * i, :ROWS, :] = partial[:, :C]
        out[2 * i + 1, :ROWS, :] = partial[:, C:]
    high, rest = halves(squares[0:4, :])
    tail = jnp.concatenate([high, rest], axis=0).astype(bf16)
    for t in range(NT):
        out[t, ROWS:, :] = tail


def loss_kernel(got, goals, value_out, send, scales, dots):
    tail = got[0, ROWS:, :].astype(f32)
    for t in range(1, NT):
        tail = tail + got[t, ROWS:, :].astype(f32)
    total = tail[0:4] + tail[4:8]
    scales[0:4, :] = lax.rsqrt(total / D + epsilon)
    scales[4:8, :] = jnp.zeros((4, 128), f32)

    for i in range(NTILES):
        here = slice(i * TILE, (i + 1) * TILE)
        total = got[0, here, :].astype(f32)
        for t in range(1, NT):
            total = total + got[t, here, :].astype(f32)
        value = total * to_rows(scales[i : i + 1, :])
        value_out[i * 16 : (i + 1) * 16] = value.reshape(16, MB, C).astype(bf16)
        goal = goals[i * 16 : (i + 1) * 16, :, F:].astype(f32).reshape(TILE, C)
        grad = (value - goal).astype(bf16)
        for t in range(NT):
            send[t, here, :] = grad
        dots[i : i + 1, :] = to_lanes(grad.astype(f32) * value)

    high, rest = halves(dots[0:4, :])
    tail = jnp.concatenate([high, rest], axis=0).astype(bf16)
    for t in range(NT):
        send[t, ROWS:, :] = tail


def grad_kernel(got, rows, gain, weights, scales, value, back, grads, gains, made, sems):
    tail = got[0, ROWS:, :].astype(f32)
    for t in range(1, NT):
        tail = tail + got[t, ROWS:, :].astype(f32)
    dots = (tail[0:4] + tail[4:8]) / D
    copies = []
    sums = [0.0] * (F // 256)
    for half in range(2):
        here = slice(half * ROWS // 2, (half + 1) * ROWS // 2)
        slots = slice(half * NP // 2, (half + 1) * NP // 2)
        for t in range(NT):
            grads[here, t * C : (t + 1) * C] = got[t, here, :]
        tiles = range(half * NTILES // 2, (half + 1) * NTILES // 2)
        scale = [scales[i : i + 1, :] for i in tiles]
        dot = [v * v * dots[i : i + 1, :] for i, v in zip(tiles, scale)]
        scale = jnp.concatenate([to_rows(v) for v in scale], axis=0)
        scale = jnp.concatenate([scale, scale], axis=1)
        dot = jnp.concatenate([to_rows(v) for v in dot], axis=0)
        dot = jnp.concatenate([dot, dot], axis=1)
        made[slots, :, F:] = value[slots]
        for i in range(F // 256):
            at = slice(i * 256, (i + 1) * 256)
            grad_normed = lax.dot_general(
                grads[here, :], weights[at, :], (((1,), (1,)), ((), ())), preferred_element_type=f32
            )
            scaled = grad_normed * scale
            x = rows[slots, :, at].astype(f32).reshape(ROWS // 2, 256)
            row_grad = scaled * gain[:, at] - x * dot
            made[slots, :, at] = row_grad.reshape(NP // 2, MB, 256).astype(bf16)
            sums[i] += jnp.sum((scaled * x).reshape(ROWS // 16, 8, 256), axis=0)
        where = pl.ds(half * NP // 2, NP // 2)
        copies.append(pltpu.make_async_copy(made.at[where], back.at[where], sems.at[half]))
        copies[-1].start()
    for i in range(F // 256):
        gains[:, i * 256 : (i + 1) * 256] = sums[i]
    for copy in copies:
        copy.wait()


def share_kernel(grads, scales, gained, gains, keep, send):
    first = lax.axis_index("core") == 0
    scale = jnp.concatenate([to_rows(scales[i : i + 1, :]) for i in range(NTILES)], axis=0)
    scale = jnp.concatenate([scale, scale], axis=1)
    for i in range(KV // 256):
        scaled = (grads[:, i * 256 : (i + 1) * 256].astype(f32) * scale).astype(bf16)
        mine = lax.dot_general(scaled, gained[...], (((0,), (0,)), ((), ())), preferred_element_type=f32)
        for j in range(8):
            at = slice(i * 128 + j * 16, i * 128 + (j + 1) * 16)
            even = mine[j * 32 : j * 32 + 16, :]
            odd = mine[j * 32 + 16 : j * 32 + 32, :]
            keep[at, :] = jnp.where(first, even, odd)
            send[at, :] = jnp.where(first, odd, even).astype(bf16)

    total = jnp.sum(gains[...], axis=0, keepdims=True)
    keep[KV // 2 :, :] = jnp.concatenate([total, jnp.zeros((EXTRA - 1, F), f32)], axis=0)
    high, mid, low = parts(total)
    tail = jnp.concatenate([high, mid, low, jnp.zeros((EXTRA - 3, F), f32)], axis=0)
    send[KV // 2 :, :] = tail.astype(bf16)


def gain_tail(total):
    high = total.astype(bf16).astype(f32)
    return jnp.concatenate([high, total - high], axis=0).astype(bf16)


def core_kernel(keep, got, own, *sends):
    me = lax.axis_index("x")
    tail = keep[KV // 2 :, :] + got[KV // 2 :, :].astype(f32)
    tail = jnp.sum(tail, axis=0, keepdims=True)
    tail = jnp.concatenate([tail[:, j * 128 : (j + 1) * 128] for j in range(F // 128)], axis=0)

    def put(out, d, tail):
        there = pl.ds(pl.multiple_of(lax.rem(me + d, X) * 128, 128), 128)
        total = keep[there, :] + got[there, :].astype(f32)
        for j in range(F // 128):
            out[j * 128 : (j + 1) * 128, :] = total[:, j * 128 : (j + 1) * 128].astype(out.dtype)
        out[F:, :] = tail

    for d, send in zip(X_STEPS, sends):
        put(send, d, gain_tail(tail))
    put(own, 0, jnp.concatenate([tail, jnp.zeros_like(tail)], axis=0))


def x_kernel(own, *refs):
    *got, out = refs
    for z in range(Z):
        for j in range(F // 128):
            at = slice(j * 128 + z * 16, j * 128 + z * 16 + 16)
            total = own[at, :]
            for g in got:
                total = total + g[at, :].astype(f32)
            out[z, j * 16 : (j + 1) * 16, :] = total.astype(bf16)
    tail = own[F:, :]
    for g in got:
        tail = tail + g[F:, :].astype(f32)
    tail = (tail[:8] + tail[8:]).astype(bf16)
    for z in range(Z):
        out[z, 128:, :] = tail


def last_kernel(got, weight_out, gain_out):
    total = got[0].astype(f32)
    for z in range(1, Z):
        total = total + got[z].astype(f32)
    total = total * GRAD_SCALE
    tail = total[128:]
    for j in range(F // 128):
        at = slice(j * 128, (j + 1) * 128)
        weight_out[:, at] = total[j * 16 : (j + 1) * 16]
        gain_out[:, at] = tail[j : j + 1]


def unpack_kernel(routes, got, rows, values):
    def take(m, _):
        d = routes[m]
        rows[m] = got[d, :, :F]
        values[m] = got[d, :, F:]
        return 0

    lax.fori_loop(0, PIECES, take, 0, unroll=8)


def shape(*dims, dtype=bf16):
    return jax.ShapeDtypeStruct(dims, dtype)


def exchange(v, axes):
    return lax.all_to_all(v, axes, split_axis=0, concat_axis=0, tiled=True)


def body(activations, targets, routes, value_weights, norm_gains):
    peer = ("x", "z", "core")
    weights = value_weights[0]
    order = routes[:, 0]
    given = order, activations.reshape(PIECES, MB, F), targets.reshape(PIECES, MB, C)
    sends = call(
        pack_kernel,
        shape(NP, MB, F + C),
        [HBM] * 3,
        [
            pltpu.SMEM((PIECES,), jnp.int32),
            pltpu.VMEM((PIECES, MB, F), bf16),
            pltpu.VMEM((PIECES, MB, C), bf16),
        ]
        + [pltpu.SemaphoreType.DMA] * 3,
        name="pack",
    )(*[pltpu.with_memory_space_constraint(v, pltpu.HBM) for v in given])
    arrived = exchange(sends, peer)
    partials, gained = call(
        value_kernel,
        (shape(NT, ROWS + SUMS, C), shape(ROWS, F)),
        [VMEM] * 3,
        [pltpu.VMEM((8, 128), f32)],
        flops=2 * ROWS * F * KV,
        name="partial_values",
    )(arrived, norm_gains, weights)
    value, grad_part, scales = call(
        loss_kernel,
        (shape(NP, MB, C), shape(NT, ROWS + SUMS, C), shape(8, 128, dtype=f32)),
        [VMEM] * 2,
        [pltpu.VMEM((8, 128), f32)],
        name="loss",
    )(exchange(partials, "tp"), arrived)
    back, grads, gains = call(
        grad_kernel,
        (shape(NP, MB, F + C), shape(ROWS, KV), shape(8, F, dtype=f32)),
        [VMEM] * 6,
        [pltpu.VMEM((NP, MB, F + C), bf16), pltpu.SemaphoreType.DMA((2,))],
        out_specs=(HBM, VMEM, VMEM),
        flops=2 * ROWS * F * KV,
        size=8 << 20,
        name="grads",
    )(exchange(grad_part, "tp"), arrived, norm_gains, weights, scales, value)
    rows_back = exchange(back, peer)

    half = (KV // CORES + EXTRA, F)
    keep, send = call(
        share_kernel,
        (shape(*half, dtype=f32), shape(*half)),
        [VMEM] * 4,
        flops=2 * ROWS * F * KV,
        name="share",
    )(grads, scales, gained, gains)
    got = lax.ppermute(send, "core", [(0, 1), (1, 0)])
    block = (F + EXTRA, 128)
    own, *sends = call(
        core_kernel, (shape(*block, dtype=f32),) + (shape(*block),) * (X - 1), [VMEM] * 2, name="sum_core"
    )(keep, got)
    got = [lax.ppermute(v, "x", [(i, (i + d) % X) for i in range(X)]) for d, v in zip(X_STEPS, sends)]
    grad_rows, values = call(
        unpack_kernel,
        (shape(PIECES, MB, F), shape(PIECES, MB, C)),
        [SMEM, VMEM],
        name="unpack",
    )(order, rows_back)
    got, grad_rows, values = lax.optimization_barrier((got, grad_rows, values))
    by_x = call(x_kernel, shape(Z, 128 + 8, 128), [VMEM] * X, name="sum_x")(own, *got)
    by_z = exchange(by_x, "z")
    weight_grad, gain_grad = call(
        last_kernel, (shape(16, F, dtype=f32), shape(1, F, dtype=f32)), [VMEM], name="sum_z"
    )(by_z)
    return (
        grad_rows.reshape(PIECES * MB, F),
        values.reshape(PIECES * MB, C),
        weight_grad,
        gain_grad[0],
    )


def solution(mesh):
    split = Mesh(mesh.devices.reshape(X, Z, CORES, NT), ("x", "z", "core", "tp"))
    peer = ("x", "z", "core")
    return jax.shard_map(
        body,
        mesh=split,
        in_specs=(
            P(peer, "tp"),
            P(peer, "tp"),
            P(peer, None),
            P(peer, "tp", None),
            P(peer, "tp"),
        ),
        out_specs=(P(peer, "tp"), P(peer, "tp"), P(peer, "tp"), P("tp")),
        check_vma=False,
    )
```

```python
import jax
import jax.numpy as jnp
from jax import lax
from jax.experimental import pallas as pl
from jax.experimental.pallas import tpu as pltpu
from jax.sharding import Mesh, PartitionSpec as P

D = 8192
KV = 1024
PIECES = 32
MB = 8
F = 1024
C = 128
NP = 64
NT = 8
X, Z, CORES = 4, 8, 2
X_STEPS = (2, 3, 1)
ROWS = NP * MB
TILE = 128
NTILES = ROWS // TILE
EXTRA = 16
SUMS = 8
GRAD_SCALE = (ROWS // 2 * NP) ** (-0.5)

epsilon = 1e-05
f32 = jnp.float32
bf16 = jnp.bfloat16
VMEM = pl.BlockSpec(memory_space=pltpu.VMEM)
HBM = pl.BlockSpec(memory_space=pltpu.HBM)
SMEM = pl.BlockSpec(memory_space=pltpu.SMEM)


def call(kernel, outs, in_specs, scratch=(), out_specs=None, flops=0, size=4 << 20, name=None):
    return pl.pallas_call(
        kernel,
        out_shape=outs,
        in_specs=in_specs,
        out_specs=jax.tree.map(lambda _: VMEM, outs) if out_specs is None else out_specs,
        scratch_shapes=scratch,
        compiler_params=pltpu.CompilerParams(vmem_limit_bytes=40 << 20),
        cost_estimate=pl.CostEstimate(flops=flops, bytes_accessed=size, transcendentals=0),
        name=name,
    )


def parts(v):
    high = v.astype(bf16).astype(f32)
    rest = v - high
    mid = rest.astype(bf16).astype(f32)
    return high, mid, rest - mid


def halves(v):
    high = v.astype(bf16).astype(f32)
    return high, v - high


def to_lanes(square):
    return jnp.sum(square.T, axis=0, keepdims=True)


def to_rows(lanes):
    return jnp.broadcast_to(lanes, (TILE, TILE)).T


def pack_kernel(routes, acts, goals, out, order, rows, columns, route_sem, row_sem, goal_sem):
    copies = [
        pltpu.make_async_copy(routes, order, route_sem),
        pltpu.make_async_copy(acts, rows, row_sem),
        pltpu.make_async_copy(goals, columns, goal_sem),
    ]
    for copy in copies:
        copy.start()

    def clear(d, _):
        out[pl.ds(d * 4, 4)] = jnp.zeros((4, MB, F + C), bf16)
        return 0

    lax.fori_loop(0, NP // 4, clear, 0)
    for copy in copies:
        copy.wait()

    def put(m, _):
        d = order[m]
        out[d, :, :F] = rows[m]
        out[d, :, F:] = columns[m]
        return 0

    lax.fori_loop(0, PIECES, put, 0, unroll=4)


def value_kernel(rows, gain, weights, out, gained, squares):
    for i in range(NTILES):
        x = rows[i * 16 : (i + 1) * 16, :, :F].astype(f32).reshape(TILE, F)
        sq = x * x
        folded = sq[:, :128]
        for j in range(1, F // 128):
            folded = folded + sq[:, j * 128 : (j + 1) * 128]
        squares[i : i + 1, :] = to_lanes(folded)
        gained[i * TILE : (i + 1) * TILE, :] = (x * gain[...]).astype(bf16)
    for i in range(KV // 256):
        partial = jnp.dot(gained[...], weights[:, i * 256 : (i + 1) * 256], preferred_element_type=f32).astype(bf16)
        out[2 * i, :ROWS, :] = partial[:, :C]
        out[2 * i + 1, :ROWS, :] = partial[:, C:]
    high, rest = halves(squares[0:4, :])
    tail = jnp.concatenate([high, rest], axis=0).astype(bf16)
    for t in range(NT):
        out[t, ROWS:, :] = tail


def loss_kernel(got, goals, value_out, send, scales, dots):
    tail = got[0, ROWS:, :].astype(f32)
    for t in range(1, NT):
        tail = tail + got[t, ROWS:, :].astype(f32)
    total = tail[0:4] + tail[4:8]
    scales[0:4, :] = lax.rsqrt(total / D + epsilon)
    scales[4:8, :] = jnp.zeros((4, 128), f32)

    for i in range(NTILES):
        here = slice(i * TILE, (i + 1) * TILE)
        total = got[0, here, :].astype(f32)
        for t in range(1, NT):
            total = total + got[t, here, :].astype(f32)
        value = total * to_rows(scales[i : i + 1, :])
        value_out[i * 16 : (i + 1) * 16] = value.reshape(16, MB, C).astype(bf16)
        goal = goals[i * 16 : (i + 1) * 16, :, F:].astype(f32).reshape(TILE, C)
        grad = (value - goal).astype(bf16)
        for t in range(NT):
            send[t, here, :] = grad
        dots[i : i + 1, :] = to_lanes(grad.astype(f32) * value)

    high, rest = halves(dots[0:4, :])
    tail = jnp.concatenate([high, rest], axis=0).astype(bf16)
    for t in range(NT):
        send[t, ROWS:, :] = tail


def grad_kernel(got, rows, gain, weights, scales, value, back, grads, gains, made, sems):
    tail = got[0, ROWS:, :].astype(f32)
    for t in range(1, NT):
        tail = tail + got[t, ROWS:, :].astype(f32)
    dots = (tail[0:4] + tail[4:8]) / D
    copies = []
    sums = [0.0] * (F // 256)
    for half in range(2):
        here = slice(half * ROWS // 2, (half + 1) * ROWS // 2)
        slots = slice(half * NP // 2, (half + 1) * NP // 2)
        for t in range(NT):
            grads[here, t * C : (t + 1) * C] = got[t, here, :]
        tiles = range(half * NTILES // 2, (half + 1) * NTILES // 2)
        scale = [scales[i : i + 1, :] for i in tiles]
        dot = [v * v * dots[i : i + 1, :] for i, v in zip(tiles, scale)]
        scale = jnp.concatenate([to_rows(v) for v in scale], axis=0)
        scale = jnp.concatenate([scale, scale], axis=1)
        dot = jnp.concatenate([to_rows(v) for v in dot], axis=0)
        dot = jnp.concatenate([dot, dot], axis=1)
        made[slots, :, F:] = value[slots]
        for i in range(F // 256):
            at = slice(i * 256, (i + 1) * 256)
            grad_normed = lax.dot_general(
                grads[here, :], weights[at, :], (((1,), (1,)), ((), ())), preferred_element_type=f32
            )
            scaled = grad_normed * scale
            x = rows[slots, :, at].astype(f32).reshape(ROWS // 2, 256)
            row_grad = scaled * gain[:, at] - x * dot
            made[slots, :, at] = row_grad.reshape(NP // 2, MB, 256).astype(bf16)
            sums[i] += jnp.sum((scaled * x).reshape(ROWS // 16, 8, 256), axis=0)
        where = pl.ds(half * NP // 2, NP // 2)
        copies.append(pltpu.make_async_copy(made.at[where], back.at[where], sems.at[half]))
        copies[-1].start()
    for i in range(F // 256):
        gains[:, i * 256 : (i + 1) * 256] = sums[i]
    for copy in copies:
        copy.wait()


def share_kernel(grads, scales, gained, gains, keep, send):
    first = lax.axis_index("core") == 0
    scale = jnp.concatenate([to_rows(scales[i : i + 1, :]) for i in range(NTILES)], axis=0)
    scale = jnp.concatenate([scale, scale], axis=1)
    for i in range(KV // 256):
        scaled = (grads[:, i * 256 : (i + 1) * 256].astype(f32) * scale).astype(bf16)
        mine = lax.dot_general(scaled, gained[...], (((0,), (0,)), ((), ())), preferred_element_type=f32)
        for j in range(8):
            at = slice(i * 128 + j * 16, i * 128 + (j + 1) * 16)
            even = mine[j * 32 : j * 32 + 16, :]
            odd = mine[j * 32 + 16 : j * 32 + 32, :]
            keep[at, :] = jnp.where(first, even, odd)
            send[at, :] = jnp.where(first, odd, even).astype(bf16)

    total = jnp.sum(gains[...], axis=0, keepdims=True)
    keep[KV // 2 :, :] = jnp.concatenate([total, jnp.zeros((EXTRA - 1, F), f32)], axis=0)
    high, mid, low = parts(total)
    tail = jnp.concatenate([high, mid, low, jnp.zeros((EXTRA - 3, F), f32)], axis=0)
    send[KV // 2 :, :] = tail.astype(bf16)


def gain_tail(total):
    high = total.astype(bf16).astype(f32)
    return jnp.concatenate([high, total - high], axis=0).astype(bf16)


def core_kernel(keep, got, own, *sends):
    me = lax.axis_index("x")
    tail = keep[KV // 2 :, :] + got[KV // 2 :, :].astype(f32)
    tail = jnp.sum(tail, axis=0, keepdims=True)
    tail = jnp.concatenate([tail[:, j * 128 : (j + 1) * 128] for j in range(F // 128)], axis=0)

    def put(out, d, tail):
        there = pl.ds(pl.multiple_of(lax.rem(me + d, X) * 128, 128), 128)
        total = keep[there, :] + got[there, :].astype(f32)
        for j in range(F // 128):
            out[j * 128 : (j + 1) * 128, :] = total[:, j * 128 : (j + 1) * 128].astype(out.dtype)
        out[F:, :] = tail

    for d, send in zip(X_STEPS, sends):
        put(send, d, gain_tail(tail))
    put(own, 0, jnp.concatenate([tail, jnp.zeros_like(tail)], axis=0))


def x_kernel(own, *refs):
    *got, out = refs
    for z in range(Z):
        for j in range(F // 128):
            at = slice(j * 128 + z * 16, j * 128 + z * 16 + 16)
            total = own[at, :]
            for g in got:
                total = total + g[at, :].astype(f32)
            out[z, j * 16 : (j + 1) * 16, :] = total.astype(bf16)
    tail = own[F:, :]
    for g in got:
        tail = tail + g[F:, :].astype(f32)
    tail = (tail[:8] + tail[8:]).astype(bf16)
    for z in range(Z):
        out[z, 128:, :] = tail


def last_kernel(got, weight_out, gain_out):
    total = got[0].astype(f32)
    for z in range(1, Z):
        total = total + got[z].astype(f32)
    total = total * GRAD_SCALE
    tail = total[128:]
    for j in range(F // 128):
        at = slice(j * 128, (j + 1) * 128)
        weight_out[:, at] = total[j * 16 : (j + 1) * 16]
        gain_out[:, at] = tail[j : j + 1]


def unpack_kernel(routes, got, rows, values):
    def take(m, _):
        d = routes[m]
        rows[m] = got[d, :, :F]
        values[m] = got[d, :, F:]
        return 0

    lax.fori_loop(0, PIECES, take, 0)


def shape(*dims, dtype=bf16):
    return jax.ShapeDtypeStruct(dims, dtype)


def exchange(v, axes):
    return lax.all_to_all(v, axes, split_axis=0, concat_axis=0, tiled=True)


def body(activations, targets, routes, value_weights, norm_gains):
    peer = ("x", "z", "core")
    weights = value_weights[0]
    order = routes[:, 0]
    given = order, activations.reshape(PIECES, MB, F), targets.reshape(PIECES, MB, C)
    sends = call(
        pack_kernel,
        shape(NP, MB, F + C),
        [HBM] * 3,
        [
            pltpu.SMEM((PIECES,), jnp.int32),
            pltpu.VMEM((PIECES, MB, F), bf16),
            pltpu.VMEM((PIECES, MB, C), bf16),
        ]
        + [pltpu.SemaphoreType.DMA] * 3,
        name="pack",
    )(*[pltpu.with_memory_space_constraint(v, pltpu.HBM) for v in given])
    arrived = exchange(sends, peer)
    partials, gained = call(
        value_kernel,
        (shape(NT, ROWS + SUMS, C), shape(ROWS, F)),
        [VMEM] * 3,
        [pltpu.VMEM((8, 128), f32)],
        flops=2 * ROWS * F * KV,
        name="partial_values",
    )(arrived, norm_gains, weights)
    value, grad_part, scales = call(
        loss_kernel,
        (shape(NP, MB, C), shape(NT, ROWS + SUMS, C), shape(8, 128, dtype=f32)),
        [VMEM] * 2,
        [pltpu.VMEM((8, 128), f32)],
        name="loss",
    )(exchange(partials, "tp"), arrived)
    back, grads, gains = call(
        grad_kernel,
        (shape(NP, MB, F + C), shape(ROWS, KV), shape(8, F, dtype=f32)),
        [VMEM] * 6,
        [pltpu.VMEM((NP, MB, F + C), bf16), pltpu.SemaphoreType.DMA((2,))],
        out_specs=(HBM, VMEM, VMEM),
        flops=2 * ROWS * F * KV,
        size=8 << 20,
        name="grads",
    )(exchange(grad_part, "tp"), arrived, norm_gains, weights, scales, value)
    rows_back = exchange(back, peer)

    half = (KV // CORES + EXTRA, F)
    keep, send = call(
        share_kernel,
        (shape(*half, dtype=f32), shape(*half)),
        [VMEM] * 4,
        flops=2 * ROWS * F * KV,
        name="share",
    )(grads, scales, gained, gains)
    got = lax.ppermute(send, "core", [(0, 1), (1, 0)])
    block = (F + EXTRA, 128)
    own, *sends = call(
        core_kernel, (shape(*block, dtype=f32),) + (shape(*block),) * (X - 1), [VMEM] * 2, name="sum_core"
    )(keep, got)
    got = [lax.ppermute(v, "x", [(i, (i + d) % X) for i in range(X)]) for d, v in zip(X_STEPS, sends)]
    grad_rows, values = call(
        unpack_kernel,
        (shape(PIECES, MB, F), shape(PIECES, MB, C)),
        [SMEM, VMEM],
        name="unpack",
    )(order, rows_back)
    got, grad_rows, values = lax.optimization_barrier((got, grad_rows, values))
    by_x = call(x_kernel, shape(Z, 128 + 8, 128), [VMEM] * X, name="sum_x")(own, *got)
    by_z = exchange(by_x, "z")
    weight_grad, gain_grad = call(
        last_kernel, (shape(16, F, dtype=f32), shape(1, F, dtype=f32)), [VMEM], name="sum_z"
    )(by_z)
    return (
        grad_rows.reshape(PIECES * MB, F),
        values.reshape(PIECES * MB, C),
        weight_grad,
        gain_grad[0],
    )


def solution(mesh):
    split = Mesh(mesh.devices.reshape(X, Z, CORES, NT), ("x", "z", "core", "tp"))
    peer = ("x", "z", "core")
    return jax.shard_map(
        body,
        mesh=split,
        in_specs=(
            P(peer, "tp"),
            P(peer, "tp"),
            P(peer, None),
            P(peer, "tp", None),
            P(peer, "tp"),
        ),
        out_specs=(P(peer, "tp"), P(peer, "tp"), P(peer, "tp"), P("tp")),
        check_vma=False,
    )
```
